128 devices in a mesh: row: 2 (over core), col: 4 (over x), rep: 16 (over z, y).
Axes of the slice: x: 4, y: 4, z: 4, core: 2. Of those that a mesh axis runs over, the one named last changes fastest.
Arguments:
- hamiltonian: bfloat16 [7168, 7168], P('row', 'col'), may hold values from -1 to 1, as said below
- pattern: int32 [56, 56], P('row', 'col'), may hold values from 0 to 1, as said below
Outputs:
- sign_matrix: bfloat16 [7168, 7168], P('row', 'col')
The draws below stay inside these ranges and needn't reach their ends.
Inputs may be any that keep to these rules, and one draw needn't show every extreme that they name: `hamiltonian`: a symmetric matrix. `pattern`: symmetric; ones on the block diagonal and on the blocks next to it, cyclically.
All inputs are finite; a program needn't handle non-finite values.
Results may differ from the reference program's by a relative error of at most 0.015.
Values may be sent and summed in bfloat16 or wider, within the bound.
No kernel may reach another device: no remote copies, remote signals or barrier semaphores. Data moves between devices by JAX's collectives and lax.ppermute only.
A program may use at most 256 MiB of HBM per device.

```python
import math
import jax
import jax.numpy as jnp
from jax import lax

BS = 128
P_SIZE = 56
STEPS = 1
N = 7168
NB = 56
N_REP = 16


def draw_hamiltonian(key, part):
    key = jax.random.fold_in(key, 11)
    key_sym, key_mag, key_sign = jax.random.split(key, 3)
    sample = jax.random.normal(key_sym, (N, N), jnp.float32)
    lowest, highest = (0.3, 0.9)
    spread = 0.55 / math.sqrt(N)
    symmetric = (sample + sample.T) * 0.5 ** 0.5 * spread
    magnitude = jax.random.uniform(key_mag, (N,), jnp.float32, lowest, highest)
    diagonal_sign = jnp.where(jax.random.randint(key_sign, (N,), 0, 2) == 0, -1.0, 1.0)
    indices = jnp.arange(N)
    on_diagonal = indices[:, None] == indices[None, :]
    values = jnp.broadcast_to((magnitude * diagonal_sign)[:, None], (N, N))
    return jnp.where(on_diagonal, values, symmetric).astype(jnp.bfloat16)


def draw_pattern(key, part):
    key = jax.random.fold_in(key, 7)
    coin_toss = jax.random.randint(key, (NB, NB), 0, 4)
    chosen = jnp.where(coin_toss == 0, 1, 0)
    chosen = jnp.maximum(chosen, chosen.T)
    indices = jnp.arange(NB)
    distance = jnp.abs(indices[:, None] - indices[None, :])
    adjacent = jnp.where(jnp.minimum(distance, NB - distance) <= 1, 1, 0)
    return jnp.maximum(chosen, adjacent).astype(jnp.int32)


def setup_inputs(seed: int = 0) -> dict:
    arg_keys = jax.random.split(jax.random.key(seed), 3)
    return {
        "hamiltonian": draw_hamiltonian(jax.random.fold_in(arg_keys[2], 71), 0),
        "pattern": draw_pattern(jax.random.fold_in(arg_keys[2], 71), 0),
    }


def expand(pattern):
    retained = pattern.astype(jnp.float32)
    blocks = pattern.shape[0]
    return jnp.broadcast_to(retained[:, None, :, None], (blocks, BS, blocks, BS)).reshape(N, N)


def layered(left_matrix, right_matrix):
    groups = N // (P_SIZE * N_REP)
    col_view = left_matrix.reshape(N, groups, N_REP, P_SIZE)
    row_view = right_matrix.reshape(groups, N_REP, P_SIZE, N)
    running = jnp.zeros((N, N), jnp.float32)
    for replica in range(N_REP):
        partial_value = jnp.dot(col_view[:, :, replica, :].reshape(N, groups * P_SIZE), row_view[:, replica].reshape(groups * P_SIZE, N), preferred_element_type=jnp.float32)
        rounded = lax.optimization_barrier(partial_value.astype(jnp.bfloat16))
        running = running + rounded.astype(jnp.float32)
    return running


def reference(hamiltonian, pattern):
    retained = expand(pattern)
    current = (hamiltonian.astype(jnp.float32) * retained).astype(jnp.bfloat16)
    for newton_step in range(STEPS):
        square = (layered(current, current) * retained).astype(jnp.bfloat16)
        cubed = layered(current, square)
        current = ((1.5 * current.astype(jnp.float32) - 0.5 * cubed) * retained).astype(jnp.bfloat16)
    return current
```

```python
import functools

import jax
import jax.numpy as jnp
from jax import lax
from jax.experimental import pallas as pl
from jax.experimental.pallas import tpu as pltpu
from jax.sharding import PartitionSpec as P

BS = 128
UNIT = 16
TIERS = (176, 192, 208, 224, 256, 320, 400)
VMEM_LIMIT = 60 * 1024 * 1024


def params():
    return pltpu.CompilerParams(vmem_limit_bytes=VMEM_LIMIT)


def mask_kernel(pat_ref, rep_ref, h_ref, x_ref, g_ref, pick_ref, *, reps):
    step = pl.program_id(0)
    stripe, width = h_ref.shape
    units = pick_ref.shape[0]

    @pl.when(step == 0)
    def _():
        u = lax.broadcasted_iota(jnp.int32, (units, width), 0)
        c = lax.broadcasted_iota(jnp.int32, (units, width), 1)
        target = (u // UNIT) * (reps * UNIT) + rep_ref[0] * UNIT + u % UNIT
        pick_ref[...] = jnp.where(c == target, 1.0, 0.0).astype(jnp.bfloat16)

    for a in range(stripe // BS):
        for b in range(width // BS):
            kept = pat_ref[step * (stripe // BS) + a, b].astype(jnp.float32)
            rows, cols = pl.ds(a * BS, BS), pl.ds(b * BS, BS)
            x_ref[rows, cols] = (h_ref[rows, cols].astype(jnp.float32) * kept).astype(jnp.bfloat16)
    g_ref[...] = lax.dot_general(
        pick_ref[...], x_ref[...], (((1,), (1,)), ((), ())), preferred_element_type=jnp.float32
    ).astype(jnp.bfloat16)


def mask_and_pick(tile, pattern, rep, reps, stripe=512):
    height, width = tile.shape
    units = width // reps
    return pl.pallas_call(
        functools.partial(mask_kernel, reps=reps),
        grid=(height // stripe,),
        in_specs=[
            pl.BlockSpec(memory_space=pltpu.SMEM),
            pl.BlockSpec(memory_space=pltpu.SMEM),
            pl.BlockSpec((stripe, width), lambda i: (i, 0)),
        ],
        out_specs=[
            pl.BlockSpec((stripe, width), lambda i: (i, 0)),
            pl.BlockSpec((units, stripe), lambda i: (0, i)),
        ],
        out_shape=[
            jax.ShapeDtypeStruct((height, width), jnp.bfloat16),
            jax.ShapeDtypeStruct((units, height), jnp.bfloat16),
        ],
        scratch_shapes=[pltpu.VMEM((units, width), jnp.bfloat16)],
        compiler_params=params(),
        name="mask_and_pick",
    )(pattern, rep, tile)


def cube_kernel(pat_ref, g_ref, q_ref, out_ref, part_ref, count_ref, *, slots):
    step = pl.program_id(0)
    stripe = g_ref.shape[1]
    width = q_ref.shape[1]

    @pl.when(step == 0)
    def _():
        count_ref[0] = 0

    turned = g_ref[...].T
    for c in range(width // (2 * BS)):
        acc = jnp.dot(
            turned, q_ref[:, 2 * BS * c : 2 * BS * (c + 1)], preferred_element_type=jnp.float32
        ).astype(jnp.bfloat16)
        part_ref[2 * c] = acc[:, :BS]
        part_ref[2 * c + 1] = acc[:, BS:]
    count = count_ref[0]
    for a in range(stripe // BS):
        for b in range(width // BS):
            kept = pat_ref[step * (stripe // BS) + a, b]
            slot = jnp.minimum(count, slots - 1)

            @pl.when(kept != 0)
            def _():
                out_ref[slot] = part_ref[b, a * BS : (a + 1) * BS, :]

            count = count + kept
    count_ref[0] = count

    @pl.when(step == pl.num_programs(0) - 1)
    def _():
        def clear(s, carry):
            out_ref[s] = jnp.zeros((BS, BS), jnp.bfloat16)
            return carry

        lax.fori_loop(jnp.minimum(count, slots), slots, clear, 0)


def cube_part(pattern, rows, square_rows, slots, stripe=512):
    depth, height = rows.shape
    width = square_rows.shape[1]
    return pl.pallas_call(
        functools.partial(cube_kernel, slots=slots),
        grid=(height // stripe,),
        in_specs=[
            pl.BlockSpec(memory_space=pltpu.SMEM),
            pl.BlockSpec((depth, stripe), lambda i: (0, i)),
            pl.BlockSpec((depth, width), lambda i: (0, 0)),
        ],
        out_specs=pl.BlockSpec((slots, BS, BS), lambda i: (0, 0, 0)),
        out_shape=jax.ShapeDtypeStruct((slots, BS, BS), jnp.bfloat16),
        scratch_shapes=[
            pltpu.VMEM((width // BS, stripe, BS), jnp.bfloat16),
            pltpu.SMEM((1,), jnp.int32),
        ],
        compiler_params=params(),
        name="cube_part",
    )(pattern, rows, square_rows)


def finish_kernel(pat_ref, h_ref, cubed_ref, out_ref, count_ref, *, slots):
    step = pl.program_id(0)
    stripe, width = h_ref.shape

    @pl.when(step == 0)
    def _():
        count_ref[0] = 0

    count = count_ref[0]
    for a in range(stripe // BS):
        for b in range(width // BS):
            kept = pat_ref[step * (stripe // BS) + a, b]
            slot = jnp.minimum(count, slots - 1)
            rows, cols = pl.ds(a * BS, BS), pl.ds(b * BS, BS)
            value = 1.5 * h_ref[rows, cols].astype(jnp.float32) - 0.5 * cubed_ref[slot].astype(
                jnp.float32
            )
            out_ref[rows, cols] = jnp.where(kept != 0, value, 0.0).astype(jnp.bfloat16)
            count = count + kept
    count_ref[0] = count


def finish(pattern, tile, cubed, slots, stripe=512):
    height, width = tile.shape
    return pl.pallas_call(
        functools.partial(finish_kernel, slots=slots),
        grid=(height // stripe,),
        in_specs=[
            pl.BlockSpec(memory_space=pltpu.SMEM),
            pl.BlockSpec((stripe, width), lambda i: (i, 0)),
            pl.BlockSpec((slots, BS, BS), lambda i: (0, 0, 0)),
        ],
        out_specs=pl.BlockSpec((stripe, width), lambda i: (i, 0)),
        out_shape=jax.ShapeDtypeStruct((height, width), jnp.bfloat16),
        scratch_shapes=[pltpu.SMEM((1,), jnp.int32)],
        compiler_params=params(),
        name="finish",
    )(pattern, tile, cubed)


def gather_rows(piece):
    cols = lax.axis_size("col")
    up = [(i, (i + 1) % cols) for i in range(cols)]
    down = [(i, (i - 1) % cols) for i in range(cols)]
    before = lax.ppermute(piece, "col", up)
    after = lax.ppermute(piece, "col", down)
    cut = 64
    far_top = lax.ppermute(before[:cut], "col", up)
    far_bottom = lax.ppermute(after[cut:], "col", down)
    return jnp.concatenate([piece, before, after, far_top, far_bottom], axis=0)


def shards(hamiltonian, pattern):
    height, width = hamiltonian.shape
    reps = lax.axis_size("rep")
    cols = lax.axis_size("col")
    rep = lax.axis_index("rep")
    col = lax.axis_index("col")
    block_rows, block_cols = pattern.shape

    patterns = lax.all_gather(pattern, ("row", "col"), axis=0).reshape(-1, cols, block_rows, block_cols)
    most = jnp.max(jnp.sum(patterns, axis=(2, 3)))
    tier = sum((most > t).astype(jnp.int32) for t in TIERS[:-1])
    panel = lax.dynamic_index_in_dim(patterns, col, 1, keepdims=False).reshape(-1, block_cols)

    current, piece = mask_and_pick(hamiltonian, pattern, rep.reshape(1), reps)
    rows = gather_rows(piece)

    unit = jnp.arange(width // (reps * UNIT))
    owners = (col + jnp.array([0, cols - 1, 1, 2])) % cols
    unit_block = (owners[:, None] * width + unit[None, :] * (reps * UNIT) + rep * UNIT) // BS
    kept = panel[unit_block.reshape(-1)].astype(jnp.bfloat16)
    mask = jnp.broadcast_to(kept[:, None, :, None], (kept.shape[0], UNIT, block_cols, BS))
    mask = mask.reshape(rows.shape[0], width)

    part = jnp.dot(rows, current, preferred_element_type=jnp.float32)
    other = lax.ppermute(part.astype(jnp.bfloat16), "row", [(0, 1), (1, 0)])
    square_rows = jnp.where(mask != 0, part + other.astype(jnp.float32), 0.0).astype(jnp.bfloat16)

    def branch(slots):
        def run(pattern, rows, square_rows, hamiltonian):
            packed = cube_part(pattern, rows, square_rows, slots)
            cubed = lax.psum(packed, "rep")
            return finish(pattern, hamiltonian, cubed, slots)

        return run

    return lax.switch(tier, [branch(t) for t in TIERS], pattern, rows, square_rows, hamiltonian)


def solution(mesh):
    in_specs = (P("row", "col"), P("row", "col"))
    out_specs = P("row", "col")
    return jax.shard_map(shards, mesh=mesh, in_specs=in_specs, out_specs=out_specs, check_vma=False)
```

```python
import functools

import jax
import jax.numpy as jnp
from jax import lax
from jax.experimental import pallas as pl
from jax.experimental.pallas import tpu as pltpu
from jax.sharding import PartitionSpec as P

BS = 128
UNIT = 16
SIDE = 4
TIERS = (96, 104, 112, 120, 136, 160, 200)
MIB = 1024 * 1024
SMEM_SPEC = pl.BlockSpec(memory_space=pltpu.SMEM)
ANY_SPEC = pl.BlockSpec(memory_space=pl.ANY)


def params(mib):
    return pltpu.CompilerParams(vmem_limit_bytes=mib * MIB)


def whole(shape):
    return pl.BlockSpec(shape, lambda *_: (0,) * len(shape))


def pick_kernel(rep_ref, pat_ref, h_ref, g_ref):
    unit = pl.program_id(0)
    first = (rep_ref[0] % (BS // UNIT)) * UNIT
    u = lax.broadcasted_iota(jnp.int32, (UNIT, BS), 0)
    c = lax.broadcasted_iota(jnp.int32, (UNIT, BS), 1)
    chosen = jnp.where(c == u + first, 1.0, 0.0).astype(jnp.bfloat16)
    block_col = 2 * unit + rep_ref[0] // (BS // UNIT)
    for a in range(h_ref.shape[0] // BS):
        rows = pl.ds(a * BS, BS)
        kept = pat_ref[a, block_col].astype(jnp.float32)
        turned = lax.dot_general(
            chosen, h_ref[rows, :], (((1,), (1,)), ((), ())), preferred_element_type=jnp.float32
        )
        g_ref[:, rows] = (turned * kept).astype(jnp.bfloat16)


def pick(rep, pattern, tile, reps):
    height, width = tile.shape
    units = width // (reps * UNIT)
    return pl.pallas_call(
        pick_kernel,
        grid_spec=pltpu.PrefetchScalarGridSpec(
            num_scalar_prefetch=2,
            grid=(units,),
            in_specs=[
                pl.BlockSpec((height, BS), lambda j, rep, pat: (0, 2 * j + rep[0] // (BS // UNIT)))
            ],
            out_specs=pl.BlockSpec((UNIT, height), lambda j, rep, pat: (j, 0)),
        ),
        out_shape=jax.ShapeDtypeStruct((units * UNIT, height), jnp.bfloat16),
        compiler_params=params(32),
        name="pick",
    )(rep, pattern, tile)


def mask_kernel(pat_ref, h_ref, x_ref):
    step = pl.program_id(0)
    stripe, width = h_ref.shape
    for a in range(stripe // BS):
        for b in range(width // BS):
            kept = pat_ref[step * (stripe // BS) + a, b].astype(jnp.float32)
            rows, cols = pl.ds(a * BS, BS), pl.ds(b * BS, BS)
            x_ref[rows, cols] = (h_ref[rows, cols].astype(jnp.float32) * kept).astype(jnp.bfloat16)


def mask_tile(pattern, tile, stripe=512):
    height, width = tile.shape
    return pl.pallas_call(
        mask_kernel,
        grid=(height // stripe,),
        in_specs=[SMEM_SPEC, pl.BlockSpec((stripe, width), lambda i: (i, 0))],
        out_specs=pl.BlockSpec((stripe, width), lambda i: (i, 0)),
        out_shape=jax.ShapeDtypeStruct((height, width), jnp.bfloat16),
        compiler_params=params(32),
        cost_estimate=pl.CostEstimate(
            flops=height * width, bytes_accessed=4 * height * width, transcendentals=0
        ),
        name="mask_tile",
    )(pattern, tile)


def square_kernel(g_ref, x_ref, own_ref, other_ref):
    half = own_ref.shape[0]
    acc = jnp.dot(g_ref[...], x_ref[...], preferred_element_type=jnp.float32)
    own_ref[...] = acc[:half]
    other_ref[...] = acc[half:].astype(jnp.bfloat16)


def square_part(rows, current, span=2 * BS):
    depth, height = rows.shape
    width = current.shape[1]
    block = pl.BlockSpec((depth // 2, span), lambda i: (0, i))
    return pl.pallas_call(
        square_kernel,
        grid=(width // span,),
        in_specs=[whole((depth, height)), pl.BlockSpec((height, span), lambda i: (0, i))],
        out_specs=[block, block],
        out_shape=[
            jax.ShapeDtypeStruct((depth // 2, width), jnp.float32),
            jax.ShapeDtypeStruct((depth // 2, width), jnp.bfloat16),
        ],
        compiler_params=params(40),
        cost_estimate=pl.CostEstimate(
            flops=2 * depth * height * width,
            bytes_accessed=2 * height * (width + depth) + 3 * depth * width,
            transcendentals=0,
        ),
        name="square_part",
    )(rows, current)


def pack_kernel(rep_ref, pat_ref, own_ref, other_ref, *rest, slots, last):
    tile_ref, out_ref, held_ref = rest if last else (None, *rest)
    rows, width = own_ref.shape
    parity = rep_ref[0] // (BS // UNIT)
    held_ref[...] = jnp.zeros_like(held_ref)
    count = jnp.int32(0)
    for b in range(width // BS):
        for j in range(rows // UNIT):
            kept = pat_ref[2 * j + parity, b]
            slot = jnp.where(kept != 0, jnp.minimum(count, slots - 1), slots)
            part, cols = pl.ds(j * UNIT, UNIT), pl.ds(b * BS, BS)
            value = own_ref[part, cols] + other_ref[part, cols].astype(jnp.float32)
            if last:
                value = 1.5 * tile_ref[j, 0, :, cols].astype(jnp.float32) - 0.5 * value
            held_ref[slot] = value.astype(jnp.bfloat16)
            count = count + kept
    out_ref[...] = held_ref[:slots]


def pack(rep, pattern, own, other, slots, tile=None):
    rows, width = own.shape
    in_specs = [whole(own.shape), whole(other.shape)]
    operands = [own, other]
    if tile is not None:
        reps = tile.shape[0] // rows
        view = tile.reshape(rows // UNIT, reps, UNIT, width)
        in_specs.append(
            pl.BlockSpec((rows // UNIT, 1, UNIT, width), lambda i, rep, pat: (0, rep[0], 0, 0))
        )
        operands.append(view)
    return pl.pallas_call(
        functools.partial(pack_kernel, slots=slots, last=tile is not None),
        grid_spec=pltpu.PrefetchScalarGridSpec(
            num_scalar_prefetch=2,
            grid=(1,),
            in_specs=in_specs,
            out_specs=whole((slots, UNIT, BS)),
            scratch_shapes=[pltpu.VMEM((slots + 1, UNIT, BS), jnp.bfloat16)],
        ),
        out_shape=jax.ShapeDtypeStruct((slots, UNIT, BS), jnp.bfloat16),
        compiler_params=params(32),
        name="pack",
    )(rep, pattern, *operands)


def gather_rep(packed):
    along_z = [(z * SIDE + y, (z + 1) % SIDE * SIDE + y) for z in range(SIDE) for y in range(SIDE)]
    along_y = [(z * SIDE + y, z * SIDE + (y + 1) % SIDE) for z in range(SIDE) for y in range(SIDE)]

    def ring(piece, up):
        down = [(d, s) for s, d in up]
        before = lax.ppermute(piece, "rep", up)
        after = lax.ppermute(piece, "rep", down)
        cut = piece.shape[0] // 2
        far_top = lax.ppermute(before[:cut], "rep", up)
        far_bottom = lax.ppermute(after[cut:], "rep", down)
        return before, after, far_top, far_bottom

    half = packed.shape[0] // 2
    first = []
    for piece, axis in ((packed[:half], along_z), (packed[half:], along_y)):
        before, after, far_top, far_bottom = ring(piece, axis)
        far = jnp.concatenate([far_top, far_bottom], axis=0)
        first.append(jnp.stack([piece, before, after, far]))
    second = []
    for payload, axis in zip(first, (along_y, along_z)):
        second += [payload, *ring(payload, axis)]
    return second


def fill(pieces, held_ref, sems, slots):
    half = slots // 2
    places = ((0, SIDE, 0), (0, SIDE, 1), (0, SIDE, 2), (0, SIDE // 2, 3), (SIDE // 2, SIDE, 3))
    copies = []
    for n, piece in enumerate(pieces):
        lo, hi, place = places[n % 5]
        near = pl.ds(lo, hi - lo)
        if n < 5:
            target = held_ref.at[near, place, pl.ds(0, half)]
        else:
            target = held_ref.at[place, near, pl.ds(half, half)]
        copies.append(pltpu.make_async_copy(piece, target, sems.at[n]))
    for copy in copies:
        copy.start()
    held_ref[:, :, slots] = jnp.zeros_like(held_ref[:, :, slots])
    for copy in copies:
        copy.wait()


def unpack(rep_ref, pat_ref, held_ref, count_ref, out_ref, slots):
    step = pl.program_id(0)
    z, y = rep_ref[0] // SIDE, rep_ref[0] % SIDE

    def place(there, here):
        away = (there - here + SIDE) % SIDE
        return jnp.where(away == 0, 0, jnp.where(away == 3, 1, away + 1))

    place_z = [place(i, z) for i in range(SIDE)]
    place_y = [place(i, y) for i in range(SIDE)]
    counts = [count_ref[0], count_ref[1]]
    per_block = BS // UNIT
    for b in range(out_ref.shape[1] // BS):
        for i in range(out_ref.shape[0] // BS):
            parity = i % 2
            kept = pat_ref[i, step * (out_ref.shape[1] // BS) + b]
            slot = jnp.where(kept != 0, jnp.minimum(counts[parity], slots - 1), slots)
            for u in range(per_block):
                source = parity * per_block + u
                out_ref[pl.ds(i * BS + u * UNIT, UNIT), pl.ds(b * BS, BS)] = held_ref[
                    place_z[source // SIDE], place_y[source % SIDE], slot
                ]
            counts[parity] = counts[parity] + kept
    count_ref[0], count_ref[1] = counts


def cube_kernel(rep_ref, pat_ref, g_ref, *rest, slots):
    pieces, (own_ref, other_ref, held_ref, square_ref, count_ref, sems) = rest[:10], rest[10:]

    @pl.when(pl.program_id(0) == 0)
    def _():
        fill(pieces, held_ref, sems, slots)
        count_ref[0] = 0
        count_ref[1] = 0

    unpack(rep_ref, pat_ref, held_ref, count_ref, square_ref, slots)
    half = own_ref.shape[0]
    acc = jnp.dot(g_ref[...], square_ref[...], preferred_element_type=jnp.float32)
    own_ref[...] = acc[:half]
    other_ref[...] = acc[half:].astype(jnp.bfloat16)


def held_shape(slots):
    return pltpu.VMEM((SIDE, SIDE, slots + 1, UNIT, BS), jnp.bfloat16)


def cube_part(rep, pattern, rows, pieces, width, slots, span=2 * BS):
    depth, height = rows.shape
    block = pl.BlockSpec((depth // 2, span), lambda i: (0, i))
    return pl.pallas_call(
        functools.partial(cube_kernel, slots=slots),
        grid=(width // span,),
        in_specs=[SMEM_SPEC, SMEM_SPEC, whole((depth, height))] + [ANY_SPEC] * 10,
        out_specs=[block, block],
        out_shape=[
            jax.ShapeDtypeStruct((depth // 2, width), jnp.float32),
            jax.ShapeDtypeStruct((depth // 2, width), jnp.bfloat16),
        ],
        scratch_shapes=[
            held_shape(slots),
            pltpu.VMEM((height, span), jnp.bfloat16),
            pltpu.SMEM((2,), jnp.int32),
            pltpu.SemaphoreType.DMA((10,)),
        ],
        compiler_params=params(48),
        name="cube_part",
    )(rep, pattern, rows, *pieces)


def finish_kernel(rep_ref, pat_ref, *rest, slots):
    pieces, (out_ref, held_ref, count_ref, sems) = rest[:10], rest[10:]

    @pl.when(pl.program_id(0) == 0)
    def _():
        fill(pieces, held_ref, sems, slots)
        count_ref[0] = 0
        count_ref[1] = 0

    unpack(rep_ref, pat_ref, held_ref, count_ref, out_ref, slots)


def finish(rep, pattern, pieces, height, width, slots, span=2 * BS):
    return pl.pallas_call(
        functools.partial(finish_kernel, slots=slots),
        grid=(width // span,),
        in_specs=[SMEM_SPEC, SMEM_SPEC] + [ANY_SPEC] * 10,
        out_specs=pl.BlockSpec((height, span), lambda i: (0, i)),
        out_shape=jax.ShapeDtypeStruct((height, width), jnp.bfloat16),
        scratch_shapes=[
            held_shape(slots),
            pltpu.SMEM((2,), jnp.int32),
            pltpu.SemaphoreType.DMA((10,)),
        ],
        compiler_params=params(48),
        name="finish",
    )(rep, pattern, *pieces)


def gather_rows(piece, row, col):
    cols = lax.axis_size("col")
    units = piece.shape[0]
    up = [(i, (i + 1) % cols) for i in range(cols)]
    down = [(i, (i - 1) % cols) for i in range(cols)]
    before = lax.ppermute(piece, "col", up)
    after = lax.ppermute(piece, "col", down)
    cut = 64
    far_top = lax.ppermute(before[:cut], "col", up)
    far_bottom = lax.ppermute(after[cut:], "col", down)
    rows = jnp.zeros((cols * units, piece.shape[1]), piece.dtype)
    for part, away, skip in ((piece, 0, 0), (before, 3, 0), (after, 1, 0), (far_top, 2, 0), (far_bottom, 2, cut)):
        owner = (col + away) % cols
        place = (owner + cols - row * (cols // 2)) % cols
        rows = lax.dynamic_update_slice(rows, part, (place * units + skip, 0))
    return rows


def largest(value):
    cols = lax.axis_size("col")
    for axis, shifts in (("col", range(1, cols)), ("row", range(1, 2))):
        size = lax.axis_size(axis)
        others = [
            lax.ppermute(value, axis, [(i, (i + s) % size) for i in range(size)]) for s in shifts
        ]
        for other in others:
            value = jnp.maximum(value, other)
    return value


def swap(part):
    return lax.ppermute(part, "row", [(0, 1), (1, 0)])


def shards(hamiltonian, pattern):
    height, width = hamiltonian.shape
    reps = lax.axis_size("rep")
    row, col = lax.axis_index("row"), lax.axis_index("col")
    rep = lax.axis_index("rep").reshape(1)

    piece = pick(rep, pattern, hamiltonian, reps)
    rows = gather_rows(piece, row, col)
    by_parity = jnp.sum(pattern.reshape(-1, 2, pattern.shape[1]), axis=(0, 2))
    most = largest(jnp.max(by_parity).reshape(1))[0]
    tier = sum((most > t).astype(jnp.int32) for t in TIERS[:-1])

    current = mask_tile(pattern, hamiltonian)
    own, other = square_part(rows, current)
    other = swap(other)

    def branch(slots):
        def run(rep, pattern, hamiltonian, rows, own, other):
            square = gather_rep(pack(rep, pattern, own, other, slots))
            own, other = cube_part(rep, pattern, rows, square, width, slots)
            new = gather_rep(pack(rep, pattern, own, swap(other), slots, hamiltonian))
            return finish(rep, pattern, new, height, width, slots)

        return run

    return lax.switch(
        tier, [branch(t) for t in TIERS], rep, pattern, hamiltonian, rows, own, other
    )


def solution(mesh):
    in_specs = (P("row", "col"), P("row", "col"))
    out_specs = P("row", "col")
    return jax.shard_map(shards, mesh=mesh, in_specs=in_specs, out_specs=out_specs, check_vma=False)
```

```python
import functools

import jax
import jax.numpy as jnp
from jax import lax
from jax.experimental import pallas as pl
from jax.experimental.pallas import tpu as pltpu
from jax.sharding import PartitionSpec as P

BS = 128
UNIT = 16
UNITS = BS // UNIT
SIDE = 4
CHUNKS = 2
ROW_CAP = 120
CHUNK_CAP = 64
MIB = 1024 * 1024
SMEM_SPEC = pl.BlockSpec(memory_space=pltpu.SMEM)
ANY_SPEC = pl.BlockSpec(memory_space=pl.ANY)
PLACES = (0, 3, 1, 2)


def params(mib):
    return pltpu.CompilerParams(vmem_limit_bytes=mib * MIB)


def cost(flops, moved):
    return pl.CostEstimate(flops=flops, bytes_accessed=moved, transcendentals=0)


def whole(shape):
    return pl.BlockSpec(shape, lambda *_: (0,) * len(shape))


def place_of(there, here):
    away = (there - here + SIDE) % SIDE
    return jnp.where(away == 0, 0, jnp.where(away == 3, 1, away + 1))


def free_slot(kept, count, slots):
    return jnp.where(kept != 0, jnp.minimum(count, slots - 1), slots)


def pick_kernel(rep_ref, pat_ref, h_ref, out_ref, held_ref, count_ref, *, slots):
    step = pl.program_id(0)

    @pl.when(step == 0)
    def _():
        held_ref[...] = jnp.zeros_like(held_ref)
        count_ref[0] = 0

    first = (rep_ref[0] % UNITS) * UNIT
    u = lax.broadcasted_iota(jnp.int32, (UNIT, BS), 0)
    c = lax.broadcasted_iota(jnp.int32, (UNIT, BS), 1)
    chosen = jnp.where(c == u + first, 1.0, 0.0).astype(jnp.bfloat16)
    block_col = 2 * step + rep_ref[0] // UNITS
    count = count_ref[0]
    for a in range(h_ref.shape[0] // BS):
        kept = pat_ref[a, block_col]
        turned = lax.dot_general(
            chosen,
            h_ref[pl.ds(a * BS, BS), :],
            (((1,), (1,)), ((), ())),
            preferred_element_type=jnp.float32,
        )
        held_ref[free_slot(kept, count, slots)] = turned.astype(jnp.bfloat16)
        count = count + kept
    count_ref[0] = count

    @pl.when(step == pl.num_programs(0) - 1)
    def _():
        out_ref[...] = held_ref[:slots]


def pick(rep, pattern, tile, slots):
    height, width = tile.shape
    return pl.pallas_call(
        functools.partial(pick_kernel, slots=slots),
        grid_spec=pltpu.PrefetchScalarGridSpec(
            num_scalar_prefetch=2,
            grid=(width // (2 * BS),),
            in_specs=[pl.BlockSpec((height, BS), lambda j, rep, pat: (0, 2 * j + rep[0] // UNITS))],
            out_specs=whole((slots, UNIT, BS)),
            scratch_shapes=[
                pltpu.VMEM((slots + 1, UNIT, BS), jnp.bfloat16),
                pltpu.SMEM((1,), jnp.int32),
            ],
        ),
        out_shape=jax.ShapeDtypeStruct((slots, UNIT, BS), jnp.bfloat16),
        compiler_params=params(16),
        cost_estimate=cost(2 * UNIT * height * width, height * width),
        name="pick",
    )(rep, pattern, tile)


def mask_kernel(pat_ref, h_ref, x_ref):
    step = pl.program_id(0)
    stripe, width = h_ref.shape
    for a in range(stripe // BS):
        for b in range(width // BS):
            kept = pat_ref[step * (stripe // BS) + a, b].astype(jnp.float32)
            rows, cols = pl.ds(a * BS, BS), pl.ds(b * BS, BS)
            x_ref[rows, cols] = (h_ref[rows, cols].astype(jnp.float32) * kept).astype(jnp.bfloat16)


def mask_tile(pattern, tile, stripe=512):
    height, width = tile.shape
    return pl.pallas_call(
        mask_kernel,
        grid=(height // stripe,),
        in_specs=[SMEM_SPEC, pl.BlockSpec((stripe, width), lambda i: (i, 0))],
        out_specs=pl.BlockSpec((stripe, width), lambda i: (i, 0)),
        out_shape=jax.ShapeDtypeStruct((height, width), jnp.bfloat16),
        compiler_params=params(16),
        cost_estimate=cost(height * width, 4 * height * width),
        name="mask_tile",
    )(pattern, tile)


def rows_kernel(where_ref, pats_ref, *rest, slots):
    pieces, (out_ref, held_ref, sems) = rest[:5], rest[5:]
    half = slots // 2
    targets = (
        held_ref.at[0, pl.ds(0, slots)],
        held_ref.at[1, pl.ds(0, slots)],
        held_ref.at[2, pl.ds(0, slots)],
        held_ref.at[3, pl.ds(0, half)],
        held_ref.at[3, pl.ds(half, half)],
    )
    copies = [
        pltpu.make_async_copy(piece, target, sems.at[n])
        for n, (piece, target) in enumerate(zip(pieces, targets))
    ]
    for copy in copies:
        copy.start()
    held_ref[:, slots] = jnp.zeros_like(held_ref[:, slots])
    for copy in copies:
        copy.wait()
    row, col, rep = where_ref[0], where_ref[1], where_ref[2]
    cols, units = SIDE, out_ref.shape[0] // (SIDE * UNIT)
    parity = rep // UNITS
    for n, away in enumerate(PLACES):
        place = ((col + away) % cols + cols - row * (cols // 2)) % cols

        def unit(j, count, n=n, place=place):
            start = pl.multiple_of((place * units + j) * UNIT, UNIT)
            for a in range(out_ref.shape[1] // BS):
                kept = pats_ref[n, a, 2 * j + parity]
                slot = free_slot(kept, count, slots)
                out_ref[pl.ds(start, UNIT), pl.ds(a * BS, BS)] = held_ref[n, slot]
                count = count + kept
            return count

        lax.fori_loop(0, units, unit, jnp.int32(0))


def unpack_rows(where, pats, pieces, height, units, slots):
    shape = (SIDE * units * UNIT, height)
    return pl.pallas_call(
        functools.partial(rows_kernel, slots=slots),
        in_specs=[SMEM_SPEC, SMEM_SPEC] + [ANY_SPEC] * 5,
        out_specs=pl.BlockSpec(memory_space=pltpu.VMEM),
        out_shape=jax.ShapeDtypeStruct(shape, jnp.bfloat16),
        scratch_shapes=[
            pltpu.VMEM((SIDE, slots + 1, UNIT, BS), jnp.bfloat16),
            pltpu.SemaphoreType.DMA((5,)),
        ],
        compiler_params=params(16),
        name="unpack_rows",
    )(where, pats, *pieces)


def accumulate(acc_ref, left, right, own_ref, other_ref):
    step = pl.program_id(0)
    half = own_ref.shape[0]
    part = jnp.dot(left, right, preferred_element_type=jnp.float32)

    @pl.when(step == 0)
    def _():
        acc_ref[...] = part

    @pl.when(step != 0)
    def _():
        acc_ref[...] += part

    @pl.when(step == pl.num_programs(0) - 1)
    def _():
        own_ref[...] = acc_ref[:half]
        other_ref[...] = acc_ref[half:].astype(jnp.bfloat16)


def part_outputs(depth, span):
    specs = [whole((depth // 2, span))] * 2
    shapes = [
        jax.ShapeDtypeStruct((depth // 2, span), jnp.float32),
        jax.ShapeDtypeStruct((depth // 2, span), jnp.bfloat16),
    ]
    return specs, shapes


def square_kernel(g_ref, x_ref, own_ref, other_ref, acc_ref):
    accumulate(acc_ref, g_ref[...], x_ref[...], own_ref, other_ref)


def square_part(rows, current, chunk, span, stripe=512):
    depth, height = rows.shape
    specs, shapes = part_outputs(depth, span)
    return pl.pallas_call(
        square_kernel,
        grid=(height // stripe,),
        in_specs=[
            pl.BlockSpec((depth, stripe), lambda k: (0, k)),
            pl.BlockSpec((stripe, span), lambda k: (k, chunk)),
        ],
        out_specs=specs,
        out_shape=shapes,
        scratch_shapes=[pltpu.VMEM((depth, span), jnp.float32)],
        compiler_params=params(24),
        cost_estimate=cost(2 * depth * height * span, 2 * height * (span + depth) + 3 * depth * span),
        name="square_part",
    )(rows, current)


def pack_kernel(rep_ref, pat_ref, own_ref, other_ref, *rest, slots, first, last):
    tile_ref, out_ref, held_ref = rest if last else (None, *rest)
    rows, width = own_ref.shape
    parity = rep_ref[0] // UNITS
    held_ref[...] = jnp.zeros_like(held_ref)
    count = jnp.int32(0)
    for j in range(rows // UNIT):
        for b in range(width // BS):
            kept = pat_ref[2 * j + parity, first + b]
            part, cols = pl.ds(j * UNIT, UNIT), pl.ds(b * BS, BS)
            value = own_ref[part, cols] + other_ref[part, cols].astype(jnp.float32)
            if last:
                value = 1.5 * tile_ref[j, 0, :, cols].astype(jnp.float32) - 0.5 * value
            held_ref[free_slot(kept, count, slots)] = value.astype(jnp.bfloat16)
            count = count + kept
    out_ref[...] = held_ref[:slots]


def pack(rep, pattern, own, other, chunk, slots, tile=None):
    rows, span = own.shape
    in_specs = [whole(own.shape), whole(other.shape)]
    operands = [own, other]
    if tile is not None:
        reps = tile.shape[0] // rows
        operands.append(tile.reshape(rows // UNIT, reps, UNIT, tile.shape[1]))
        in_specs.append(
            pl.BlockSpec((rows // UNIT, 1, UNIT, span), lambda i, rep, pat: (0, rep[0], 0, chunk))
        )
    return pl.pallas_call(
        functools.partial(
            pack_kernel, slots=slots, first=chunk * span // BS, last=tile is not None
        ),
        grid_spec=pltpu.PrefetchScalarGridSpec(
            num_scalar_prefetch=2,
            grid=(1,),
            in_specs=in_specs,
            out_specs=whole((slots, UNIT, BS)),
            scratch_shapes=[pltpu.VMEM((slots + 1, UNIT, BS), jnp.bfloat16)],
        ),
        out_shape=jax.ShapeDtypeStruct((slots, UNIT, BS), jnp.bfloat16),
        compiler_params=params(16),
        cost_estimate=cost(4 * rows * span, 8 * rows * span),
        name="pack",
    )(rep, pattern, *operands)


def fill(pieces, held_ref, sems, slots):
    low, high = pl.ds(0, SIDE // 2), pl.ds(SIDE // 2, SIDE // 2)
    used = pl.ds(0, slots)
    targets = [held_ref.at[:, place, used] for place in range(SIDE - 1)]
    targets += [held_ref.at[low, SIDE - 1, used], held_ref.at[high, SIDE - 1, used]]
    copies = [
        pltpu.make_async_copy(piece, target, sems.at[n])
        for n, (piece, target) in enumerate(zip(pieces, targets))
    ]
    for copy in copies:
        copy.start()
    held_ref[:, :, slots] = jnp.zeros_like(held_ref[:, :, slots])
    for copy in copies:
        copy.wait()


def unpack(rep_ref, pat_ref, held_ref, count_ref, out_ref, chunk, slots):
    step = pl.program_id(0)
    z, y = rep_ref[0] // SIDE, rep_ref[0] % SIDE
    place_z = [place_of(i, z) for i in range(SIDE)]
    place_y = [place_of(i, y) for i in range(SIDE)]
    counts = [count_ref[0], count_ref[1]]
    block_rows, block_cols = out_ref.shape[0] // BS, out_ref.shape[1] // BS
    for a in range(block_rows):
        parity = a % 2
        for b in range(block_cols):
            kept = pat_ref[step * block_rows + a, chunk * block_cols + b]
            slot = free_slot(kept, counts[parity], slots)
            for u in range(UNITS):
                source = parity * UNITS + u
                places = place_z[source // SIDE], place_y[source % SIDE]
                first, second = places if chunk == 0 else places[::-1]
                out_ref[pl.ds(a * BS + u * UNIT, UNIT), pl.ds(b * BS, BS)] = held_ref[
                    first, second, slot
                ]
            counts[parity] = counts[parity] + kept
    count_ref[0], count_ref[1] = counts


def begin(pieces, held_ref, count_ref, sems, slots):
    @pl.when(pl.program_id(0) == 0)
    def _():
        fill(pieces, held_ref, sems, slots)
        count_ref[0] = 0
        count_ref[1] = 0


def gathered_scratch(slots):
    return [
        pltpu.VMEM((SIDE, SIDE, slots + 1, UNIT, BS), jnp.bfloat16),
        pltpu.SMEM((2,), jnp.int32),
        pltpu.SemaphoreType.DMA((5,)),
    ]


def cube_kernel(rep_ref, pat_ref, g_ref, *rest, chunk, slots):
    pieces, (own_ref, other_ref, held_ref, count_ref, sems, square_ref, acc_ref) = rest[:5], rest[5:]
    begin(pieces, held_ref, count_ref, sems, slots)
    unpack(rep_ref, pat_ref, held_ref, count_ref, square_ref, chunk, slots)
    accumulate(acc_ref, g_ref[...], square_ref[...], own_ref, other_ref)


def cube_part(rep, pattern, rows, pieces, chunk, span, slots, stripe=512):
    depth, height = rows.shape
    specs, shapes = part_outputs(depth, span)
    return pl.pallas_call(
        functools.partial(cube_kernel, chunk=chunk, slots=slots),
        grid=(height // stripe,),
        in_specs=[SMEM_SPEC, SMEM_SPEC, pl.BlockSpec((depth, stripe), lambda k: (0, k))]
        + [ANY_SPEC] * 5,
        out_specs=specs,
        out_shape=shapes,
        scratch_shapes=gathered_scratch(slots)
        + [pltpu.VMEM((stripe, span), jnp.bfloat16), pltpu.VMEM((depth, span), jnp.float32)],
        compiler_params=params(24),
        cost_estimate=cost(2 * depth * height * span, 2 * height * (span + depth) + 3 * depth * span),
        name="cube_part",
    )(rep, pattern, rows, *pieces)


def finish_kernel(rep_ref, pat_ref, *rest, chunk, slots):
    pieces, (out_ref, held_ref, count_ref, sems) = rest[:5], rest[-4:]
    begin(pieces, held_ref, count_ref, sems, slots)
    unpack(rep_ref, pat_ref, held_ref, count_ref, out_ref, chunk, slots)


def finish(rep, pattern, pieces, shape, chunk, slots, so_far=None, stripe=512):
    height, width = shape
    span = width // CHUNKS
    operands = [rep, pattern, *pieces] + ([] if so_far is None else [so_far])
    return pl.pallas_call(
        functools.partial(finish_kernel, chunk=chunk, slots=slots),
        grid=(height // stripe,),
        in_specs=[SMEM_SPEC, SMEM_SPEC] + [ANY_SPEC] * (len(operands) - 2),
        out_specs=pl.BlockSpec((stripe, span), lambda k: (k, chunk)),
        out_shape=jax.ShapeDtypeStruct(shape, jnp.bfloat16),
        scratch_shapes=gathered_scratch(slots),
        input_output_aliases={} if so_far is None else {7: 0},
        compiler_params=params(24),
        cost_estimate=cost(height * span, 4 * height * span),
        name="finish",
    )(*operands)


def shifted(value, axis, pairs):
    return lax.ppermute(value, axis, pairs)


def ring(piece, axis, up):
    down = [(d, s) for s, d in up]
    before = lax.ppermute(piece, axis, up)
    after = lax.ppermute(piece, axis, down)
    cut = piece.shape[0] // 2
    far_top = lax.ppermute(before[:cut], axis, up)
    far_bottom = lax.ppermute(after[cut:], axis, down)
    return before, after, far_top, far_bottom


COL_UP = [(i, (i + 1) % SIDE) for i in range(SIDE)]
Z_UP = [(z * SIDE + y, (z + 1) % SIDE * SIDE + y) for z in range(SIDE) for y in range(SIDE)]
Y_UP = [(z * SIDE + y, z * SIDE + (y + 1) % SIDE) for z in range(SIDE) for y in range(SIDE)]


def gather_col(packed):
    return [packed, *ring(packed, "col", COL_UP)]


def gather_rep(packed, chunk):
    one, two = (Z_UP, Y_UP) if chunk == 0 else (Y_UP, Z_UP)
    before, after, far_top, far_bottom = ring(packed, "rep", one)
    far = jnp.concatenate([far_top, far_bottom], axis=0)
    payload = jnp.stack([packed, before, after, far])
    return [payload, *ring(payload, "rep", two)]


def by_place(gathered, here):
    order = (here + jnp.array(PLACES)) % SIDE
    return jnp.take(gathered, order, axis=0)


def gather_col_any(packed):
    placed = by_place(lax.all_gather(packed, "col", axis=0), lax.axis_index("col"))
    cut = packed.shape[0] // 2
    return [placed[0], placed[1], placed[2], placed[3, :cut], placed[3, cut:]]


def gather_rep_any(packed, chunk):
    rep = lax.axis_index("rep")
    gathered = lax.all_gather(packed, "rep", axis=0).reshape(SIDE, SIDE, *packed.shape)
    placed = by_place(gathered, rep // SIDE).swapaxes(0, 1)
    placed = by_place(placed, rep % SIDE)
    if chunk == 1:
        placed = placed.swapaxes(0, 1)
    cut = SIDE // 2
    return [placed[0], placed[1], placed[2], placed[3, :cut], placed[3, cut:]]


def swap(part):
    return lax.ppermute(part, "row", [(0, 1), (1, 0)])


def newton_step(hamiltonian, pattern, pats, caps, gathers):
    height, width = hamiltonian.shape
    row_cap, chunk_cap = caps
    over_col, over_rep = gathers
    span = width // CHUNKS
    units = width // (2 * BS)
    rep = lax.axis_index("rep").reshape(1)
    where = jnp.stack([lax.axis_index("row"), lax.axis_index("col"), lax.axis_index("rep")])

    picked = over_col(pick(rep, pattern, hamiltonian, row_cap))
    current = mask_tile(pattern, hamiltonian)
    rows = unpack_rows(where, pats, picked, height, units, row_cap)
    square, new = [], []
    for c in range(CHUNKS):
        own, other = square_part(rows, current, c, span)
        square.append(over_rep(pack(rep, pattern, own, swap(other), c, chunk_cap), c))
    for c in range(CHUNKS):
        own, other = cube_part(rep, pattern, rows, square[c], c, span, chunk_cap)
        new.append(over_rep(pack(rep, pattern, own, swap(other), c, chunk_cap, hamiltonian), c))
    return rep, new


def shards(hamiltonian, pattern):
    shape = hamiltonian.shape
    width = shape[1]
    span = width // CHUNKS
    blocks = span // BS
    row_full = width // (2 * BS) * pattern.shape[0]
    chunk_full = pattern.shape[0] // 2 * blocks

    pats = jnp.stack(
        [pattern]
        + [lax.ppermute(pattern, "col", [(i, (i - a) % SIDE) for i in range(SIDE)]) for a in PLACES[1:]]
    )
    by_parity = pats.reshape(SIDE, -1, 2, CHUNKS, blocks)
    chunk_most = jnp.max(jnp.sum(by_parity, axis=(1, 4)))
    row_most = jnp.max(jnp.sum(pats.reshape(SIDE, -1, width // (2 * BS), 2), axis=(1, 2)))
    excess = jnp.maximum(chunk_most - CHUNK_CAP, row_most - ROW_CAP).reshape(1)
    excess = jnp.maximum(excess, lax.ppermute(excess, "row", [(0, 1), (1, 0)]))[0]

    rep, new = newton_step(
        hamiltonian, pattern, pats, (ROW_CAP, CHUNK_CAP), (gather_col, gather_rep)
    )
    so_far = finish(rep, pattern, new[0], shape, 0, CHUNK_CAP)

    def fits(hamiltonian, pattern, pats, rep, pieces, so_far):
        return finish(rep, pattern, pieces, shape, 1, CHUNK_CAP, so_far)

    def any_pattern(hamiltonian, pattern, pats, rep, pieces, so_far):
        caps = (row_full, (chunk_full + 7) // 8 * 8)
        rep, new = newton_step(hamiltonian, pattern, pats, caps, (gather_col_any, gather_rep_any))
        out = finish(rep, pattern, new[0], shape, 0, caps[1])
        return finish(rep, pattern, new[1], shape, 1, caps[1], out)

    return lax.cond(
        excess > 0, any_pattern, fits, hamiltonian, pattern, pats, rep, new[1], so_far
    )


def solution(mesh):
    in_specs = (P("row", "col"), P("row", "col"))
    out_specs = P("row", "col")
    return jax.shard_map(shards, mesh=mesh, in_specs=in_specs, out_specs=out_specs, check_vma=False)
```

```python
import functools

import jax
import jax.numpy as jnp
from jax import lax
from jax.experimental import pallas as pl
from jax.experimental.pallas import tpu as pltpu
from jax.sharding import PartitionSpec as P

BS = 128
UNIT = 16
UNITS = BS // UNIT
SIDE = 4
CHUNKS = 2
ROW_CAP = 120
CHUNK_CAP = 64
MIB = 1024 * 1024
SMEM_SPEC = pl.BlockSpec(memory_space=pltpu.SMEM)
ANY_SPEC = pl.BlockSpec(memory_space=pl.ANY)
PIECES = 5
PLACES = (0, 3, 1, 2)


def params(mib):
    return pltpu.CompilerParams(vmem_limit_bytes=mib * MIB)


def cost(flops, moved):
    return pl.CostEstimate(flops=flops, bytes_accessed=moved, transcendentals=0)


def whole(shape):
    return pl.BlockSpec(shape, lambda *_: (0,) * len(shape))


def place_of(there, here):
    away = (there - here + SIDE) % SIDE
    return jnp.where(away == 0, 0, jnp.where(away == 3, 1, away + 1))


def free_slot(kept, count, slots):
    return jnp.where(kept != 0, jnp.minimum(count, slots - 1), slots)


def pick_kernel(rep_ref, pat_ref, h_ref, out_ref, held_ref, count_ref, *, slots):
    step = pl.program_id(0)

    @pl.when(step == 0)
    def _():
        held_ref[...] = jnp.zeros_like(held_ref)
        count_ref[0] = 0

    first = (rep_ref[0] % UNITS) * UNIT
    u = lax.broadcasted_iota(jnp.int32, (UNIT, BS), 0)
    c = lax.broadcasted_iota(jnp.int32, (UNIT, BS), 1)
    chosen = jnp.where(c == u + first, 1.0, 0.0).astype(jnp.bfloat16)
    block_col = 2 * step + rep_ref[0] // UNITS
    turned = lax.dot_general(
        chosen, h_ref[...], (((1,), (1,)), ((), ())), preferred_element_type=jnp.float32
    ).astype(jnp.bfloat16)
    count = count_ref[0]
    for a in range(h_ref.shape[0] // BS):
        kept = pat_ref[a, block_col]
        held_ref[free_slot(kept, count, slots)] = turned[:, a * BS : (a + 1) * BS]
        count = count + kept
    count_ref[0] = count

    @pl.when(step == pl.num_programs(0) - 1)
    def _():
        out_ref[...] = held_ref[:slots]


def pick(rep, pattern, tile, slots):
    height, width = tile.shape
    return pl.pallas_call(
        functools.partial(pick_kernel, slots=slots),
        grid_spec=pltpu.PrefetchScalarGridSpec(
            num_scalar_prefetch=2,
            grid=(width // (2 * BS),),
            in_specs=[pl.BlockSpec((height, BS), lambda j, rep, pat: (0, 2 * j + rep[0] // UNITS))],
            out_specs=whole((slots, UNIT, BS)),
            scratch_shapes=[
                pltpu.VMEM((slots + 1, UNIT, BS), jnp.bfloat16),
                pltpu.SMEM((1,), jnp.int32),
            ],
        ),
        out_shape=jax.ShapeDtypeStruct((slots, UNIT, BS), jnp.bfloat16),
        compiler_params=params(16),
        cost_estimate=cost(2 * UNIT * height * width, height * width),
        name="pick",
    )(rep, pattern, tile)


def rows_kernel(where_ref, table_ref, *rest, slots):
    pieces, (out_ref, held_ref, sems) = rest[:5], rest[5:]
    half = slots // 2
    targets = (
        held_ref.at[0, pl.ds(0, slots)],
        held_ref.at[1, pl.ds(0, slots)],
        held_ref.at[2, pl.ds(0, slots)],
        held_ref.at[3, pl.ds(0, half)],
        held_ref.at[3, pl.ds(half, half)],
    )
    copies = [
        pltpu.make_async_copy(piece, target, sems.at[n])
        for n, (piece, target) in enumerate(zip(pieces, targets))
    ]
    for copy in copies:
        copy.start()
    held_ref[:, slots] = jnp.zeros_like(held_ref[:, slots])
    for copy in copies:
        copy.wait()
    row, col = where_ref[0], where_ref[1]
    cols, units = SIDE, out_ref.shape[0] // (SIDE * UNIT)
    blocks = out_ref.shape[1] // BS
    for n, away in enumerate(PLACES):
        place = ((col + away) % cols + cols - row * (cols // 2)) % cols

        def unit(j, carry, n=n, place=place):
            start = pl.multiple_of((place * units + j) * UNIT, UNIT)
            values = [held_ref[n, table_ref[n, j * blocks + a]] for a in range(blocks)]
            for a, value in enumerate(values):
                out_ref[pl.ds(start, UNIT), pl.ds(a * BS, BS)] = value
            return carry

        lax.fori_loop(0, units, unit, 0)


def unpack_rows(where, table, pieces, height, units, slots):
    shape = (SIDE * units * UNIT, height)
    return pl.pallas_call(
        functools.partial(rows_kernel, slots=slots),
        in_specs=[SMEM_SPEC, SMEM_SPEC] + [ANY_SPEC] * 5,
        out_specs=pl.BlockSpec(memory_space=pltpu.VMEM),
        out_shape=jax.ShapeDtypeStruct(shape, jnp.bfloat16),
        scratch_shapes=[
            pltpu.VMEM((SIDE, slots + 1, UNIT, BS), jnp.bfloat16),
            pltpu.SemaphoreType.DMA((5,)),
        ],
        compiler_params=params(16),
        name="unpack_rows",
    )(where, table, *pieces)


def accumulate(acc_ref, left, right, own_ref, other_ref):
    step = pl.program_id(0)
    half = own_ref.shape[0]
    part = jnp.dot(left, right, preferred_element_type=jnp.float32)

    @pl.when(step == 0)
    def _():
        acc_ref[...] = part

    @pl.when(step != 0)
    def _():
        acc_ref[...] += part

    @pl.when(step == pl.num_programs(0) - 1)
    def _():
        own_ref[...] = acc_ref[:half]
        other_ref[...] = acc_ref[half:].astype(jnp.bfloat16)


def part_outputs(depth, span):
    specs = [whole((depth // 2, span))] * 2
    shapes = [
        jax.ShapeDtypeStruct((depth // 2, span), jnp.float32),
        jax.ShapeDtypeStruct((depth // 2, span), jnp.bfloat16),
    ]
    return specs, shapes


def square_kernel(pat_ref, g_ref, h_ref, own_ref, other_ref, x_ref, acc_ref, *, chunk):
    block_rows, block_cols = h_ref.shape[0] // BS, h_ref.shape[1] // BS
    for a in range(block_rows):
        for b in range(block_cols):
            kept = pat_ref[pl.program_id(0) * block_rows + a, chunk * block_cols + b]
            block = pl.ds(a * BS, BS), pl.ds(b * BS, BS)

            @pl.when(kept != 0)
            def _():
                x_ref[block] = h_ref[block]

            @pl.when(kept == 0)
            def _():
                x_ref[block] = jnp.zeros((BS, BS), jnp.bfloat16)

    accumulate(acc_ref, g_ref[...], x_ref[...], own_ref, other_ref)


def square_part(pattern, rows, tile, chunk, span, stripe=512):
    depth, height = rows.shape
    specs, shapes = part_outputs(depth, span)
    return pl.pallas_call(
        functools.partial(square_kernel, chunk=chunk),
        grid=(height // stripe,),
        in_specs=[
            SMEM_SPEC,
            pl.BlockSpec((depth, stripe), lambda k: (0, k)),
            pl.BlockSpec((stripe, span), lambda k: (k, chunk)),
        ],
        out_specs=specs,
        out_shape=shapes,
        scratch_shapes=[
            pltpu.VMEM((stripe, span), jnp.bfloat16),
            pltpu.VMEM((depth, span), jnp.float32),
        ],
        compiler_params=params(24),
        cost_estimate=cost(2 * depth * height * span, 2 * height * (span + depth) + 3 * depth * span),
        name="square_part",
    )(pattern, rows, tile)


def pack_kernel(rep_ref, table_ref, own_ref, other_ref, *rest, slots, first, last):
    tile_ref, out_ref, held_ref = rest if last else (None, *rest)
    rows, width = own_ref.shape
    parity = rep_ref[0] // UNITS
    held_ref[...] = jnp.zeros_like(held_ref)
    for j in range(rows // UNIT):
        for b in range(width // BS):
            part, cols = pl.ds(j * UNIT, UNIT), pl.ds(b * BS, BS)
            value = own_ref[part, cols] + other_ref[part, cols].astype(jnp.float32)
            if last:
                value = 1.5 * tile_ref[j, 0, :, cols].astype(jnp.float32) - 0.5 * value
            held_ref[table_ref[2 * j + parity, first + b]] = value.astype(jnp.bfloat16)
    out_ref[...] = held_ref[:slots]


def pack(rep, table, own, other, chunk, slots, tile=None):
    rows, span = own.shape
    in_specs = [whole(own.shape), whole(other.shape)]
    operands = [own, other]
    if tile is not None:
        reps = tile.shape[0] // rows
        operands.append(tile.reshape(rows // UNIT, reps, UNIT, tile.shape[1]))
        in_specs.append(
            pl.BlockSpec((rows // UNIT, 1, UNIT, span), lambda i, rep, tab: (0, rep[0], 0, chunk))
        )
    return pl.pallas_call(
        functools.partial(
            pack_kernel, slots=slots, first=chunk * span // BS, last=tile is not None
        ),
        grid_spec=pltpu.PrefetchScalarGridSpec(
            num_scalar_prefetch=2,
            grid=(1,),
            in_specs=in_specs,
            out_specs=whole((slots, UNIT, BS)),
            scratch_shapes=[pltpu.VMEM((slots + 1, UNIT, BS), jnp.bfloat16)],
        ),
        out_shape=jax.ShapeDtypeStruct((slots, UNIT, BS), jnp.bfloat16),
        compiler_params=params(16),
        cost_estimate=cost(4 * rows * span, 8 * rows * span),
        name="pack",
    )(rep, table, *operands)


def fill(pieces, held_ref, sems, slots):
    low, high = pl.ds(0, SIDE // 2), pl.ds(SIDE // 2, SIDE // 2)
    used = pl.ds(0, slots)
    targets = [held_ref.at[:, place, used] for place in range(SIDE - 1)]
    targets += [held_ref.at[low, SIDE - 1, used], held_ref.at[high, SIDE - 1, used]]
    copies = [
        pltpu.make_async_copy(piece, target, sems.at[n])
        for n, (piece, target) in enumerate(zip(pieces, targets))
    ]
    for copy in copies:
        copy.start()
    held_ref[:, :, slots] = jnp.zeros_like(held_ref[:, :, slots])
    for copy in copies:
        copy.wait()


def unpack(rep_ref, table_ref, held_ref, out_ref, chunk):
    step = pl.program_id(0)
    z, y = rep_ref[0] // SIDE, rep_ref[0] % SIDE
    place_z = [place_of(i, z) for i in range(SIDE)]
    place_y = [place_of(i, y) for i in range(SIDE)]
    block_rows, block_cols = out_ref.shape[0] // BS, out_ref.shape[1] // BS
    for a in range(block_rows):
        slots = [table_ref[step * block_rows + a, chunk * block_cols + b] for b in range(block_cols)]
        for u in range(0, UNITS, SIDE):
            values = {}
            for v in range(u, u + SIDE):
                source = a % 2 * UNITS + v
                places = place_z[source // SIDE], place_y[source % SIDE]
                first, second = places if chunk == 0 else places[::-1]
                for b, slot in enumerate(slots):
                    values[v, b] = held_ref[first, second, slot]
            for (v, b), value in values.items():
                out_ref[pl.ds(a * BS + v * UNIT, UNIT), pl.ds(b * BS, BS)] = value


def begin(pieces, held_ref, sems, slots):
    @pl.when(pl.program_id(0) == 0)
    def _():
        fill(pieces, held_ref, sems, slots)


def gathered_scratch(slots):
    return [
        pltpu.VMEM((SIDE, SIDE, slots + 1, UNIT, BS), jnp.bfloat16),
        pltpu.SemaphoreType.DMA((PIECES,)),
    ]


def cube_kernel(rep_ref, table_ref, g_ref, *rest, chunk, slots):
    pieces, rest = rest[:PIECES], rest[PIECES:]
    own_ref, other_ref, held_ref, sems, square_ref, acc_ref = rest
    begin(pieces, held_ref, sems, slots)
    unpack(rep_ref, table_ref, held_ref, square_ref, chunk)
    accumulate(acc_ref, g_ref[...], square_ref[...], own_ref, other_ref)


def cube_part(rep, table, rows, pieces, chunk, span, slots, stripe=512):
    depth, height = rows.shape
    specs, shapes = part_outputs(depth, span)
    return pl.pallas_call(
        functools.partial(cube_kernel, chunk=chunk, slots=slots),
        grid=(height // stripe,),
        in_specs=[SMEM_SPEC, SMEM_SPEC, pl.BlockSpec((depth, stripe), lambda k: (0, k))]
        + [ANY_SPEC] * PIECES,
        out_specs=specs,
        out_shape=shapes,
        scratch_shapes=gathered_scratch(slots)
        + [pltpu.VMEM((stripe, span), jnp.bfloat16), pltpu.VMEM((depth, span), jnp.float32)],
        compiler_params=params(24),
        cost_estimate=cost(2 * depth * height * span, 2 * height * (span + depth) + 3 * depth * span),
        name="cube_part",
    )(rep, table, rows, *pieces)


def finish_kernel(rep_ref, table_ref, *rest, chunk, slots):
    pieces, (out_ref, held_ref, sems) = rest[:PIECES], rest[-3:]
    begin(pieces, held_ref, sems, slots)
    unpack(rep_ref, table_ref, held_ref, out_ref, chunk)


def finish(rep, table, pieces, shape, chunk, slots, so_far=None, stripe=512):
    height, width = shape
    span = width // CHUNKS
    operands = [rep, table, *pieces] + ([] if so_far is None else [so_far])
    return pl.pallas_call(
        functools.partial(finish_kernel, chunk=chunk, slots=slots),
        grid=(height // stripe,),
        in_specs=[SMEM_SPEC, SMEM_SPEC] + [ANY_SPEC] * (len(operands) - 2),
        out_specs=pl.BlockSpec((stripe, span), lambda k: (k, chunk)),
        out_shape=jax.ShapeDtypeStruct(shape, jnp.bfloat16),
        scratch_shapes=gathered_scratch(slots),
        input_output_aliases={} if so_far is None else {2 + PIECES: 0},
        compiler_params=params(24),
        cost_estimate=cost(height * span, 4 * height * span),
        name="finish",
    )(*operands)


COL_UP = [(i, (i + 1) % SIDE) for i in range(SIDE)]
Z_UP = [(z * SIDE + y, (z + 1) % SIDE * SIDE + y) for z in range(SIDE) for y in range(SIDE)]
Y_UP = [(z * SIDE + y, z * SIDE + (y + 1) % SIDE) for z in range(SIDE) for y in range(SIDE)]


def both_ways(piece, axis, up):
    return [lax.ppermute(piece, axis, pairs) for pairs in (up, [(d, s) for s, d in up])]


def onward(before, after, axis, up):
    top = lax.ppermute(before, axis, up)
    return top, lax.ppermute(after, axis, [(d, s) for s, d in up])


def gather_col(packed):
    before, after = both_ways(packed, "col", COL_UP)
    cut = packed.shape[0] // 2
    return [packed, before, after, *onward(before[:cut], after[cut:], "col", COL_UP)]


def gather_rep(packed, chunk):
    one, two = (Z_UP, Y_UP) if chunk == 0 else (Y_UP, Z_UP)
    cut = packed.shape[0] // 2
    before, after = both_ways(packed, "rep", one)
    far = jnp.concatenate(onward(before[:cut], after[cut:], "rep", one), axis=0)
    payload = jnp.stack([packed, before, after, far])
    before, after = both_ways(payload, "rep", two)
    cut = SIDE // 2
    return [payload, before, after, *onward(before[:cut], after[cut:], "rep", two)]


def swap(part):
    return lax.ppermute(part, "row", [(0, 1), (1, 0)])


def tables(pats, rep, caps):
    row_cap, chunk_cap = caps

    def slots(flags, cap):
        size = flags.shape[1]
        earlier = jnp.arange(size)[:, None] < jnp.arange(size)[None, :]
        ahead = jnp.dot(
            flags.astype(jnp.bfloat16),
            earlier.astype(jnp.bfloat16),
            preferred_element_type=jnp.float32,
        ).astype(jnp.int32)
        return jnp.where(flags != 0, jnp.minimum(ahead, cap - 1), cap)

    block_rows, block_cols = pats.shape[1:]
    by_parity = pats.reshape(SIDE, block_rows, block_cols // 2, 2)
    by_parity = lax.dynamic_index_in_dim(by_parity, rep // UNITS, 3, keepdims=False)
    row_table = slots(by_parity.swapaxes(1, 2).reshape(SIDE, -1), row_cap)
    own = pats[0].reshape(block_rows // 2, 2, CHUNKS, -1).transpose(1, 2, 0, 3)
    tile_table = slots(own.reshape(2 * CHUNKS, -1), chunk_cap).reshape(own.shape)
    return row_table, tile_table.transpose(2, 0, 1, 3).reshape(block_rows, block_cols)


def newton_step(hamiltonian, pattern, pats, caps):
    height, width = hamiltonian.shape
    row_cap, chunk_cap = caps
    span = width // CHUNKS
    units = width // (2 * BS)
    rep = lax.axis_index("rep").reshape(1)
    where = jnp.stack([lax.axis_index("row"), lax.axis_index("col")])
    row_table, table = tables(pats, rep[0], caps)

    picked = gather_col(pick(rep, pattern, hamiltonian, row_cap))
    rows = unpack_rows(where, row_table, picked, height, units, row_cap)
    square, new = [], []
    for c in range(CHUNKS):
        own, other = square_part(pattern, rows, hamiltonian, c, span)
        square.append(gather_rep(pack(rep, table, own, swap(other), c, chunk_cap), c))
    for c in range(CHUNKS):
        own, other = cube_part(rep, table, rows, square[c], c, span, chunk_cap)
        new.append(gather_rep(pack(rep, table, own, swap(other), c, chunk_cap, hamiltonian), c))
    return rep, table, new


def shards(hamiltonian, pattern):
    shape = hamiltonian.shape
    width = shape[1]
    span = width // CHUNKS
    blocks = span // BS
    row_full = width // (2 * BS) * pattern.shape[0]
    chunk_full = pattern.shape[0] // 2 * blocks

    pats = jnp.stack(
        [pattern]
        + [lax.ppermute(pattern, "col", [(i, (i - a) % SIDE) for i in range(SIDE)]) for a in PLACES[1:]]
    )
    by_parity = pats.reshape(SIDE, -1, 2, CHUNKS, blocks)
    chunk_most = jnp.max(jnp.sum(by_parity, axis=(1, 4)))
    row_most = jnp.max(jnp.sum(pats.reshape(SIDE, -1, width // (2 * BS), 2), axis=(1, 2)))
    excess = jnp.maximum(chunk_most - CHUNK_CAP, row_most - ROW_CAP).reshape(1)
    excess = jnp.maximum(excess, lax.ppermute(excess, "row", [(0, 1), (1, 0)]))[0]
    excess, placed = lax.optimization_barrier((excess, pats))

    rep, table, new = newton_step(hamiltonian, pattern, placed, (ROW_CAP, CHUNK_CAP))
    so_far = finish(rep, table, new[0], shape, 0, CHUNK_CAP)

    def fits(hamiltonian, pattern, pats, rep, table, pieces, so_far):
        return finish(rep, table, pieces, shape, 1, CHUNK_CAP, so_far)

    def any_pattern(hamiltonian, pattern, pats, rep, table, pieces, so_far):
        caps = (row_full, (chunk_full + 7) // 8 * 8)
        rep, table, new = newton_step(hamiltonian, pattern, pats, caps)
        out = finish(rep, table, new[0], shape, 0, caps[1])
        return finish(rep, table, new[1], shape, 1, caps[1], out)

    return lax.cond(
        excess > 0, any_pattern, fits, hamiltonian, pattern, pats, rep, table, new[1], so_far
    )


def solution(mesh):
    in_specs = (P("row", "col"), P("row", "col"))
    out_specs = P("row", "col")
    return jax.shard_map(shards, mesh=mesh, in_specs=in_specs, out_specs=out_specs, check_vma=False)
```

```python
import functools

import jax
import jax.numpy as jnp
from jax import lax
from jax.experimental import pallas as pl
from jax.experimental.pallas import tpu as pltpu
from jax.sharding import PartitionSpec as P

BS = 128
UNIT = 16
UNITS = BS // UNIT
SIDE = 4
CHUNKS = 2
ROW_CAP = 120
CHUNK_CAP = 64
MIB = 1024 * 1024
SMEM_SPEC = pl.BlockSpec(memory_space=pltpu.SMEM)
ANY_SPEC = pl.BlockSpec(memory_space=pl.ANY)
PAIR = 2 * BS
PLACES = (0, 3, 1, 2)


def params(mib):
    return pltpu.CompilerParams(vmem_limit_bytes=mib * MIB)


def cost(flops, moved):
    return pl.CostEstimate(flops=flops, bytes_accessed=moved, transcendentals=0)


def whole(shape):
    return pl.BlockSpec(shape, lambda *_: (0,) * len(shape))


def place_of(there, here):
    away = (there - here + SIDE) % SIDE
    return jnp.where(away == 0, 0, jnp.where(away == 3, 1, away + 1))


def free_slot(kept, count, slots):
    return jnp.where(kept != 0, jnp.minimum(count, slots - 1), slots)


def pick_kernel(rep_ref, pat_ref, h_ref, out_ref, held_ref, count_ref, *, slots):
    step = pl.program_id(0)

    @pl.when(step == 0)
    def _():
        held_ref[...] = jnp.zeros_like(held_ref)
        count_ref[0] = 0

    first = (rep_ref[0] % UNITS) * UNIT
    u = lax.broadcasted_iota(jnp.int32, (UNIT, BS), 0)
    c = lax.broadcasted_iota(jnp.int32, (UNIT, BS), 1)
    chosen = jnp.where(c == u + first, 1.0, 0.0).astype(jnp.bfloat16)
    block_col = 2 * step + rep_ref[0] // UNITS
    turned = lax.dot_general(
        chosen, h_ref[...], (((1,), (1,)), ((), ())), preferred_element_type=jnp.float32
    ).astype(jnp.bfloat16)
    count = count_ref[0]
    for a in range(h_ref.shape[0] // BS):
        kept = pat_ref[a, block_col]
        held_ref[free_slot(kept, count, slots)] = turned[:, a * BS : (a + 1) * BS]
        count = count + kept
    count_ref[0] = count

    @pl.when(step == pl.num_programs(0) - 1)
    def _():
        out_ref[...] = held_ref[:slots]


def pick(rep, pattern, tile, slots):
    height, width = tile.shape
    return pl.pallas_call(
        functools.partial(pick_kernel, slots=slots),
        grid_spec=pltpu.PrefetchScalarGridSpec(
            num_scalar_prefetch=2,
            grid=(width // (2 * BS),),
            in_specs=[pl.BlockSpec((height, BS), lambda j, rep, pat: (0, 2 * j + rep[0] // UNITS))],
            out_specs=whole((slots, UNIT, BS)),
            scratch_shapes=[
                pltpu.VMEM((slots + 1, UNIT, BS), jnp.bfloat16),
                pltpu.SMEM((1,), jnp.int32),
            ],
        ),
        out_shape=jax.ShapeDtypeStruct((slots, UNIT, BS), jnp.bfloat16),
        compiler_params=params(16),
        cost_estimate=cost(2 * UNIT * height * width, height * width),
        name="pick",
    )(rep, pattern, tile)


def excess_kernel(*refs):
    pats, out_ref = refs[:-1], refs[-1]
    row = lax.broadcasted_iota(jnp.int32, pats[0].shape, 0)
    col = lax.broadcasted_iota(jnp.int32, pats[0].shape, 1)
    span = pats[0].shape[1] // CHUNKS
    most = jnp.int32(-(2**30))
    for pat in pats:
        flags = pat[...]
        for p in range(2):
            most = jnp.maximum(most, jnp.sum(jnp.where(col % 2 == p, flags, 0)) - ROW_CAP)
            for c in range(CHUNKS):
                chosen = (row % 2 == p) & (col // span == c)
                most = jnp.maximum(most, jnp.sum(jnp.where(chosen, flags, 0)) - CHUNK_CAP)
    out_ref[...] = jnp.full(out_ref.shape, most, jnp.int32)


def over_caps(pats):
    return pl.pallas_call(
        excess_kernel,
        in_specs=[pl.BlockSpec(memory_space=pltpu.VMEM)] * len(pats),
        out_specs=pl.BlockSpec(memory_space=pltpu.VMEM),
        out_shape=jax.ShapeDtypeStruct((8, BS), jnp.int32),
        compiler_params=params(4),
        name="over_caps",
    )(*pats)


def rows_kernel(row_ref, col_ref, rep_ref, *rest, slots):
    pats, pieces, (out_ref, held_ref, sems) = rest[:SIDE], rest[SIDE : SIDE + 5], rest[SIDE + 5 :]
    half = slots // 2
    targets = (
        held_ref.at[0, pl.ds(0, slots)],
        held_ref.at[1, pl.ds(0, slots)],
        held_ref.at[2, pl.ds(0, slots)],
        held_ref.at[3, pl.ds(0, half)],
        held_ref.at[3, pl.ds(half, half)],
    )
    copies = [
        pltpu.make_async_copy(piece, target, sems.at[n])
        for n, (piece, target) in enumerate(zip(pieces, targets))
    ]
    for copy in copies:
        copy.start()
    held_ref[:, slots] = jnp.zeros_like(held_ref[:, slots])
    for copy in copies:
        copy.wait()
    row, col, rep = row_ref[0], col_ref[0], rep_ref[0]
    cols, units = SIDE, out_ref.shape[0] // (SIDE * UNIT)
    parity = rep // UNITS
    for n, away in enumerate(PLACES):
        place = ((col + away) % cols + cols - row * (cols // 2)) % cols

        def unit(j, count, n=n, place=place):
            start = pl.multiple_of((place * units + j) * UNIT, UNIT)
            values = []
            for a in range(out_ref.shape[1] // BS):
                kept = pats[n][a, 2 * j + parity]
                values.append(held_ref[n, free_slot(kept, count, slots)])
                count = count + kept
            for a, value in enumerate(values):
                out_ref[pl.ds(start, UNIT), pl.ds(a * BS, BS)] = value
            return count

        lax.fori_loop(0, units, unit, jnp.int32(0))


def unpack_rows(where, pats, pieces, height, units, slots):
    shape = (SIDE * units * UNIT, height)
    return pl.pallas_call(
        functools.partial(rows_kernel, slots=slots),
        in_specs=[SMEM_SPEC] * (3 + SIDE) + [ANY_SPEC] * 5,
        out_specs=pl.BlockSpec(memory_space=pltpu.VMEM),
        out_shape=jax.ShapeDtypeStruct(shape, jnp.bfloat16),
        scratch_shapes=[
            pltpu.VMEM((SIDE, slots + 1, UNIT, BS), jnp.bfloat16),
            pltpu.SemaphoreType.DMA((5,)),
        ],
        compiler_params=params(16),
        name="unpack_rows",
    )(*where, *pats, *pieces)


def put_parts(rows, right, own_ref, other_ref):
    half = own_ref.shape[0]
    acc = jnp.dot(rows, right, preferred_element_type=jnp.float32)
    own_ref[...] = acc[:half]
    other_ref[...] = acc[half:].astype(jnp.bfloat16)


def part_outputs(depth, chunk, width):
    first, last = chunk * width // (2 * PAIR), -(-(chunk + 1) * width // (2 * PAIR))
    block = pl.BlockSpec((depth // 2, PAIR), lambda i: (0, i))
    span = (last - first) * PAIR
    shapes = [
        jax.ShapeDtypeStruct((depth // 2, span), jnp.float32),
        jax.ShapeDtypeStruct((depth // 2, span), jnp.bfloat16),
    ]
    return first, last - first, [block, block], shapes


def square_kernel(pat_ref, g_ref, h_ref, own_ref, other_ref, x_ref, *, first):
    for a in range(h_ref.shape[0] // BS):
        for b in range(h_ref.shape[1] // BS):
            kept = pat_ref[a, (first + pl.program_id(0)) * (PAIR // BS) + b].astype(jnp.float32)
            block = pl.ds(a * BS, BS), pl.ds(b * BS, BS)
            x_ref[block] = h_ref[block] * jnp.full((BS, BS), kept, jnp.float32).astype(jnp.bfloat16)
    put_parts(g_ref[...], x_ref[...], own_ref, other_ref)


def square_part(pattern, rows, tile, chunk):
    depth, height = rows.shape
    first, pairs, specs, shapes = part_outputs(depth, chunk, tile.shape[1])
    return pl.pallas_call(
        functools.partial(square_kernel, first=first),
        grid=(pairs,),
        in_specs=[
            SMEM_SPEC,
            whole(rows.shape),
            pl.BlockSpec((height, PAIR), lambda i: (0, first + i)),
        ],
        out_specs=specs,
        out_shape=shapes,
        scratch_shapes=[pltpu.VMEM((height, PAIR), jnp.bfloat16)],
        compiler_params=params(32),
        cost_estimate=cost(2 * depth * height * PAIR * pairs, 2 * height * (PAIR * pairs + depth)),
        name="square_part",
    )(pattern, rows, tile)


def pack_kernel(rep_ref, pat_ref, own_ref, other_ref, *rest, slots, chunk, offset, last):
    tile_ref, out_ref, held_ref = rest if last else (None, *rest)
    units, blocks = own_ref.shape[0] // UNIT, pat_ref.shape[1] // CHUNKS
    parity = rep_ref[0] // UNITS
    held_ref[...] = jnp.zeros_like(held_ref)
    count = jnp.int32(0)
    order = [(j, b) for b in range(blocks) for j in range(units)]
    for j, b in sorted(order) if last else order:
        kept = pat_ref[2 * j + parity, chunk * blocks + b]
        part, cols = pl.ds(j * UNIT, UNIT), pl.ds(offset + b * BS, BS)
        value = own_ref[part, cols] + other_ref[part, cols].astype(jnp.float32)
        if last:
            value = 1.5 * tile_ref[j, 0, :, pl.ds(b * BS, BS)].astype(jnp.float32) - 0.5 * value
        held_ref[free_slot(kept, count, slots)] = value.astype(jnp.bfloat16)
        count = count + kept
    out_ref[...] = held_ref[:slots]


def pack(rep, pattern, own, other, chunk, slots, width, tile=None):
    rows = own.shape[0]
    in_specs = [whole(own.shape), whole(other.shape)]
    operands = [own, other]
    span = width // CHUNKS
    if tile is not None:
        reps = tile.shape[0] // rows
        operands.append(tile.reshape(rows // UNIT, reps, UNIT, width))
        in_specs.append(
            pl.BlockSpec((rows // UNIT, 1, UNIT, span), lambda i, rep, pat: (0, rep[0], 0, chunk))
        )
    return pl.pallas_call(
        functools.partial(
            pack_kernel, slots=slots, chunk=chunk, offset=chunk * span % PAIR, last=tile is not None
        ),
        grid_spec=pltpu.PrefetchScalarGridSpec(
            num_scalar_prefetch=2,
            grid=(1,),
            in_specs=in_specs,
            out_specs=whole((slots, UNIT, BS)),
            scratch_shapes=[pltpu.VMEM((slots + 1, UNIT, BS), jnp.bfloat16)],
        ),
        out_shape=jax.ShapeDtypeStruct((slots, UNIT, BS), jnp.bfloat16),
        compiler_params=params(16),
        cost_estimate=cost(4 * rows * span, 8 * rows * span),
        name="pack",
    )(rep, pattern, *operands)


def fill(pieces, held_ref, sems, slots):
    low, high = pl.ds(0, SIDE // 2), pl.ds(SIDE // 2, SIDE // 2)
    used = pl.ds(0, slots)
    targets = [held_ref.at[:, place, used] for place in range(SIDE - 1)]
    targets += [held_ref.at[low, SIDE - 1, used], held_ref.at[high, SIDE - 1, used]]
    copies = [
        pltpu.make_async_copy(piece, target, sems.at[n])
        for n, (piece, target) in enumerate(zip(pieces, targets))
    ]
    for copy in copies:
        copy.start()
    held_ref[:, :, slots] = jnp.zeros_like(held_ref[:, :, slots])
    for copy in copies:
        copy.wait()


def places_of(rep_ref, chunk):
    z, y = rep_ref[0] // SIDE, rep_ref[0] % SIDE
    place_z = [place_of(i, z) for i in range(SIDE)]
    place_y = [place_of(i, y) for i in range(SIDE)]
    both = [(place_z[s // SIDE], place_y[s % SIDE]) for s in range(SIDE * SIDE)]
    return both if chunk == 0 else [places[::-1] for places in both]


def unpack(places, held_ref, out_ref, parity, blocks):
    for u in range(0, UNITS, SIDE):
        values = {}
        for v in range(u, u + SIDE):
            first, second = places[parity * UNITS + v]
            for row, col, slot in blocks:
                values[row + v * UNIT, col] = held_ref[first, second, slot]
        for (row, col), value in values.items():
            out_ref[pl.ds(row, UNIT), pl.ds(col, BS)] = value


def begin(pieces, held_ref, count_ref, sems, slots):
    @pl.when(pl.program_id(0) == 0)
    def _():
        fill(pieces, held_ref, sems, slots)
        count_ref[0] = 0
        count_ref[1] = 0


def gathered_scratch(slots):
    return [
        pltpu.VMEM((SIDE, SIDE, slots + 1, UNIT, BS), jnp.bfloat16),
        pltpu.SMEM((2,), jnp.int32),
        pltpu.SemaphoreType.DMA((5,)),
    ]


def cube_kernel(rep_ref, pat_ref, g_ref, *rest, chunk, first, slots):
    pieces, (own_ref, other_ref, held_ref, count_ref, sems, square_ref) = rest[:5], rest[5:]
    begin(pieces, held_ref, count_ref, sems, slots)
    places = places_of(rep_ref, chunk)
    blocks = pat_ref.shape[1] // CHUNKS
    for b in range(PAIR // BS):
        col = (first + pl.program_id(0)) * (PAIR // BS) + b

        @pl.when(col // blocks == chunk)
        def _(b=b, col=col):
            counts = [count_ref[0], count_ref[1]]
            for i in range(0, pat_ref.shape[0], SIDE):
                taken = [[], []]
                for a in range(i, i + SIDE):
                    kept = pat_ref[a, col]
                    slot = free_slot(kept, counts[a % 2], slots)
                    taken[a % 2].append((a * BS, b * BS, slot))
                    counts[a % 2] = counts[a % 2] + kept
                for parity in range(2):
                    unpack(places, held_ref, square_ref, parity, taken[parity])
            count_ref[0], count_ref[1] = counts

        @pl.when(col // blocks != chunk)
        def _(b=b):
            square_ref[:, b * BS : (b + 1) * BS] = jnp.zeros((square_ref.shape[0], BS), jnp.bfloat16)

    put_parts(g_ref[...], square_ref[...], own_ref, other_ref)


def cube_part(rep, pattern, rows, pieces, chunk, width, slots):
    depth, height = rows.shape
    first, pairs, specs, shapes = part_outputs(depth, chunk, width)
    return pl.pallas_call(
        functools.partial(cube_kernel, chunk=chunk, first=first, slots=slots),
        grid=(pairs,),
        in_specs=[SMEM_SPEC, SMEM_SPEC, whole(rows.shape)] + [ANY_SPEC] * 5,
        out_specs=specs,
        out_shape=shapes,
        scratch_shapes=gathered_scratch(slots) + [pltpu.VMEM((height, PAIR), jnp.bfloat16)],
        compiler_params=params(32),
        cost_estimate=cost(2 * depth * height * PAIR * pairs, 2 * height * (PAIR * pairs + depth)),
        name="cube_part",
    )(rep, pattern, rows, *pieces)


def finish_kernel(rep_ref, pat_ref, *rest, chunk, slots):
    pieces, (out_ref, held_ref, count_ref, sems) = rest[:5], rest[-4:]
    begin(pieces, held_ref, count_ref, sems, slots)
    places = places_of(rep_ref, chunk)
    counts = [count_ref[0], count_ref[1]]
    block_rows, block_cols = out_ref.shape[0] // BS, out_ref.shape[1] // BS
    for a in range(block_rows):
        taken = []
        for b in range(block_cols):
            kept = pat_ref[pl.program_id(0) * block_rows + a, chunk * block_cols + b]
            taken.append((a * BS, b * BS, free_slot(kept, counts[a % 2], slots)))
            counts[a % 2] = counts[a % 2] + kept
        unpack(places, held_ref, out_ref, a % 2, taken)
    count_ref[0], count_ref[1] = counts


def finish(rep, pattern, pieces, shape, chunk, slots, so_far=None, stripe=512):
    height, width = shape
    span = width // CHUNKS
    operands = [rep, pattern, *pieces] + ([] if so_far is None else [so_far])
    return pl.pallas_call(
        functools.partial(finish_kernel, chunk=chunk, slots=slots),
        grid=(height // stripe,),
        in_specs=[SMEM_SPEC, SMEM_SPEC] + [ANY_SPEC] * (len(operands) - 2),
        out_specs=pl.BlockSpec((stripe, span), lambda k: (k, chunk)),
        out_shape=jax.ShapeDtypeStruct(shape, jnp.bfloat16),
        scratch_shapes=gathered_scratch(slots),
        input_output_aliases={} if so_far is None else {7: 0},
        compiler_params=params(24),
        cost_estimate=cost(height * span, 4 * height * span),
        name="finish",
    )(*operands)


def ring(piece, axis, up):
    down = [(d, s) for s, d in up]
    before = lax.ppermute(piece, axis, up)
    after = lax.ppermute(piece, axis, down)
    cut = piece.shape[0] // 2
    far_top = lax.ppermute(before[:cut], axis, up)
    far_bottom = lax.ppermute(after[cut:], axis, down)
    return before, after, far_top, far_bottom


COL_UP = [(i, (i + 1) % SIDE) for i in range(SIDE)]
Z_UP = [(z * SIDE + y, (z + 1) % SIDE * SIDE + y) for z in range(SIDE) for y in range(SIDE)]
Y_UP = [(z * SIDE + y, z * SIDE + (y + 1) % SIDE) for z in range(SIDE) for y in range(SIDE)]


def gather_col(packed):
    return [packed, *ring(packed, "col", COL_UP)]


def gather_rep(packed, chunk):
    one, two = (Z_UP, Y_UP) if chunk == 0 else (Y_UP, Z_UP)
    before, after, far_top, far_bottom = ring(packed, "rep", one)
    far = jnp.concatenate([far_top, far_bottom], axis=0)
    payload = jnp.stack([packed, before, after, far])
    return [payload, *ring(payload, "rep", two)]


def swap(part):
    return lax.ppermute(part, "row", [(0, 1), (1, 0)])


def newton_step(hamiltonian, pattern, pats, caps):
    height, width = hamiltonian.shape
    row_cap, chunk_cap = caps
    units = width // PAIR
    rep = lax.axis_index("rep").reshape(1)
    where = [lax.axis_index(axis).reshape(1) for axis in ("row", "col")] + [rep]

    picked = gather_col(pick(rep, pattern, hamiltonian, row_cap))
    rows = unpack_rows(where, pats, picked, height, units, row_cap)
    square, new = [], []
    for c in range(CHUNKS):
        own, other = square_part(pattern, rows, hamiltonian, c)
        square.append(gather_rep(pack(rep, pattern, own, swap(other), c, chunk_cap, width), c))
    for c in range(CHUNKS):
        own, other = cube_part(rep, pattern, rows, square[c], c, width, chunk_cap)
        packed = pack(rep, pattern, own, swap(other), c, chunk_cap, width, hamiltonian)
        new.append(gather_rep(packed, c))
    return rep, new


def shards(hamiltonian, pattern):
    shape = hamiltonian.shape
    row_full = shape[1] // PAIR * pattern.shape[0]
    chunk_full = pattern.shape[0] // 2 * (pattern.shape[1] // CHUNKS)

    shifts = [[(i, (i - a) % SIDE) for i in range(SIDE)] for a in PLACES[1:]]
    pats = [pattern] + [lax.ppermute(pattern, "col", pairs) for pairs in shifts]
    excess = over_caps(pats)
    excess = jnp.maximum(excess, swap(excess))[0, 0]

    rep, new = newton_step(hamiltonian, pattern, pats, (ROW_CAP, CHUNK_CAP))
    so_far = finish(rep, pattern, new[0], shape, 0, CHUNK_CAP)

    def fits(hamiltonian, pattern, pats, rep, pieces, so_far):
        return finish(rep, pattern, pieces, shape, 1, CHUNK_CAP, so_far)

    def any_pattern(hamiltonian, pattern, pats, rep, pieces, so_far):
        caps = (row_full, (chunk_full + 7) // 8 * 8)
        rep, new = newton_step(hamiltonian, pattern, pats, caps)
        out = finish(rep, pattern, new[0], shape, 0, caps[1])
        return finish(rep, pattern, new[1], shape, 1, caps[1], out)

    return lax.cond(
        excess > 0, any_pattern, fits, hamiltonian, pattern, pats, rep, new[1], so_far
    )


def solution(mesh):
    in_specs = (P("row", "col"), P("row", "col"))
    out_specs = P("row", "col")
    return jax.shard_map(shards, mesh=mesh, in_specs=in_specs, out_specs=out_specs, check_vma=False)
```

```python
import functools

import jax
import jax.numpy as jnp
from jax import lax
from jax.experimental import pallas as pl
from jax.experimental.pallas import tpu as pltpu
from jax.sharding import PartitionSpec as P

BS = 128
UNIT = 16
UNITS = BS // UNIT
SIDE = 4
CHUNKS = 2
ROW_CAP = 120
CHUNK_CAP = 64
MIB = 1024 * 1024
SMEM_SPEC = pl.BlockSpec(memory_space=pltpu.SMEM)
ANY_SPEC = pl.BlockSpec(memory_space=pl.ANY)
PAIR = 2 * BS
PLACES = (0, 1, 3, 2)


def params(mib):
    return pltpu.CompilerParams(vmem_limit_bytes=mib * MIB)


def cost(flops, moved):
    return pl.CostEstimate(flops=flops, bytes_accessed=moved, transcendentals=0)


def whole(shape):
    return pl.BlockSpec(shape, lambda *_: (0,) * len(shape))


def place_of(there, here):
    away = there ^ here
    return away ^ (away >> 1)


def take_slot(kept, free):
    return kept * free, free + kept


def pick_kernel(rep_ref, pat_ref, h_ref, top_ref, bottom_ref, held_ref, count_ref):
    step = pl.program_id(0)

    @pl.when(step == 0)
    def _():
        held_ref[...] = jnp.zeros_like(held_ref)
        count_ref[0] = 0

    first = (rep_ref[0] % UNITS) * UNIT
    u = lax.broadcasted_iota(jnp.int32, (UNIT, BS), 0)
    c = lax.broadcasted_iota(jnp.int32, (UNIT, BS), 1)
    chosen = jnp.where(c == u + first, 1.0, 0.0).astype(jnp.bfloat16)
    block_col = 2 * step + rep_ref[0] // UNITS
    turned = lax.dot_general(
        chosen, h_ref[...], (((1,), (1,)), ((), ())), preferred_element_type=jnp.float32
    ).astype(jnp.bfloat16)
    count = count_ref[0]
    for a in range(h_ref.shape[0] // BS):
        kept = pat_ref[a, block_col]
        held_ref[count] = turned[:, a * BS : (a + 1) * BS]
        count = count + kept
    count_ref[0] = count

    @pl.when(step == pl.num_programs(0) - 1)
    def _():
        put_halves(held_ref, top_ref, bottom_ref)


def put_halves(held_ref, top_ref, bottom_ref):
    half = top_ref.shape[0]
    top_ref[...] = held_ref[:half]
    bottom_ref[...] = held_ref[half : 2 * half]


def half_outputs(slots):
    shape = (slots // 2, UNIT, BS)
    return [whole(shape)] * 2, [jax.ShapeDtypeStruct(shape, jnp.bfloat16)] * 2


def pick(rep, pattern, tile, slots):
    height, width = tile.shape
    full = width // PAIR * (height // BS)
    out_specs, out_shape = half_outputs(slots)
    return pl.pallas_call(
        pick_kernel,
        grid_spec=pltpu.PrefetchScalarGridSpec(
            num_scalar_prefetch=2,
            grid=(width // (2 * BS),),
            in_specs=[pl.BlockSpec((height, BS), lambda j, rep, pat: (0, 2 * j + rep[0] // UNITS))],
            out_specs=out_specs,
            scratch_shapes=[
                pltpu.VMEM((full + 1, UNIT, BS), jnp.bfloat16),
                pltpu.SMEM((1,), jnp.int32),
            ],
        ),
        out_shape=out_shape,
        compiler_params=params(16),
        cost_estimate=cost(2 * UNIT * height * width, height * width),
        name="pick",
    )(rep, pattern, tile)


def excess_kernel(*refs):
    pats, out_ref = refs[:-1], refs[-1]
    row = lax.broadcasted_iota(jnp.int32, pats[0].shape, 0)
    col = lax.broadcasted_iota(jnp.int32, pats[0].shape, 1)
    span = pats[0].shape[1] // CHUNKS
    most = jnp.int32(-(2**30))
    for pat in pats:
        flags = pat[...]
        for p in range(2):
            most = jnp.maximum(most, jnp.sum(jnp.where(col % 2 == p, flags, 0)) - ROW_CAP)
            for c in range(CHUNKS):
                chosen = (row % 2 == p) & (col // span == c)
                most = jnp.maximum(most, jnp.sum(jnp.where(chosen, flags, 0)) - CHUNK_CAP)
    out_ref[...] = jnp.full(out_ref.shape, most, jnp.int32)


def over_caps(pats):
    return pl.pallas_call(
        excess_kernel,
        in_specs=[pl.BlockSpec(memory_space=pltpu.VMEM)] * len(pats),
        out_specs=pl.BlockSpec(memory_space=pltpu.VMEM),
        out_shape=jax.ShapeDtypeStruct((8, BS), jnp.int32),
        compiler_params=params(4),
        name="over_caps",
    )(*pats)


def rows_kernel(row_ref, col_ref, rep_ref, *rest, slots):
    pats, pieces, (out_ref, held_ref, sems) = rest[:SIDE], rest[SIDE : SIDE + 4], rest[SIDE + 4 :]
    half = slots // 2
    top, bottom = pl.ds(1, half), pl.ds(1 + half, half)
    targets = [(pieces[0], held_ref.at[pl.ds(0, 2), top]), (pieces[1], held_ref.at[pl.ds(2, 2), top])]
    for n, place in enumerate((0, 2, 1, 3)):
        targets.append((pieces[2 + n // 2].at[n % 2], held_ref.at[place, bottom]))
    copy_all(targets, sems)
    held_ref[:, 0] = jnp.zeros_like(held_ref[:, 0])
    wait_all(targets, sems)
    row, col, rep = row_ref[0], col_ref[0], rep_ref[0]
    cols, units = SIDE, out_ref.shape[0] // (SIDE * UNIT)
    parity = rep // UNITS
    for n, away in enumerate(PLACES):
        place = ((col ^ away) + cols - row * (cols // 2)) % cols

        def unit(j, free, n=n, place=place):
            start = pl.multiple_of((place * units + j) * UNIT, UNIT)
            values = []
            for a in range(out_ref.shape[1] // BS):
                slot, free = take_slot(pats[n][a, 2 * j + parity], free)
                values.append(held_ref[n, slot])
            for a, value in enumerate(values):
                out_ref[pl.ds(start, UNIT), pl.ds(a * BS, BS)] = value
            return free

        lax.fori_loop(0, units, unit, jnp.int32(1))


def unpack_rows(where, pats, pieces, height, units, slots):
    shape = (SIDE * units * UNIT, height)
    return pl.pallas_call(
        functools.partial(rows_kernel, slots=slots),
        in_specs=[SMEM_SPEC] * (3 + SIDE) + [ANY_SPEC] * 4,
        out_specs=pl.BlockSpec(memory_space=pltpu.VMEM),
        out_shape=jax.ShapeDtypeStruct(shape, jnp.bfloat16),
        scratch_shapes=[
            pltpu.VMEM((SIDE, units * (height // BS) + 1, UNIT, BS), jnp.bfloat16),
            pltpu.SemaphoreType.DMA((6,)),
        ],
        compiler_params=params(16),
        name="unpack_rows",
    )(*where, *pats, *pieces)


def copy_all(targets, sems):
    for n, (source, target) in enumerate(targets):
        pltpu.make_async_copy(source, target, sems.at[n]).start()


def wait_all(targets, sems):
    for n, (source, target) in enumerate(targets):
        pltpu.make_async_copy(source, target, sems.at[n]).wait()


def put_parts(rows, right, own_ref, other_ref):
    half = own_ref.shape[0]
    acc = jnp.dot(rows, right, preferred_element_type=jnp.float32)
    own_ref[...] = acc[:half]
    other_ref[...] = acc[half:].astype(jnp.bfloat16)


def part_outputs(depth, chunk, width):
    first, last = chunk * width // (2 * PAIR), -(-(chunk + 1) * width // (2 * PAIR))
    block = pl.BlockSpec((depth // 2, PAIR), lambda i: (0, i))
    span = (last - first) * PAIR
    shapes = [
        jax.ShapeDtypeStruct((depth // 2, span), jnp.float32),
        jax.ShapeDtypeStruct((depth // 2, span), jnp.bfloat16),
    ]
    return first, last - first, [block, block], shapes


def square_kernel(pat_ref, g_ref, h_ref, own_ref, other_ref, x_ref, *, first):
    for a in range(h_ref.shape[0] // BS):
        for b in range(h_ref.shape[1] // BS):
            kept = pat_ref[a, (first + pl.program_id(0)) * (PAIR // BS) + b].astype(jnp.float32)
            block = pl.ds(a * BS, BS), pl.ds(b * BS, BS)
            x_ref[block] = h_ref[block] * jnp.full((BS, BS), kept, jnp.float32).astype(jnp.bfloat16)
    put_parts(g_ref[...], x_ref[...], own_ref, other_ref)


def square_part(pattern, rows, tile, chunk):
    depth, height = rows.shape
    first, pairs, specs, shapes = part_outputs(depth, chunk, tile.shape[1])
    return pl.pallas_call(
        functools.partial(square_kernel, first=first),
        grid=(pairs,),
        in_specs=[
            SMEM_SPEC,
            whole(rows.shape),
            pl.BlockSpec((height, PAIR), lambda i: (0, first + i)),
        ],
        out_specs=specs,
        out_shape=shapes,
        scratch_shapes=[pltpu.VMEM((height, PAIR), jnp.bfloat16)],
        compiler_params=params(32),
        cost_estimate=cost(2 * depth * height * PAIR * pairs, 2 * height * (PAIR * pairs + depth)),
        name="square_part",
    )(pattern, rows, tile)


def pack_kernel(rep_ref, pat_ref, own_ref, other_ref, *rest, chunk, offset, last):
    tile_ref, top_ref, bottom_ref, held_ref = rest if last else (None, *rest)
    units, blocks = own_ref.shape[0] // UNIT, pat_ref.shape[1] // CHUNKS
    parity = rep_ref[0] // UNITS
    held_ref[...] = jnp.zeros_like(held_ref)
    count = jnp.int32(0)
    order = [(j, b) for b in range(blocks) for j in range(units)]
    for j, b in sorted(order) if last else order:
        kept = pat_ref[2 * j + parity, chunk * blocks + b]
        part, cols = pl.ds(j * UNIT, UNIT), pl.ds(offset + b * BS, BS)
        value = own_ref[part, cols] + other_ref[part, cols].astype(jnp.float32)
        if last:
            value = 1.5 * tile_ref[j, 0, :, pl.ds(b * BS, BS)].astype(jnp.float32) - 0.5 * value
        held_ref[count] = value.astype(jnp.bfloat16)
        count = count + kept
    put_halves(held_ref, top_ref, bottom_ref)


def pack(rep, pattern, own, other, chunk, slots, width, tile=None):
    rows = own.shape[0]
    in_specs = [whole(own.shape), whole(other.shape)]
    operands = [own, other]
    span = width // CHUNKS
    out_specs, out_shape = half_outputs(slots)
    if tile is not None:
        reps = tile.shape[0] // rows
        operands.append(tile.reshape(rows // UNIT, reps, UNIT, width))
        in_specs.append(
            pl.BlockSpec((rows // UNIT, 1, UNIT, span), lambda i, rep, pat: (0, rep[0], 0, chunk))
        )
    return pl.pallas_call(
        functools.partial(
            pack_kernel, chunk=chunk, offset=chunk * span % PAIR, last=tile is not None
        ),
        grid_spec=pltpu.PrefetchScalarGridSpec(
            num_scalar_prefetch=2,
            grid=(1,),
            in_specs=in_specs,
            out_specs=out_specs,
            scratch_shapes=[pltpu.VMEM((rows // UNIT * (span // BS) + 1, UNIT, BS), jnp.bfloat16)],
        ),
        out_shape=out_shape,
        compiler_params=params(16),
        cost_estimate=cost(4 * rows * span, 8 * rows * span),
        name="pack",
    )(rep, pattern, *operands)


def fill(pieces, held_ref, sems, slots):
    half = slots // 2
    top, bottom = pl.ds(1, half), pl.ds(1 + half, half)
    every = pl.ds(0, SIDE)
    targets = [(pieces[n], held_ref.at[pl.ds(2 * n, 2), every, top]) for n in range(2)]
    swapped = (0, 2, 1, 3)
    for n, second in enumerate(swapped):
        for m, first in enumerate(swapped):
            targets.append((pieces[2 + n // 2].at[n % 2, m], held_ref.at[second, first, bottom]))
    copy_all(targets, sems)
    held_ref[:, :, 0] = jnp.zeros_like(held_ref[:, :, 0])
    wait_all(targets, sems)


def places_of(rep_ref, chunk):
    z, y = rep_ref[0] // SIDE, rep_ref[0] % SIDE
    place_z = [place_of(i, z) for i in range(SIDE)]
    place_y = [place_of(i, y) for i in range(SIDE)]
    both = [(place_z[s // SIDE], place_y[s % SIDE]) for s in range(SIDE * SIDE)]
    return [places[::-1] for places in both] if chunk == 0 else both


def unpack(places, held_ref, out_ref, parity, blocks):
    for u in range(0, UNITS, SIDE):
        values = {}
        for v in range(u, u + SIDE):
            second, first = places[parity * UNITS + v]
            for row, col, slot in blocks:
                values[row + v * UNIT, col] = held_ref[second, first, slot]
        for (row, col), value in values.items():
            out_ref[pl.ds(row, UNIT), pl.ds(col, BS)] = value


def begin(pieces, held_ref, count_ref, sems, slots):
    @pl.when(pl.program_id(0) == 0)
    def _():
        fill(pieces, held_ref, sems, slots)
        count_ref[0] = 1
        count_ref[1] = 1


def gathered_scratch(full):
    return [
        pltpu.VMEM((SIDE, SIDE, full + 1, UNIT, BS), jnp.bfloat16),
        pltpu.SMEM((2,), jnp.int32),
        pltpu.SemaphoreType.DMA((2 + SIDE * SIDE,)),
    ]


def cube_kernel(rep_ref, pat_ref, g_ref, *rest, chunk, first, slots):
    pieces, (own_ref, other_ref, held_ref, count_ref, sems, square_ref) = rest[:4], rest[4:]
    begin(pieces, held_ref, count_ref, sems, slots)
    places = places_of(rep_ref, chunk)
    blocks = pat_ref.shape[1] // CHUNKS
    free = [count_ref[0], count_ref[1]]
    for b in range(PAIR // BS):
        col = (first + pl.program_id(0)) * (PAIR // BS) + b
        inside = (col // blocks == chunk).astype(jnp.int32)
        for i in range(0, pat_ref.shape[0], SIDE):
            taken = [[], []]
            for a in range(i, i + SIDE):
                slot, free[a % 2] = take_slot(pat_ref[a, col] * inside, free[a % 2])
                taken[a % 2].append((a * BS, b * BS, slot))
            for parity in range(2):
                unpack(places, held_ref, square_ref, parity, taken[parity])
    count_ref[0], count_ref[1] = free
    put_parts(g_ref[...], square_ref[...], own_ref, other_ref)


def cube_part(rep, pattern, rows, pieces, chunk, width, slots):
    depth, height = rows.shape
    first, pairs, specs, shapes = part_outputs(depth, chunk, width)
    full = height // PAIR * (width // (CHUNKS * BS))
    return pl.pallas_call(
        functools.partial(cube_kernel, chunk=chunk, first=first, slots=slots),
        grid=(pairs,),
        in_specs=[SMEM_SPEC, SMEM_SPEC, whole(rows.shape)] + [ANY_SPEC] * 4,
        out_specs=specs,
        out_shape=shapes,
        scratch_shapes=gathered_scratch(full) + [pltpu.VMEM((height, PAIR), jnp.bfloat16)],
        compiler_params=params(32),
        cost_estimate=cost(2 * depth * height * PAIR * pairs, 2 * height * (PAIR * pairs + depth)),
        name="cube_part",
    )(rep, pattern, rows, *pieces)


def finish_kernel(rep_ref, pat_ref, *rest, chunk, slots):
    pieces, (out_ref, held_ref, count_ref, sems) = rest[:4], rest[-4:]
    begin(pieces, held_ref, count_ref, sems, slots)
    places = places_of(rep_ref, chunk)
    free = [count_ref[0], count_ref[1]]
    block_rows, block_cols = out_ref.shape[0] // BS, out_ref.shape[1] // BS
    for a in range(block_rows):
        taken = []
        for b in range(block_cols):
            kept = pat_ref[pl.program_id(0) * block_rows + a, chunk * block_cols + b]
            slot, free[a % 2] = take_slot(kept, free[a % 2])
            taken.append((a * BS, b * BS, slot))
        unpack(places, held_ref, out_ref, a % 2, taken)
    count_ref[0], count_ref[1] = free


def finish(rep, pattern, pieces, shape, chunk, slots, so_far=None, stripe=512):
    height, width = shape
    span = width // CHUNKS
    operands = [rep, pattern, *pieces] + ([] if so_far is None else [so_far])
    return pl.pallas_call(
        functools.partial(finish_kernel, chunk=chunk, slots=slots),
        grid=(height // stripe,),
        in_specs=[SMEM_SPEC, SMEM_SPEC] + [ANY_SPEC] * (len(operands) - 2),
        out_specs=pl.BlockSpec((stripe, span), lambda k: (k, chunk)),
        out_shape=jax.ShapeDtypeStruct(shape, jnp.bfloat16),
        scratch_shapes=gathered_scratch(height // PAIR * (span // BS)),
        input_output_aliases={} if so_far is None else {6: 0},
        compiler_params=params(24),
        cost_estimate=cost(height * span, 4 * height * span),
        name="finish",
    )(*operands)


def exchanged(piece, axis, ring, steps):
    for step in steps[:-1]:
        piece = jnp.concatenate([piece, lax.ppermute(piece, axis, ring(step))], axis=0)
    return piece, lax.ppermute(piece, axis, ring(steps[-1]))


def col_ring(step):
    return [(i, i ^ step) for i in range(SIDE)]


def z_ring(step):
    return [(z * SIDE + y, (z ^ step) * SIDE + y) for z in range(SIDE) for y in range(SIDE)]


def y_ring(step):
    return [(z * SIDE + y, z * SIDE + (y ^ step)) for z in range(SIDE) for y in range(SIDE)]


def gather_col(halves):
    pieces = []
    for part, steps in zip(halves, ((1, 3), (3, 1))):
        for piece in exchanged(part, "col", col_ring, steps):
            pieces.append(piece.reshape(2, *part.shape))
    return pieces


def gather_rep(halves, chunk):
    one, two = (z_ring, y_ring) if chunk == 0 else (y_ring, z_ring)
    ring = lambda step: one(step[1]) if step[0] == 0 else two(step[1])
    pieces = []
    for part, (a, b) in zip(halves, ((1, 3), (3, 1))):
        for piece in exchanged(part, "rep", ring, ((0, a), (0, b), (1, a), (1, b))):
            pieces.append(piece.reshape(2, SIDE, *part.shape))
    return pieces


def swap(part):
    return lax.ppermute(part, "row", [(0, 1), (1, 0)])


def newton_step(hamiltonian, pattern, pats, caps):
    height, width = hamiltonian.shape
    row_cap, chunk_cap = caps
    units = width // PAIR
    rep = lax.axis_index("rep").reshape(1)
    where = [lax.axis_index(axis).reshape(1) for axis in ("row", "col")] + [rep]

    picked = gather_col(pick(rep, pattern, hamiltonian, row_cap))
    rows = unpack_rows(where, pats, picked, height, units, row_cap)
    square, new = [], []
    for c in range(CHUNKS):
        own, other = square_part(pattern, rows, hamiltonian, c)
        square.append(gather_rep(pack(rep, pattern, own, swap(other), c, chunk_cap, width), c))
    for c in range(CHUNKS):
        own, other = cube_part(rep, pattern, rows, square[c], c, width, chunk_cap)
        packed = pack(rep, pattern, own, swap(other), c, chunk_cap, width, hamiltonian)
        new.append(gather_rep(packed, c))
    return rep, new


def shards(hamiltonian, pattern):
    shape = hamiltonian.shape
    row_full = shape[1] // PAIR * pattern.shape[0]
    chunk_full = pattern.shape[0] // 2 * (pattern.shape[1] // CHUNKS)

    pats = [pattern] + [lax.ppermute(pattern, "col", col_ring(a)) for a in PLACES[1:]]
    excess = over_caps(pats)
    excess = jnp.maximum(excess, swap(excess))[0, 0]

    rep, new = newton_step(hamiltonian, pattern, pats, (ROW_CAP, CHUNK_CAP))
    so_far = finish(rep, pattern, new[0], shape, 0, CHUNK_CAP)

    def fits(hamiltonian, pattern, pats, rep, pieces, so_far):
        return finish(rep, pattern, pieces, shape, 1, CHUNK_CAP, so_far)

    def any_pattern(hamiltonian, pattern, pats, rep, pieces, so_far):
        caps = (row_full, chunk_full)
        rep, new = newton_step(hamiltonian, pattern, pats, caps)
        out = finish(rep, pattern, new[0], shape, 0, caps[1])
        return finish(rep, pattern, new[1], shape, 1, caps[1], out)

    return lax.cond(
        excess > 0, any_pattern, fits, hamiltonian, pattern, pats, rep, new[1], so_far
    )


def solution(mesh):
    in_specs = (P("row", "col"), P("row", "col"))
    out_specs = P("row", "col")
    return jax.shard_map(shards, mesh=mesh, in_specs=in_specs, out_specs=out_specs, check_vma=False)
```

```python
import functools

import jax
import jax.numpy as jnp
from jax import lax
from jax.experimental import pallas as pl
from jax.experimental.pallas import tpu as pltpu
from jax.sharding import PartitionSpec as P

BS = 128
UNIT = 16
UNITS = BS // UNIT
SIDE = 4
CHUNKS = 2
ROW_CAP = 120
CHUNK_CAP = 64
MIB = 1024 * 1024
SMEM_SPEC = pl.BlockSpec(memory_space=pltpu.SMEM)
ANY_SPEC = pl.BlockSpec(memory_space=pl.ANY)
VMEM_SPEC = pl.BlockSpec(memory_space=pltpu.VMEM)
PIECES = 5
PAIR = 2 * BS
PLACES = (0, 1, 3, 2)


def params(mib):
    return pltpu.CompilerParams(vmem_limit_bytes=mib * MIB)


def cost(flops, moved):
    return pl.CostEstimate(flops=flops, bytes_accessed=moved, transcendentals=0)


def whole(shape):
    return pl.BlockSpec(shape, lambda *_: (0,) * len(shape))


def take_slot(kept, free):
    factor = jnp.full((UNIT, BS), kept.astype(jnp.float32), jnp.float32).astype(jnp.bfloat16)
    return kept * free, factor, free + kept


def pick_kernel(rep_ref, pat_ref, h_ref, out_ref, held_ref, count_ref):
    step = pl.program_id(0)

    @pl.when(step == 0)
    def _():
        held_ref[...] = jnp.zeros_like(held_ref)
        count_ref[0] = 0

    first = (rep_ref[0] % UNITS) * UNIT
    u = lax.broadcasted_iota(jnp.int32, (UNIT, BS), 0)
    c = lax.broadcasted_iota(jnp.int32, (UNIT, BS), 1)
    chosen = jnp.where(c == u + first, 1.0, 0.0).astype(jnp.bfloat16)
    block_col = 2 * step + rep_ref[0] // UNITS
    turned = lax.dot_general(
        chosen, h_ref[...], (((1,), (1,)), ((), ())), preferred_element_type=jnp.float32
    ).astype(jnp.bfloat16)
    count = count_ref[0]
    for a in range(h_ref.shape[0] // BS):
        kept = pat_ref[a, block_col]
        held_ref[count] = turned[:, a * BS : (a + 1) * BS]
        count = count + kept
    count_ref[0] = count

    @pl.when(step == pl.num_programs(0) - 1)
    def _():
        out_ref[...] = held_ref[: out_ref.shape[0]]


def pick(rep, pattern, tile, slots):
    height, width = tile.shape
    full = width // PAIR * (height // BS)
    return pl.pallas_call(
        pick_kernel,
        grid_spec=pltpu.PrefetchScalarGridSpec(
            num_scalar_prefetch=2,
            grid=(width // (2 * BS),),
            in_specs=[pl.BlockSpec((height, BS), lambda j, rep, pat: (0, 2 * j + rep[0] // UNITS))],
            out_specs=whole((slots, UNIT, BS)),
            scratch_shapes=[
                pltpu.VMEM((full + 1, UNIT, BS), jnp.bfloat16),
                pltpu.SMEM((1,), jnp.int32),
            ],
        ),
        out_shape=jax.ShapeDtypeStruct((slots, UNIT, BS), jnp.bfloat16),
        compiler_params=params(16),
        cost_estimate=cost(2 * UNIT * height * width, height * width),
        name="pick",
    )(rep, pattern, tile)


def excess_kernel(*refs):
    pats, out_ref = refs[:-1], refs[-1]
    row = lax.broadcasted_iota(jnp.int32, pats[0].shape, 0)
    col = lax.broadcasted_iota(jnp.int32, pats[0].shape, 1)
    span = pats[0].shape[1] // CHUNKS
    most = jnp.int32(-(2**30))
    for pat in pats:
        flags = pat[...]
        for p in range(2):
            most = jnp.maximum(most, jnp.sum(jnp.where(col % 2 == p, flags, 0)) - ROW_CAP)
            for c in range(CHUNKS):
                chosen = (row % 2 == p) & (col // span == c)
                most = jnp.maximum(most, jnp.sum(jnp.where(chosen, flags, 0)) - CHUNK_CAP)
    out_ref[...] = jnp.full(out_ref.shape, most, jnp.int32)


def over_caps(pats):
    return pl.pallas_call(
        excess_kernel,
        in_specs=[pl.BlockSpec(memory_space=pltpu.VMEM)] * len(pats),
        out_specs=pl.BlockSpec(memory_space=pltpu.VMEM),
        out_shape=jax.ShapeDtypeStruct((8, BS), jnp.int32),
        compiler_params=params(4),
        name="over_caps",
    )(*pats)


def rows_kernel(row_ref, col_ref, rep_ref, *rest):
    pats, pieces, out_ref = rest[:SIDE], rest[SIDE : 2 * SIDE], rest[2 * SIDE]
    row, col, rep = row_ref[0], col_ref[0], rep_ref[0]
    units = out_ref.shape[0] // (SIDE * UNIT)
    parity = rep // UNITS
    starts = [((col ^ away) + SIDE - row * (SIDE // 2)) % SIDE * units for away in PLACES]

    def unit(j, free):
        free = list(free)
        for n, start in enumerate(starts):
            line = pl.ds(pl.multiple_of((start + j) * UNIT, UNIT), UNIT)
            values = []
            for a in range(out_ref.shape[1] // BS):
                slot, factor, free[n] = take_slot(pats[n][a, 2 * j + parity], free[n])
                values.append(pieces[n][slot] * factor)
            for a, value in enumerate(values):
                out_ref[line, pl.ds(a * BS, BS)] = value
        return tuple(free)

    lax.fori_loop(0, units, unit, (jnp.int32(0),) * SIDE)


def unpack_rows(where, pats, pieces, height, units):
    return pl.pallas_call(
        rows_kernel,
        in_specs=[SMEM_SPEC] * (3 + SIDE) + [VMEM_SPEC] * SIDE,
        out_specs=VMEM_SPEC,
        out_shape=jax.ShapeDtypeStruct((SIDE * units * UNIT, height), jnp.bfloat16),
        compiler_params=params(8),
        name="unpack_rows",
    )(*where, *pats, *pieces)


def put_parts(rows, right, own_ref, other_ref, cols):
    half = own_ref.shape[0]
    acc = jnp.dot(rows, right, preferred_element_type=jnp.float32)
    own_ref[:, cols] = acc[:half]
    other_ref[:, cols] = acc[half:].astype(jnp.bfloat16)


def pairs_of(chunk, width):
    first, last = chunk * width // (2 * PAIR), -(-(chunk + 1) * width // (2 * PAIR))
    return first, last - first


def part_shapes(depth, pairs):
    shape = (depth // 2, pairs * PAIR)
    return [jax.ShapeDtypeStruct(shape, jnp.float32), jax.ShapeDtypeStruct(shape, jnp.bfloat16)]


def square_kernel(pat_ref, g_ref, h_ref, own_ref, other_ref, read_ref, x_ref, sems, *, first, pairs):
    def read(t):
        cols = pl.ds((first + t) * PAIR, PAIR)
        return pltpu.make_async_copy(h_ref.at[:, cols], read_ref.at[t % 2], sems.at[t % 2])

    read(0).start()
    for t in range(pairs):
        if t + 1 < pairs:
            read(t + 1).start()
        read(t).wait()
        for a in range(x_ref.shape[0] // BS):
            for b in range(PAIR // BS):
                kept = pat_ref[a, (first + t) * (PAIR // BS) + b].astype(jnp.float32)
                factor = jnp.full((BS, BS), kept, jnp.float32).astype(jnp.bfloat16)
                rows, cols = pl.ds(a * BS, BS), pl.ds(b * BS, BS)
                x_ref[rows, cols] = read_ref[t % 2, rows, cols] * factor
        put_parts(g_ref[...], x_ref[...], own_ref, other_ref, pl.ds(t * PAIR, PAIR))


def square_part(pattern, rows, tile, chunk):
    depth, height = rows.shape
    first, pairs = pairs_of(chunk, tile.shape[1])
    return pl.pallas_call(
        functools.partial(square_kernel, first=first, pairs=pairs),
        in_specs=[SMEM_SPEC, VMEM_SPEC, ANY_SPEC],
        out_specs=[VMEM_SPEC, VMEM_SPEC],
        out_shape=part_shapes(depth, pairs),
        scratch_shapes=[
            pltpu.VMEM((2, height, PAIR), jnp.bfloat16),
            pltpu.VMEM((height, PAIR), jnp.bfloat16),
            pltpu.SemaphoreType.DMA((2,)),
        ],
        compiler_params=params(16),
        cost_estimate=cost(2 * depth * height * PAIR * pairs, 2 * height * (PAIR * pairs + depth)),
        name="square_part",
    )(pattern, rows, tile)


def pack_kernel(rep_ref, pat_ref, own_ref, other_ref, *rest, chunk, offset, last):
    tile_ref, out_ref, held_ref = rest if last else (None, *rest)
    units, blocks = own_ref.shape[0] // UNIT, pat_ref.shape[1] // CHUNKS
    parity = rep_ref[0] // UNITS
    held_ref[...] = jnp.zeros_like(held_ref)
    count = jnp.int32(0)
    order = [(j, b) for b in range(blocks) for j in range(units)]
    for j, b in sorted(order) if last else order:
        kept = pat_ref[2 * j + parity, chunk * blocks + b]
        part, cols = pl.ds(j * UNIT, UNIT), pl.ds(offset + b * BS, BS)
        value = own_ref[part, cols] + other_ref[part, cols].astype(jnp.float32)
        if last:
            value = 1.5 * tile_ref[j, 0, :, pl.ds(b * BS, BS)].astype(jnp.float32) - 0.5 * value
        held_ref[count] = value.astype(jnp.bfloat16)
        count = count + kept
    out_ref[...] = held_ref[: out_ref.shape[0]]


def pack(rep, pattern, own, other, chunk, slots, width, tile=None):
    rows = own.shape[0]
    in_specs = [whole(own.shape), whole(other.shape)]
    operands = [own, other]
    span = width // CHUNKS
    if tile is not None:
        reps = tile.shape[0] // rows
        operands.append(tile.reshape(rows // UNIT, reps, UNIT, width))
        in_specs.append(
            pl.BlockSpec((rows // UNIT, 1, UNIT, span), lambda i, rep, pat: (0, rep[0], 0, chunk))
        )
    return pl.pallas_call(
        functools.partial(
            pack_kernel, chunk=chunk, offset=chunk * span % PAIR, last=tile is not None
        ),
        grid_spec=pltpu.PrefetchScalarGridSpec(
            num_scalar_prefetch=2,
            grid=(1,),
            in_specs=in_specs,
            out_specs=whole((slots, UNIT, BS)),
            scratch_shapes=[pltpu.VMEM((rows // UNIT * (span // BS) + 1, UNIT, BS), jnp.bfloat16)],
        ),
        out_shape=jax.ShapeDtypeStruct((slots, UNIT, BS), jnp.bfloat16),
        compiler_params=params(16),
        cost_estimate=cost(4 * rows * span, 8 * rows * span),
        name="pack",
    )(rep, pattern, *operands)


class Gathered:
    def __init__(self, rep, refs, chunk):
        self.refs, self.chunk = refs, chunk
        self.z, self.y = rep // SIDE, rep % SIDE

    def unit(self, q, p, slot):
        if q < SIDE - 1:
            return self.refs[q][p, slot]
        return self.refs[q + p // 2][p % 2, slot]

    def device(self, q, p):
        z, y = (p, q) if self.chunk == 0 else (q, p)
        return (self.z ^ PLACES[z]) * SIDE + (self.y ^ PLACES[y])

    def turned(self, q, p):
        return (p if self.chunk == 0 else q) // 2

    def parity(self, turned):
        return self.z // 2 ^ turned


def cube_kernel(rep_ref, pat_ref, g_ref, *rest, chunk, first, pairs):
    refs, (own_ref, other_ref, square_ref) = rest[:PIECES], rest[PIECES:]
    gathered = Gathered(rep_ref[0], refs, chunk)
    places = [(q, p) for q in range(SIDE) for p in range(SIDE)]
    lines = {place: gathered.device(*place) * UNIT for place in places}
    blocks = pat_ref.shape[1] // CHUNKS
    stride = UNIT * SIDE * SIDE

    def pair(t, free):
        free = list(free)
        for b in range(PAIR // BS):
            col = (first + t) * (PAIR // BS) + b
            inside = (col // blocks == chunk).astype(jnp.int32)
            for j in range(square_ref.shape[0] // stride):
                values = {}
                for turned in range(2):
                    kept = pat_ref[2 * j + gathered.parity(turned), col] * inside
                    slot, factor, free[turned] = take_slot(kept, free[turned])
                    for place in places:
                        if gathered.turned(*place) == turned:
                            values[place] = gathered.unit(*place, slot) * factor
                for place, value in values.items():
                    line = pl.ds(pl.multiple_of(j * stride + lines[place], UNIT), UNIT)
                    square_ref[line, pl.ds(b * BS, BS)] = value
        cols = pl.ds(pl.multiple_of(t * PAIR, PAIR), PAIR)
        put_parts(g_ref[...], square_ref[...], own_ref, other_ref, cols)
        return tuple(free)

    lax.fori_loop(0, pairs, pair, (jnp.int32(0), jnp.int32(0)))


def cube_part(rep, pattern, rows, pieces, chunk, width):
    depth, height = rows.shape
    first, pairs = pairs_of(chunk, width)
    return pl.pallas_call(
        functools.partial(cube_kernel, chunk=chunk, first=first, pairs=pairs),
        in_specs=[SMEM_SPEC, SMEM_SPEC, VMEM_SPEC] + [VMEM_SPEC] * PIECES,
        out_specs=[VMEM_SPEC, VMEM_SPEC],
        out_shape=part_shapes(depth, pairs),
        scratch_shapes=[pltpu.VMEM((height, PAIR), jnp.bfloat16)],
        compiler_params=params(8),
        cost_estimate=cost(2 * depth * height * PAIR * pairs, 2 * height * (PAIR * pairs + depth)),
        name="cube_part",
    )(rep, pattern, rows, *pieces)


def finish_kernel(rep_ref, pat_ref, *rest, chunk, far, count):
    refs, (out_ref, held_ref, sems) = rest[:count], rest[-3:]
    refs = [None] * (SIDE - 1) + list(refs) if far else refs
    gathered = Gathered(rep_ref[0], refs, chunk)
    seconds = [SIDE - 1] if far else range(SIDE - 1)
    units, blocks = held_ref.shape[1], held_ref.shape[3] // BS
    copies = []
    for turned in range(2):
        places = [(q, p) for q in seconds for p in range(SIDE) if gathered.turned(q, p) == turned]
        if not places:
            continue
        base = len(copies)

        def line(j, free, turned=turned, places=places, base=base):
            values = {}
            for b in range(blocks):
                kept = pat_ref[2 * j + gathered.parity(turned), chunk * blocks + b]
                slot, factor, free = take_slot(kept, free)
                for n, place in enumerate(places):
                    values[n, b] = gathered.unit(*place, slot) * factor
            for (n, b), value in values.items():
                held_ref[base + n, j, :, pl.ds(b * BS, BS)] = value
            return free

        lax.fori_loop(0, units, line, jnp.int32(0))
        cols = pl.ds(chunk * blocks * BS, blocks * BS)
        for n, place in enumerate(places):
            target = out_ref.at[:, gathered.device(*place), :, cols]
            copies.append(pltpu.make_async_copy(held_ref.at[base + n], target, sems.at[base + n]))
            copies[-1].start()
    for copy in copies:
        copy.wait()


def finish(rep, pattern, pieces, shape, chunk, far, so_far=None):
    units, reps, _, width = shape
    sources = (1 if far else SIDE - 1) * SIDE
    span = width // CHUNKS
    pieces = pieces[SIDE - 1 :] if far else pieces[: SIDE - 1]
    operands = [rep, pattern, *pieces] + ([] if so_far is None else [so_far])
    return pl.pallas_call(
        functools.partial(finish_kernel, chunk=chunk, far=far, count=len(pieces)),
        in_specs=[SMEM_SPEC, SMEM_SPEC]
        + [VMEM_SPEC] * len(pieces)
        + ([] if so_far is None else [ANY_SPEC]),
        out_specs=ANY_SPEC,
        out_shape=jax.ShapeDtypeStruct(shape, jnp.bfloat16),
        scratch_shapes=[
            pltpu.VMEM((sources, units, UNIT, span), jnp.bfloat16),
            pltpu.SemaphoreType.DMA((sources,)),
        ],
        input_output_aliases={} if so_far is None else {2 + len(pieces): 0},
        compiler_params=params(16),
        cost_estimate=cost(sources * units * UNIT * span, 4 * sources * units * UNIT * span),
        name="finish_far" if far else "finish_near",
    )(*operands)


def ring(piece, axis, pairs):
    one = lax.ppermute(piece, axis, pairs(1))
    three = lax.ppermute(piece, axis, pairs(3))
    cut = piece.shape[0] // 2
    top = lax.ppermute(three[:cut], axis, pairs(1))
    bottom = lax.ppermute(one[cut:], axis, pairs(3))
    return one, three, top, bottom


def col_ring(step):
    return [(i, i ^ step) for i in range(SIDE)]


def z_ring(step):
    return [(z * SIDE + y, (z ^ step) * SIDE + y) for z in range(SIDE) for y in range(SIDE)]


def y_ring(step):
    return [(z * SIDE + y, z * SIDE + (y ^ step)) for z in range(SIDE) for y in range(SIDE)]


def gather_col(packed):
    one, three, top, bottom = ring(packed, "col", col_ring)
    return [packed, one, three, jnp.concatenate([top, bottom], axis=0)]


def gather_rep(packed, chunk):
    first, second = (z_ring, y_ring) if chunk == 0 else (y_ring, z_ring)
    one, three, top, bottom = ring(packed, "rep", first)
    payload = jnp.stack([packed, one, three, jnp.concatenate([top, bottom], axis=0)])
    return [payload, *ring(payload, "rep", second)]


def swap(part):
    return lax.ppermute(part, "row", [(0, 1), (1, 0)])


def newton_step(hamiltonian, pattern, pats, caps):
    height, width = hamiltonian.shape
    row_cap, chunk_cap = caps
    units = width // PAIR
    rep = lax.axis_index("rep").reshape(1)
    where = [lax.axis_index(axis).reshape(1) for axis in ("row", "col")] + [rep]

    picked = gather_col(pick(rep, pattern, hamiltonian, row_cap))
    rows = unpack_rows(where, pats, picked, height, units)
    square, new = [], []
    for c in range(CHUNKS):
        own, other = square_part(pattern, rows, hamiltonian, c)
        square.append(gather_rep(pack(rep, pattern, own, swap(other), c, chunk_cap, width), c))
    for c in range(CHUNKS):
        own, other = cube_part(rep, pattern, rows, square[c], c, width)
        packed = pack(rep, pattern, own, swap(other), c, chunk_cap, width, hamiltonian)
        new.append(gather_rep(packed, c))
    return rep, new


def shards(hamiltonian, pattern):
    shape = hamiltonian.shape
    row_full = shape[1] // PAIR * pattern.shape[0]
    chunk_full = pattern.shape[0] // 2 * (pattern.shape[1] // CHUNKS)

    pats = [pattern] + [lax.ppermute(pattern, "col", col_ring(a)) for a in PLACES[1:]]
    excess = over_caps(pats)
    excess = jnp.maximum(excess, swap(excess))[0, 0]

    units = shape[0] // (lax.axis_size("rep") * UNIT)
    split = (units, lax.axis_size("rep"), UNIT, shape[1])

    rep, new = newton_step(hamiltonian, pattern, pats, (ROW_CAP, CHUNK_CAP))
    so_far = finish(rep, pattern, new[0], split, 0, False)
    so_far = finish(rep, pattern, new[1], split, 1, False, so_far)
    so_far = finish(rep, pattern, new[0], split, 0, True, so_far)

    def fits(hamiltonian, pattern, pats, rep, pieces, so_far):
        return finish(rep, pattern, pieces, split, 1, True, so_far).reshape(shape)

    def any_pattern(hamiltonian, pattern, pats, rep, pieces, so_far):
        rep, new = newton_step(hamiltonian, pattern, pats, (row_full, chunk_full))
        out = None
        for c in range(CHUNKS):
            for far in (False, True):
                out = finish(rep, pattern, new[c], split, c, far, out)
        return out.reshape(shape)

    return lax.cond(
        excess > 0, any_pattern, fits, hamiltonian, pattern, pats, rep, new[1], so_far
    )


def solution(mesh):
    in_specs = (P("row", "col"), P("row", "col"))
    out_specs = P("row", "col")
    return jax.shard_map(shards, mesh=mesh, in_specs=in_specs, out_specs=out_specs, check_vma=False)
```

```python
import functools

import jax
import jax.numpy as jnp
from jax import lax
from jax.experimental import pallas as pl
from jax.experimental.pallas import tpu as pltpu
from jax.sharding import PartitionSpec as P

BS = 128
UNIT = 16
UNITS = BS // UNIT
SIDE = 4
CHUNKS = 2
ROW_CAP = 120
CHUNK_CAP = 64
MIB = 1024 * 1024
SMEM_SPEC = pl.BlockSpec(memory_space=pltpu.SMEM)
ANY_SPEC = pl.BlockSpec(memory_space=pl.ANY)
VMEM_SPEC = pl.BlockSpec(memory_space=pltpu.VMEM)
PIECES = 5
PAIR = 2 * BS
PLACES = (0, 1, 3, 2)


def params(mib):
    return pltpu.CompilerParams(vmem_limit_bytes=mib * MIB)


def cost(flops, moved):
    return pl.CostEstimate(flops=flops, bytes_accessed=moved, transcendentals=0)


def whole(shape):
    return pl.BlockSpec(shape, lambda *_: (0,) * len(shape))


def take_slot(kept, free):
    factor = jnp.full((UNIT, BS), kept.astype(jnp.float32), jnp.float32).astype(jnp.bfloat16)
    return kept * free, factor, free + kept


def pick_kernel(rep_ref, pat_ref, h_ref, out_ref, held_ref, count_ref):
    step = pl.program_id(0)

    @pl.when(step == 0)
    def _():
        held_ref[...] = jnp.zeros_like(held_ref)
        count_ref[0] = 0

    first = (rep_ref[0] % UNITS) * UNIT
    u = lax.broadcasted_iota(jnp.int32, (UNIT, BS), 0)
    c = lax.broadcasted_iota(jnp.int32, (UNIT, BS), 1)
    chosen = jnp.where(c == u + first, 1.0, 0.0).astype(jnp.bfloat16)
    block_col = 2 * step + rep_ref[0] // UNITS
    turned = lax.dot_general(
        chosen, h_ref[...], (((1,), (1,)), ((), ())), preferred_element_type=jnp.float32
    ).astype(jnp.bfloat16)
    count = count_ref[0]
    for a in range(h_ref.shape[0] // BS):
        kept = pat_ref[a, block_col]
        held_ref[count] = turned[:, a * BS : (a + 1) * BS]
        count = count + kept
    count_ref[0] = count

    @pl.when(step == pl.num_programs(0) - 1)
    def _():
        out_ref[...] = held_ref[: out_ref.shape[0]]


def pick(rep, pattern, tile, slots):
    height, width = tile.shape
    full = width // PAIR * (height // BS)
    return pl.pallas_call(
        pick_kernel,
        grid_spec=pltpu.PrefetchScalarGridSpec(
            num_scalar_prefetch=2,
            grid=(width // (2 * BS),),
            in_specs=[pl.BlockSpec((height, BS), lambda j, rep, pat: (0, 2 * j + rep[0] // UNITS))],
            out_specs=whole((slots, UNIT, BS)),
            scratch_shapes=[
                pltpu.VMEM((full + 1, UNIT, BS), jnp.bfloat16),
                pltpu.SMEM((1,), jnp.int32),
            ],
        ),
        out_shape=jax.ShapeDtypeStruct((slots, UNIT, BS), jnp.bfloat16),
        compiler_params=params(16),
        cost_estimate=cost(2 * UNIT * height * width, height * width),
        name="pick",
    )(rep, pattern, tile)


def excess_kernel(*refs):
    pats, out_ref = refs[:-1], refs[-1]
    row = lax.broadcasted_iota(jnp.int32, pats[0].shape, 0)
    col = lax.broadcasted_iota(jnp.int32, pats[0].shape, 1)
    span = pats[0].shape[1] // CHUNKS
    most = jnp.int32(-(2**30))
    for pat in pats:
        flags = pat[...]
        for p in range(2):
            most = jnp.maximum(most, jnp.sum(jnp.where(col % 2 == p, flags, 0)) - ROW_CAP)
            for c in range(CHUNKS):
                chosen = (row % 2 == p) & (col // span == c)
                most = jnp.maximum(most, jnp.sum(jnp.where(chosen, flags, 0)) - CHUNK_CAP)
    out_ref[...] = jnp.full(out_ref.shape, most, jnp.int32)


def over_caps(pats):
    return pl.pallas_call(
        excess_kernel,
        in_specs=[pl.BlockSpec(memory_space=pltpu.VMEM)] * len(pats),
        out_specs=pl.BlockSpec(memory_space=pltpu.VMEM),
        out_shape=jax.ShapeDtypeStruct((8, BS), jnp.int32),
        compiler_params=params(4),
        name="over_caps",
    )(*pats)


def rows_kernel(row_ref, col_ref, rep_ref, *rest):
    pats, pieces, out_ref = rest[:SIDE], rest[SIDE : 2 * SIDE], rest[2 * SIDE]
    row, col, rep = row_ref[0], col_ref[0], rep_ref[0]
    units = out_ref.shape[0] // (SIDE * UNIT)
    parity = rep // UNITS
    starts = [((col ^ away) + SIDE - row * (SIDE // 2)) % SIDE * units for away in PLACES]

    def unit(j, free):
        free = list(free)
        for n, start in enumerate(starts):
            line = pl.ds(pl.multiple_of((start + j) * UNIT, UNIT), UNIT)
            values = []
            for a in range(out_ref.shape[1] // BS):
                slot, factor, free[n] = take_slot(pats[n][a, 2 * j + parity], free[n])
                values.append(pieces[n][slot] * factor)
            for a, value in enumerate(values):
                out_ref[line, pl.ds(a * BS, BS)] = value
        return tuple(free)

    lax.fori_loop(0, units, unit, (jnp.int32(0),) * SIDE)


def unpack_rows(where, pats, pieces, height, units):
    return pl.pallas_call(
        rows_kernel,
        in_specs=[SMEM_SPEC] * (3 + SIDE) + [VMEM_SPEC] * SIDE,
        out_specs=VMEM_SPEC,
        out_shape=jax.ShapeDtypeStruct((SIDE * units * UNIT, height), jnp.bfloat16),
        compiler_params=params(8),
        name="unpack_rows",
    )(*where, *pats, *pieces)


def put_parts(rows, right, own_ref, other_ref, cols):
    half = own_ref.shape[0]
    acc = jnp.dot(rows, right, preferred_element_type=jnp.float32)
    own_ref[:, cols] = acc[:half]
    other_ref[:, cols] = acc[half:].astype(jnp.bfloat16)


def pairs_of(chunk, width):
    first, last = chunk * width // (2 * PAIR), -(-(chunk + 1) * width // (2 * PAIR))
    return first, last - first


def part_shapes(depth, pairs):
    shape = (depth // 2, pairs * PAIR)
    return [jax.ShapeDtypeStruct(shape, jnp.float32), jax.ShapeDtypeStruct(shape, jnp.bfloat16)]


def in_turn(pairs, prepare, buffers, rows, own_ref, other_ref):
    prepare(0, buffers[0])
    for t in range(pairs):
        if t + 1 < pairs:
            prepare(t + 1, buffers[(t + 1) % 2])
        put_parts(rows, buffers[t % 2][...], own_ref, other_ref, pl.ds(t * PAIR, PAIR))


def square_kernel(pat_ref, g_ref, h_ref, own_ref, other_ref, *buffers, first, pairs):
    def prepare(t, x_ref):
        for a in range(x_ref.shape[0] // BS):
            for b in range(PAIR // BS):
                col = (first + t) * (PAIR // BS) + b
                kept = pat_ref[a, col].astype(jnp.float32)
                factor = jnp.full((BS, BS), kept, jnp.float32).astype(jnp.bfloat16)
                rows = pl.ds(a * BS, BS)
                x_ref[rows, pl.ds(b * BS, BS)] = h_ref[rows, pl.ds(col * BS, BS)] * factor

    in_turn(pairs, prepare, buffers, g_ref[...], own_ref, other_ref)


def square_part(pattern, rows, tile, chunk):
    depth, height = rows.shape
    first, pairs = pairs_of(chunk, tile.shape[1])
    return pl.pallas_call(
        functools.partial(square_kernel, first=first, pairs=pairs),
        in_specs=[SMEM_SPEC, VMEM_SPEC, VMEM_SPEC],
        out_specs=[VMEM_SPEC, VMEM_SPEC],
        out_shape=part_shapes(depth, pairs),
        scratch_shapes=[pltpu.VMEM((height, PAIR), jnp.bfloat16)] * 2,
        compiler_params=params(16),
        cost_estimate=cost(2 * depth * height * PAIR * pairs, 2 * height * (PAIR * pairs + depth)),
        name="square_part",
    )(pattern, rows, tile)


def pack_kernel(rep_ref, pat_ref, own_ref, other_ref, *rest, chunk, offset, last):
    tile_ref, out_ref, held_ref = rest if last else (None, *rest)
    units, blocks = own_ref.shape[0] // UNIT, pat_ref.shape[1] // CHUNKS
    parity = rep_ref[0] // UNITS
    held_ref[...] = jnp.zeros_like(held_ref)
    count = jnp.int32(0)
    order = [(j, b) for b in range(blocks) for j in range(units)]
    for j, b in sorted(order) if last else order:
        kept = pat_ref[2 * j + parity, chunk * blocks + b]
        part, cols = pl.ds(j * UNIT, UNIT), pl.ds(offset + b * BS, BS)
        value = own_ref[part, cols] + other_ref[part, cols].astype(jnp.float32)
        if last:
            value = 1.5 * tile_ref[j, 0, :, pl.ds(b * BS, BS)].astype(jnp.float32) - 0.5 * value
        held_ref[count] = value.astype(jnp.bfloat16)
        count = count + kept
    out_ref[...] = held_ref[: out_ref.shape[0]]


def pack(rep, pattern, own, other, chunk, slots, width, tile=None):
    rows = own.shape[0]
    in_specs = [whole(own.shape), whole(other.shape)]
    operands = [own, other]
    span = width // CHUNKS
    if tile is not None:
        reps = tile.shape[0] // rows
        operands.append(tile.reshape(rows // UNIT, reps, UNIT, width))
        in_specs.append(
            pl.BlockSpec((rows // UNIT, 1, UNIT, span), lambda i, rep, pat: (0, rep[0], 0, chunk))
        )
    return pl.pallas_call(
        functools.partial(
            pack_kernel, chunk=chunk, offset=chunk * span % PAIR, last=tile is not None
        ),
        grid_spec=pltpu.PrefetchScalarGridSpec(
            num_scalar_prefetch=2,
            grid=(1,),
            in_specs=in_specs,
            out_specs=whole((slots, UNIT, BS)),
            scratch_shapes=[pltpu.VMEM((rows // UNIT * (span // BS) + 1, UNIT, BS), jnp.bfloat16)],
        ),
        out_shape=jax.ShapeDtypeStruct((slots, UNIT, BS), jnp.bfloat16),
        compiler_params=params(16),
        cost_estimate=cost(4 * rows * span, 8 * rows * span),
        name="pack",
    )(rep, pattern, *operands)


class Gathered:
    def __init__(self, rep, refs, chunk):
        self.refs, self.chunk = refs, chunk
        self.z, self.y = rep // SIDE, rep % SIDE

    def unit(self, q, p, slot):
        if q < SIDE - 1:
            return self.refs[q][p, slot]
        return self.refs[q + p // 2][p % 2, slot]

    def device(self, q, p):
        z, y = (p, q) if self.chunk == 0 else (q, p)
        return (self.z ^ PLACES[z]) * SIDE + (self.y ^ PLACES[y])

    def turned(self, q, p):
        return (p if self.chunk == 0 else q) // 2

    def parity(self, turned):
        return self.z // 2 ^ turned


def cube_kernel(rep_ref, pat_ref, g_ref, *rest, chunk, first, pairs):
    refs, (own_ref, other_ref, square_ref) = rest[:PIECES], rest[PIECES:]
    gathered = Gathered(rep_ref[0], refs, chunk)
    places = [(q, p) for q in range(SIDE) for p in range(SIDE)]
    lines = {place: gathered.device(*place) * UNIT for place in places}
    blocks = pat_ref.shape[1] // CHUNKS
    stride = UNIT * SIDE * SIDE

    def pair(t, free):
        free = list(free)
        for b in range(PAIR // BS):
            col = (first + t) * (PAIR // BS) + b
            inside = (col // blocks == chunk).astype(jnp.int32)
            for j in range(square_ref.shape[0] // stride):
                values = {}
                for turned in range(2):
                    kept = pat_ref[2 * j + gathered.parity(turned), col] * inside
                    slot, factor, free[turned] = take_slot(kept, free[turned])
                    for place in places:
                        if gathered.turned(*place) == turned:
                            values[place] = gathered.unit(*place, slot) * factor
                for place, value in values.items():
                    line = pl.ds(pl.multiple_of(j * stride + lines[place], UNIT), UNIT)
                    square_ref[line, pl.ds(b * BS, BS)] = value
        cols = pl.ds(pl.multiple_of(t * PAIR, PAIR), PAIR)
        put_parts(g_ref[...], square_ref[...], own_ref, other_ref, cols)
        return tuple(free)

    lax.fori_loop(0, pairs, pair, (jnp.int32(0), jnp.int32(0)))


def cube_part(rep, pattern, rows, pieces, chunk, width):
    depth, height = rows.shape
    first, pairs = pairs_of(chunk, width)
    return pl.pallas_call(
        functools.partial(cube_kernel, chunk=chunk, first=first, pairs=pairs),
        in_specs=[SMEM_SPEC, SMEM_SPEC, VMEM_SPEC] + [VMEM_SPEC] * PIECES,
        out_specs=[VMEM_SPEC, VMEM_SPEC],
        out_shape=part_shapes(depth, pairs),
        scratch_shapes=[pltpu.VMEM((height, PAIR), jnp.bfloat16)],
        compiler_params=params(8),
        cost_estimate=cost(2 * depth * height * PAIR * pairs, 2 * height * (PAIR * pairs + depth)),
        name="cube_part",
    )(rep, pattern, rows, *pieces)


def finish_kernel(rep_ref, pat_ref, *rest, chunk, far, count):
    refs, (out_ref, held_ref, sems) = rest[:count], rest[-3:]
    refs = [None] * (SIDE - 1) + list(refs) if far else refs
    gathered = Gathered(rep_ref[0], refs, chunk)
    seconds = [SIDE - 1] if far else range(SIDE - 1)
    units, blocks = held_ref.shape[1], held_ref.shape[3] // BS
    copies = []
    for turned in range(2):
        places = [(q, p) for q in seconds for p in range(SIDE) if gathered.turned(q, p) == turned]
        if not places:
            continue
        base = len(copies)

        def line(j, free, turned=turned, places=places, base=base):
            values = {}
            for b in range(blocks):
                kept = pat_ref[2 * j + gathered.parity(turned), chunk * blocks + b]
                slot, factor, free = take_slot(kept, free)
                for n, place in enumerate(places):
                    values[n, b] = gathered.unit(*place, slot) * factor
            for (n, b), value in values.items():
                held_ref[base + n, j, :, pl.ds(b * BS, BS)] = value
            return free

        lax.fori_loop(0, units, line, jnp.int32(0))
        cols = pl.ds(chunk * blocks * BS, blocks * BS)
        for n, place in enumerate(places):
            target = out_ref.at[:, gathered.device(*place), :, cols]
            copies.append(pltpu.make_async_copy(held_ref.at[base + n], target, sems.at[base + n]))
            copies[-1].start()
    for copy in copies:
        copy.wait()


def finish(rep, pattern, pieces, shape, chunk, far, so_far=None):
    units, reps, _, width = shape
    sources = (1 if far else SIDE - 1) * SIDE
    span = width // CHUNKS
    pieces = pieces[SIDE - 1 :] if far else pieces[: SIDE - 1]
    operands = [rep, pattern, *pieces] + ([] if so_far is None else [so_far])
    return pl.pallas_call(
        functools.partial(finish_kernel, chunk=chunk, far=far, count=len(pieces)),
        in_specs=[SMEM_SPEC, SMEM_SPEC]
        + [VMEM_SPEC] * len(pieces)
        + ([] if so_far is None else [ANY_SPEC]),
        out_specs=ANY_SPEC,
        out_shape=jax.ShapeDtypeStruct(shape, jnp.bfloat16),
        scratch_shapes=[
            pltpu.VMEM((sources, units, UNIT, span), jnp.bfloat16),
            pltpu.SemaphoreType.DMA((sources,)),
        ],
        input_output_aliases={} if so_far is None else {2 + len(pieces): 0},
        compiler_params=params(16),
        cost_estimate=cost(sources * units * UNIT * span, 4 * sources * units * UNIT * span),
        name="finish_far" if far else "finish_near",
    )(*operands)


def ring(piece, axis, pairs):
    one = lax.ppermute(piece, axis, pairs(1))
    three = lax.ppermute(piece, axis, pairs(3))
    cut = piece.shape[0] // 2
    top = lax.ppermute(three[:cut], axis, pairs(1))
    bottom = lax.ppermute(one[cut:], axis, pairs(3))
    return one, three, top, bottom


def col_ring(step):
    return [(i, i ^ step) for i in range(SIDE)]


def z_ring(step):
    return [(z * SIDE + y, (z ^ step) * SIDE + y) for z in range(SIDE) for y in range(SIDE)]


def y_ring(step):
    return [(z * SIDE + y, z * SIDE + (y ^ step)) for z in range(SIDE) for y in range(SIDE)]


def gather_col(packed):
    cut = packed.shape[0] // 2
    top, bottom = packed[:cut], packed[cut:]
    three_top = lax.ppermute(top, "col", col_ring(3))
    one_bottom = lax.ppermute(bottom, "col", col_ring(1))
    one = lax.ppermute(top, "col", col_ring(1)), one_bottom
    three = three_top, lax.ppermute(bottom, "col", col_ring(3))
    far = lax.ppermute(three_top, "col", col_ring(1)), lax.ppermute(one_bottom, "col", col_ring(3))
    return [packed] + [jnp.concatenate(halves, axis=0) for halves in (one, three, far)]


def gather_rep(packed, chunk):
    first, second = (z_ring, y_ring) if chunk == 0 else (y_ring, z_ring)
    one, three, top, bottom = ring(packed, "rep", first)
    payload = jnp.stack([packed, one, three, jnp.concatenate([top, bottom], axis=0)])
    return [payload, *ring(payload, "rep", second)]


def swap(part):
    return lax.ppermute(part, "row", [(0, 1), (1, 0)])


def newton_step(hamiltonian, pattern, caps):
    height, width = hamiltonian.shape
    row_cap, chunk_cap = caps
    units = width // PAIR
    rep = lax.axis_index("rep").reshape(1)
    where = [lax.axis_index(axis).reshape(1) for axis in ("row", "col")] + [rep]

    picked = gather_col(pick(rep, pattern, hamiltonian, row_cap))
    picked[1], picked[2], sent = lax.optimization_barrier((picked[1], picked[2], pattern))
    pats = [pattern] + [lax.ppermute(sent, "col", col_ring(a)) for a in PLACES[1:]]
    rows = unpack_rows(where, pats, picked, height, units)
    square, new = [], []
    for c in range(CHUNKS):
        own, other = square_part(pattern, rows, hamiltonian, c)
        square.append(gather_rep(pack(rep, pattern, own, swap(other), c, chunk_cap, width), c))
    for c in range(CHUNKS):
        own, other = cube_part(rep, pattern, rows, square[c], c, width)
        packed = pack(rep, pattern, own, swap(other), c, chunk_cap, width, hamiltonian)
        new.append(gather_rep(packed, c))
    return rep, pats, new


def shards(hamiltonian, pattern):
    shape = hamiltonian.shape
    row_full = shape[1] // PAIR * pattern.shape[0]
    chunk_full = pattern.shape[0] // 2 * (pattern.shape[1] // CHUNKS)

    units = shape[0] // (lax.axis_size("rep") * UNIT)
    split = (units, lax.axis_size("rep"), UNIT, shape[1])

    rep, pats, new = newton_step(hamiltonian, pattern, (ROW_CAP, CHUNK_CAP))
    excess = over_caps(pats)
    excess = jnp.maximum(excess, swap(excess))[0, 0]
    so_far = finish(rep, pattern, new[0], split, 0, False)
    so_far = finish(rep, pattern, new[1], split, 1, False, so_far)
    so_far = finish(rep, pattern, new[0], split, 0, True, so_far)

    def fits(hamiltonian, pattern, rep, pieces, so_far):
        return finish(rep, pattern, pieces, split, 1, True, so_far).reshape(shape)

    def any_pattern(hamiltonian, pattern, rep, pieces, so_far):
        rep, _, new = newton_step(hamiltonian, pattern, (row_full, chunk_full))
        out = None
        for c in range(CHUNKS):
            for far in (False, True):
                out = finish(rep, pattern, new[c], split, c, far, out)
        return out.reshape(shape)

    return lax.cond(excess > 0, any_pattern, fits, hamiltonian, pattern, rep, new[1], so_far)


def solution(mesh):
    in_specs = (P("row", "col"), P("row", "col"))
    out_specs = P("row", "col")
    return jax.shard_map(shards, mesh=mesh, in_specs=in_specs, out_specs=out_specs, check_vma=False)
```

```python
import functools

import jax
import jax.numpy as jnp
from jax import lax
from jax.experimental import pallas as pl
from jax.experimental.pallas import tpu as pltpu
from jax.sharding import PartitionSpec as P

BS = 128
UNIT = 16
UNITS = BS // UNIT
SIDE = 4
CHUNKS = 2
ROW_CAP = 120
CHUNK_CAP = 64
MIB = 1024 * 1024
SMEM_SPEC = pl.BlockSpec(memory_space=pltpu.SMEM)
ANY_SPEC = pl.BlockSpec(memory_space=pl.ANY)
VMEM_SPEC = pl.BlockSpec(memory_space=pltpu.VMEM)
PIECES = 5
PAIR = 2 * BS
PLACES = (0, 1, 3, 2)


def params(mib):
    return pltpu.CompilerParams(vmem_limit_bytes=mib * MIB)


def cost(flops, moved):
    return pl.CostEstimate(flops=flops, bytes_accessed=moved, transcendentals=0)


def whole(shape):
    return pl.BlockSpec(shape, lambda *_: (0,) * len(shape))


def take_slot(kept, free):
    factor = jnp.full((UNIT, BS), kept.astype(jnp.float32), jnp.float32).astype(jnp.bfloat16)
    return kept * free, factor, free + kept


def pick_kernel(rep_ref, pat_ref, h_ref, out_ref, held_ref, count_ref):
    step = pl.program_id(0)

    @pl.when(step == 0)
    def _():
        held_ref[...] = jnp.zeros_like(held_ref)
        count_ref[0] = 0

    first = (rep_ref[0] % UNITS) * UNIT
    u = lax.broadcasted_iota(jnp.int32, (UNIT, BS), 0)
    c = lax.broadcasted_iota(jnp.int32, (UNIT, BS), 1)
    chosen = jnp.where(c == u + first, 1.0, 0.0).astype(jnp.bfloat16)
    block_col = 2 * step + rep_ref[0] // UNITS
    turned = lax.dot_general(
        chosen, h_ref[...], (((1,), (1,)), ((), ())), preferred_element_type=jnp.float32
    ).astype(jnp.bfloat16)
    count = count_ref[0]
    for a in range(h_ref.shape[0] // BS):
        kept = pat_ref[a, block_col]
        held_ref[count] = turned[:, a * BS : (a + 1) * BS]
        count = count + kept
    count_ref[0] = count

    @pl.when(step == pl.num_programs(0) - 1)
    def _():
        out_ref[...] = held_ref[: out_ref.shape[0]]


def pick(rep, pattern, tile, slots):
    height, width = tile.shape
    full = width // PAIR * (height // BS)
    return pl.pallas_call(
        pick_kernel,
        grid_spec=pltpu.PrefetchScalarGridSpec(
            num_scalar_prefetch=2,
            grid=(width // (2 * BS),),
            in_specs=[pl.BlockSpec((height, BS), lambda j, rep, pat: (0, 2 * j + rep[0] // UNITS))],
            out_specs=whole((slots, UNIT, BS)),
            scratch_shapes=[
                pltpu.VMEM((full + 1, UNIT, BS), jnp.bfloat16),
                pltpu.SMEM((1,), jnp.int32),
            ],
        ),
        out_shape=jax.ShapeDtypeStruct((slots, UNIT, BS), jnp.bfloat16),
        compiler_params=params(16),
        cost_estimate=cost(2 * UNIT * height * width, height * width),
        name="pick",
    )(rep, pattern, tile)


def excess_kernel(*refs):
    pats, out_ref = refs[:-1], refs[-1]
    row = lax.broadcasted_iota(jnp.int32, pats[0].shape, 0)
    col = lax.broadcasted_iota(jnp.int32, pats[0].shape, 1)
    span = pats[0].shape[1] // CHUNKS
    most = jnp.int32(-(2**30))
    for pat in pats:
        flags = pat[...]
        for p in range(2):
            most = jnp.maximum(most, jnp.sum(jnp.where(col % 2 == p, flags, 0)) - ROW_CAP)
            for c in range(CHUNKS):
                chosen = (row % 2 == p) & (col // span == c)
                most = jnp.maximum(most, jnp.sum(jnp.where(chosen, flags, 0)) - CHUNK_CAP)
    out_ref[...] = jnp.full(out_ref.shape, most, jnp.int32)


def over_caps(pats):
    return pl.pallas_call(
        excess_kernel,
        in_specs=[pl.BlockSpec(memory_space=pltpu.VMEM)] * len(pats),
        out_specs=pl.BlockSpec(memory_space=pltpu.VMEM),
        out_shape=jax.ShapeDtypeStruct((8, BS), jnp.int32),
        compiler_params=params(4),
        name="over_caps",
    )(*pats)


def rows_kernel(row_ref, col_ref, rep_ref, *rest):
    pats, own, halves, (out_ref, held_ref) = rest[:SIDE], rest[SIDE], rest[SIDE + 1 : -2], rest[-2:]
    cut = halves[0].shape[0]
    for n, half in enumerate(halves):
        held_ref[n // 2, n % 2 * cut : (n % 2 + 1) * cut] = half[...]
    pieces = [own] + [held_ref.at[n] for n in range(SIDE - 1)]
    row, col, rep = row_ref[0], col_ref[0], rep_ref[0]
    units = out_ref.shape[0] // (SIDE * UNIT)
    parity = rep // UNITS
    starts = [((col ^ away) + SIDE - row * (SIDE // 2)) % SIDE * units for away in PLACES]

    def unit(j, free):
        free = list(free)
        for n, start in enumerate(starts):
            line = pl.ds(pl.multiple_of((start + j) * UNIT, UNIT), UNIT)
            values = []
            for a in range(out_ref.shape[1] // BS):
                slot, factor, free[n] = take_slot(pats[n][a, 2 * j + parity], free[n])
                values.append(pieces[n][slot] * factor)
            for a, value in enumerate(values):
                out_ref[line, pl.ds(a * BS, BS)] = value
        return tuple(free)

    lax.fori_loop(0, units, unit, (jnp.int32(0),) * SIDE)


def unpack_rows(where, pats, pieces, height, units):
    return pl.pallas_call(
        rows_kernel,
        in_specs=[SMEM_SPEC] * (3 + SIDE) + [VMEM_SPEC] * len(pieces),
        out_specs=VMEM_SPEC,
        out_shape=jax.ShapeDtypeStruct((SIDE * units * UNIT, height), jnp.bfloat16),
        scratch_shapes=[pltpu.VMEM((SIDE - 1, *pieces[0].shape), jnp.bfloat16)],
        compiler_params=params(8),
        name="unpack_rows",
    )(*where, *pats, *pieces)


def put_parts(rows, right, own_ref, other_ref, cols):
    half = own_ref.shape[0]
    acc = jnp.dot(rows, right, preferred_element_type=jnp.float32)
    own_ref[:, cols] = acc[:half]
    other_ref[:, cols] = acc[half:].astype(jnp.bfloat16)


def pairs_of(chunk, width):
    first, last = chunk * width // (2 * PAIR), -(-(chunk + 1) * width // (2 * PAIR))
    return first, last - first


def part_shapes(depth, pairs):
    shape = (depth // 2, pairs * PAIR)
    return [jax.ShapeDtypeStruct(shape, jnp.float32), jax.ShapeDtypeStruct(shape, jnp.bfloat16)]


def in_turn(pairs, prepare, buffers, rows_ref, own_ref, other_ref):
    prepare(0, buffers[0])
    for t in range(pairs):
        if t + 1 < pairs:
            prepare(t + 1, buffers[(t + 1) % 2])
        put_parts(rows_ref[...], buffers[t % 2][...], own_ref, other_ref, pl.ds(t * PAIR, PAIR))


def square_kernel(pat_ref, g_ref, h_ref, own_ref, other_ref, *buffers, first, pairs):
    def prepare(t, x_ref):
        for a in range(x_ref.shape[0] // BS):
            for b in range(PAIR // BS):
                col = (first + t) * (PAIR // BS) + b
                kept = pat_ref[a, col].astype(jnp.float32)
                factor = jnp.full((BS, BS), kept, jnp.float32).astype(jnp.bfloat16)
                rows = pl.ds(a * BS, BS)
                x_ref[rows, pl.ds(b * BS, BS)] = h_ref[rows, pl.ds(col * BS, BS)] * factor

    in_turn(pairs, prepare, buffers, g_ref, own_ref, other_ref)


def square_part(pattern, rows, tile, chunk):
    depth, height = rows.shape
    first, pairs = pairs_of(chunk, tile.shape[1])
    return pl.pallas_call(
        functools.partial(square_kernel, first=first, pairs=pairs),
        in_specs=[SMEM_SPEC, VMEM_SPEC, VMEM_SPEC],
        out_specs=[VMEM_SPEC, VMEM_SPEC],
        out_shape=part_shapes(depth, pairs),
        scratch_shapes=[pltpu.VMEM((height, PAIR), jnp.bfloat16)] * 2,
        compiler_params=params(16),
        cost_estimate=cost(2 * depth * height * PAIR * pairs, 2 * height * (PAIR * pairs + depth)),
        name="square_part",
    )(pattern, rows, tile)


def pack_kernel(rep_ref, pat_ref, own_ref, other_ref, *rest, chunk, offset, last):
    tile_ref, out_ref, held_ref = rest if last else (None, *rest)
    units, blocks = own_ref.shape[0] // UNIT, pat_ref.shape[1] // CHUNKS
    parity = rep_ref[0] // UNITS
    held_ref[...] = jnp.zeros_like(held_ref)
    count = jnp.int32(0)
    order = [(j, b) for b in range(blocks) for j in range(units)]
    for j, b in sorted(order) if last else order:
        kept = pat_ref[2 * j + parity, chunk * blocks + b]
        part, cols = pl.ds(j * UNIT, UNIT), pl.ds(offset + b * BS, BS)
        value = own_ref[part, cols] + other_ref[part, cols].astype(jnp.float32)
        if last:
            value = 1.5 * tile_ref[j, 0, :, pl.ds(b * BS, BS)].astype(jnp.float32) - 0.5 * value
        held_ref[count] = value.astype(jnp.bfloat16)
        count = count + kept
    out_ref[...] = held_ref[: out_ref.shape[0]]


def pack(rep, pattern, own, other, chunk, slots, width, tile=None):
    rows = own.shape[0]
    in_specs = [whole(own.shape), whole(other.shape)]
    operands = [own, other]
    span = width // CHUNKS
    if tile is not None:
        reps = tile.shape[0] // rows
        operands.append(tile.reshape(rows // UNIT, reps, UNIT, width))
        in_specs.append(
            pl.BlockSpec((rows // UNIT, 1, UNIT, span), lambda i, rep, pat: (0, rep[0], 0, chunk))
        )
    return pl.pallas_call(
        functools.partial(
            pack_kernel, chunk=chunk, offset=chunk * span % PAIR, last=tile is not None
        ),
        grid_spec=pltpu.PrefetchScalarGridSpec(
            num_scalar_prefetch=2,
            grid=(1,),
            in_specs=in_specs,
            out_specs=whole((slots, UNIT, BS)),
            scratch_shapes=[pltpu.VMEM((rows // UNIT * (span // BS) + 1, UNIT, BS), jnp.bfloat16)],
        ),
        out_shape=jax.ShapeDtypeStruct((slots, UNIT, BS), jnp.bfloat16),
        compiler_params=params(16),
        cost_estimate=cost(4 * rows * span, 8 * rows * span),
        name="pack",
    )(rep, pattern, *operands)


class Gathered:
    def __init__(self, rep, refs, chunk):
        self.refs, self.chunk = refs, chunk
        self.z, self.y = rep // SIDE, rep % SIDE

    def unit(self, q, p, slot):
        if q < SIDE - 1:
            return self.refs[q][p, slot]
        return self.refs[q + p // 2][p % 2, slot]

    def device(self, q, p):
        z, y = (p, q) if self.chunk == 0 else (q, p)
        return (self.z ^ PLACES[z]) * SIDE + (self.y ^ PLACES[y])

    def turned(self, q, p):
        return (p if self.chunk == 0 else q) // 2

    def parity(self, turned):
        return self.z // 2 ^ turned


def cube_kernel(rep_ref, pat_ref, g_ref, *rest, chunk, first, pairs):
    refs, (own_ref, other_ref, square_ref) = rest[:PIECES], rest[PIECES:]
    gathered = Gathered(rep_ref[0], refs, chunk)
    places = [(q, p) for q in range(SIDE) for p in range(SIDE)]
    lines = {place: gathered.device(*place) * UNIT for place in places}
    blocks = pat_ref.shape[1] // CHUNKS
    stride = UNIT * SIDE * SIDE

    def pair(t, free):
        free = list(free)
        for b in range(PAIR // BS):
            col = (first + t) * (PAIR // BS) + b
            inside = (col // blocks == chunk).astype(jnp.int32)
            for j in range(square_ref.shape[0] // stride):
                values = {}
                for turned in range(2):
                    kept = pat_ref[2 * j + gathered.parity(turned), col] * inside
                    slot, factor, free[turned] = take_slot(kept, free[turned])
                    for place in places:
                        if gathered.turned(*place) == turned:
                            values[place] = gathered.unit(*place, slot) * factor
                for place, value in values.items():
                    line = pl.ds(pl.multiple_of(j * stride + lines[place], UNIT), UNIT)
                    square_ref[line, pl.ds(b * BS, BS)] = value
        cols = pl.ds(pl.multiple_of(t * PAIR, PAIR), PAIR)
        put_parts(g_ref[...], square_ref[...], own_ref, other_ref, cols)
        return tuple(free)

    lax.fori_loop(0, pairs, pair, (jnp.int32(0), jnp.int32(0)))


def cube_part(rep, pattern, rows, pieces, chunk, width):
    depth, height = rows.shape
    first, pairs = pairs_of(chunk, width)
    return pl.pallas_call(
        functools.partial(cube_kernel, chunk=chunk, first=first, pairs=pairs),
        in_specs=[SMEM_SPEC, SMEM_SPEC, VMEM_SPEC] + [VMEM_SPEC] * PIECES,
        out_specs=[VMEM_SPEC, VMEM_SPEC],
        out_shape=part_shapes(depth, pairs),
        scratch_shapes=[pltpu.VMEM((height, PAIR), jnp.bfloat16)],
        compiler_params=params(8),
        cost_estimate=cost(2 * depth * height * PAIR * pairs, 2 * height * (PAIR * pairs + depth)),
        name="cube_part",
    )(rep, pattern, rows, *pieces)


def finish_kernel(rep_ref, pat_ref, *rest, chunk, far, count):
    refs, (out_ref, held_ref, sems) = rest[:count], rest[-3:]
    refs = [None] * (SIDE - 1) + list(refs) if far else refs
    gathered = Gathered(rep_ref[0], refs, chunk)
    seconds = [SIDE - 1] if far else range(SIDE - 1)
    units, blocks = held_ref.shape[1], held_ref.shape[3] // BS
    copies = []
    for turned in range(2):
        places = [(q, p) for q in seconds for p in range(SIDE) if gathered.turned(q, p) == turned]
        if not places:
            continue
        base = len(copies)

        def line(j, free, turned=turned, places=places, base=base):
            values = {}
            for b in range(blocks):
                kept = pat_ref[2 * j + gathered.parity(turned), chunk * blocks + b]
                slot, factor, free = take_slot(kept, free)
                for n, place in enumerate(places):
                    values[n, b] = gathered.unit(*place, slot) * factor
            for (n, b), value in values.items():
                held_ref[base + n, j, :, pl.ds(b * BS, BS)] = value
            return free

        lax.fori_loop(0, units, line, jnp.int32(0))
        cols = pl.ds(chunk * blocks * BS, blocks * BS)
        for n, place in enumerate(places):
            target = out_ref.at[:, gathered.device(*place), :, cols]
            copies.append(pltpu.make_async_copy(held_ref.at[base + n], target, sems.at[base + n]))
            copies[-1].start()
    for copy in copies:
        copy.wait()


def finish(rep, pattern, pieces, shape, chunk, far, so_far=None):
    units, reps, _, width = shape
    sources = (1 if far else SIDE - 1) * SIDE
    span = width // CHUNKS
    pieces = pieces[SIDE - 1 :] if far else pieces[: SIDE - 1]
    operands = [rep, pattern, *pieces] + ([] if so_far is None else [so_far])
    return pl.pallas_call(
        functools.partial(finish_kernel, chunk=chunk, far=far, count=len(pieces)),
        in_specs=[SMEM_SPEC, SMEM_SPEC]
        + [VMEM_SPEC] * len(pieces)
        + ([] if so_far is None else [ANY_SPEC]),
        out_specs=ANY_SPEC,
        out_shape=jax.ShapeDtypeStruct(shape, jnp.bfloat16),
        scratch_shapes=[
            pltpu.VMEM((sources, units, UNIT, span), jnp.bfloat16),
            pltpu.SemaphoreType.DMA((sources,)),
        ],
        input_output_aliases={} if so_far is None else {2 + len(pieces): 0},
        compiler_params=params(16),
        cost_estimate=cost(sources * units * UNIT * span, 4 * sources * units * UNIT * span),
        name="finish_far" if far else "finish_near",
    )(*operands)


def ring(piece, axis, pairs):
    one = lax.ppermute(piece, axis, pairs(1))
    three = lax.ppermute(piece, axis, pairs(3))
    cut = piece.shape[0] // 2
    top = lax.ppermute(three[:cut], axis, pairs(1))
    bottom = lax.ppermute(one[cut:], axis, pairs(3))
    return one, three, top, bottom


def col_ring(step):
    return [(i, i ^ step) for i in range(SIDE)]


def z_ring(step):
    return [(z * SIDE + y, (z ^ step) * SIDE + y) for z in range(SIDE) for y in range(SIDE)]


def y_ring(step):
    return [(z * SIDE + y, z * SIDE + (y ^ step)) for z in range(SIDE) for y in range(SIDE)]


def gather_col(packed):
    cut = packed.shape[0] // 2
    top, bottom = packed[:cut], packed[cut:]
    three_top = lax.ppermute(top, "col", col_ring(3))
    one_bottom = lax.ppermute(bottom, "col", col_ring(1))
    one = lax.ppermute(top, "col", col_ring(1)), one_bottom
    three = three_top, lax.ppermute(bottom, "col", col_ring(3))
    far = lax.ppermute(three_top, "col", col_ring(1)), lax.ppermute(one_bottom, "col", col_ring(3))
    return [packed, *one, *three, *far]


def gather_rep(packed, chunk):
    first, second = (z_ring, y_ring) if chunk == 0 else (y_ring, z_ring)
    one, three, top, bottom = ring(packed, "rep", first)
    payload = jnp.stack([packed, one, three, jnp.concatenate([top, bottom], axis=0)])
    return [payload, *ring(payload, "rep", second)]


def swap(part):
    return lax.ppermute(part, "row", [(0, 1), (1, 0)])


def newton_step(hamiltonian, pattern, caps):
    height, width = hamiltonian.shape
    row_cap, chunk_cap = caps
    units = width // PAIR
    rep = lax.axis_index("rep").reshape(1)
    where = [lax.axis_index(axis).reshape(1) for axis in ("row", "col")] + [rep]

    picked = gather_col(pick(rep, pattern, hamiltonian, row_cap))
    picked[1], picked[4], sent = lax.optimization_barrier((picked[1], picked[4], pattern))
    pats = [pattern] + [lax.ppermute(sent, "col", col_ring(a)) for a in PLACES[1:]]
    rows = unpack_rows(where, pats, picked, height, units)
    square, new = [], []
    for c in range(CHUNKS):
        own, other = square_part(pattern, rows, hamiltonian, c)
        square.append(gather_rep(pack(rep, pattern, own, swap(other), c, chunk_cap, width), c))
    for c in range(CHUNKS):
        own, other = cube_part(rep, pattern, rows, square[c], c, width)
        packed = pack(rep, pattern, own, swap(other), c, chunk_cap, width, hamiltonian)
        new.append(gather_rep(packed, c))
    return rep, pats, new


def shards(hamiltonian, pattern):
    shape = hamiltonian.shape
    row_full = shape[1] // PAIR * pattern.shape[0]
    chunk_full = pattern.shape[0] // 2 * (pattern.shape[1] // CHUNKS)

    units = shape[0] // (lax.axis_size("rep") * UNIT)
    split = (units, lax.axis_size("rep"), UNIT, shape[1])

    rep, pats, new = newton_step(hamiltonian, pattern, (ROW_CAP, CHUNK_CAP))
    excess = over_caps(pats)
    excess = jnp.maximum(excess, swap(excess))[0, 0]
    so_far = finish(rep, pattern, new[0], split, 0, False)
    so_far = finish(rep, pattern, new[1], split, 1, False, so_far)
    so_far = finish(rep, pattern, new[0], split, 0, True, so_far)

    def fits(hamiltonian, pattern, rep, pieces, so_far):
        return finish(rep, pattern, pieces, split, 1, True, so_far).reshape(shape)

    def any_pattern(hamiltonian, pattern, rep, pieces, so_far):
        rep, _, new = newton_step(hamiltonian, pattern, (row_full, chunk_full))
        out = None
        for c in range(CHUNKS):
            for far in (False, True):
                out = finish(rep, pattern, new[c], split, c, far, out)
        return out.reshape(shape)

    return lax.cond(excess > 0, any_pattern, fits, hamiltonian, pattern, rep, new[1], so_far)


def solution(mesh):
    in_specs = (P("row", "col"), P("row", "col"))
    out_specs = P("row", "col")
    return jax.shard_map(shards, mesh=mesh, in_specs=in_specs, out_specs=out_specs, check_vma=False)
```

```python
import functools

import jax
import jax.numpy as jnp
from jax import lax
from jax.experimental import pallas as pl
from jax.experimental.pallas import tpu as pltpu
from jax.sharding import PartitionSpec as P

BS = 128
UNIT = 16
UNITS = BS // UNIT
SIDE = 4
CHUNKS = 2
ROW_CAP = 120
CHUNK_CAP = 64
MIB = 1024 * 1024
SMEM_SPEC = pl.BlockSpec(memory_space=pltpu.SMEM)
ANY_SPEC = pl.BlockSpec(memory_space=pl.ANY)
VMEM_SPEC = pl.BlockSpec(memory_space=pltpu.VMEM)
PIECES = 5
PAIR = 2 * BS
PLACES = (0, 1, 3, 2)


def params(mib):
    return pltpu.CompilerParams(vmem_limit_bytes=mib * MIB)


def cost(flops, moved):
    return pl.CostEstimate(flops=flops, bytes_accessed=moved, transcendentals=0)


def whole(shape):
    return pl.BlockSpec(shape, lambda *_: (0,) * len(shape))


def take_slot(kept, free):
    factor = jnp.full((UNIT, BS), kept.astype(jnp.float32), jnp.float32).astype(jnp.bfloat16)
    return kept * free, factor, free + kept


def pick_kernel(rep_ref, pat_ref, h_ref, out_ref, held_ref, count_ref):
    step = pl.program_id(0)

    @pl.when(step == 0)
    def _():
        held_ref[...] = jnp.zeros_like(held_ref)
        count_ref[0] = 0

    first = (rep_ref[0] % UNITS) * UNIT
    u = lax.broadcasted_iota(jnp.int32, (UNIT, BS), 0)
    c = lax.broadcasted_iota(jnp.int32, (UNIT, BS), 1)
    chosen = jnp.where(c == u + first, 1.0, 0.0).astype(jnp.bfloat16)
    block_col = 2 * step + rep_ref[0] // UNITS
    turned = lax.dot_general(
        chosen, h_ref[...], (((1,), (1,)), ((), ())), preferred_element_type=jnp.float32
    ).astype(jnp.bfloat16)
    count = count_ref[0]
    for a in range(h_ref.shape[0] // BS):
        kept = pat_ref[a, block_col]
        held_ref[count] = turned[:, a * BS : (a + 1) * BS]
        count = count + kept
    count_ref[0] = count

    @pl.when(step == pl.num_programs(0) - 1)
    def _():
        out_ref[...] = held_ref[: out_ref.shape[0]]


def pick(rep, pattern, tile, slots):
    height, width = tile.shape
    full = width // PAIR * (height // BS)
    return pl.pallas_call(
        pick_kernel,
        grid_spec=pltpu.PrefetchScalarGridSpec(
            num_scalar_prefetch=2,
            grid=(width // (2 * BS),),
            in_specs=[pl.BlockSpec((height, BS), lambda j, rep, pat: (0, 2 * j + rep[0] // UNITS))],
            out_specs=whole((slots, UNIT, BS)),
            scratch_shapes=[
                pltpu.VMEM((full + 1, UNIT, BS), jnp.bfloat16),
                pltpu.SMEM((1,), jnp.int32),
            ],
        ),
        out_shape=jax.ShapeDtypeStruct((slots, UNIT, BS), jnp.bfloat16),
        compiler_params=params(16),
        cost_estimate=cost(2 * UNIT * height * width, height * width),
        name="pick",
    )(rep, pattern, tile)


def excess_kernel(*refs):
    pats, out_ref = refs[:-1], refs[-1]
    row = lax.broadcasted_iota(jnp.int32, pats[0].shape, 0)
    col = lax.broadcasted_iota(jnp.int32, pats[0].shape, 1)
    span = pats[0].shape[1] // CHUNKS
    most = jnp.int32(-(2**30))
    for pat in pats:
        flags = pat[...]
        for p in range(2):
            most = jnp.maximum(most, jnp.sum(jnp.where(col % 2 == p, flags, 0)) - ROW_CAP)
            for c in range(CHUNKS):
                chosen = (row % 2 == p) & (col // span == c)
                most = jnp.maximum(most, jnp.sum(jnp.where(chosen, flags, 0)) - CHUNK_CAP)
    out_ref[...] = jnp.full(out_ref.shape, most, jnp.int32)


def over_caps(pats):
    return pl.pallas_call(
        excess_kernel,
        in_specs=[pl.BlockSpec(memory_space=pltpu.VMEM)] * len(pats),
        out_specs=pl.BlockSpec(memory_space=pltpu.VMEM),
        out_shape=jax.ShapeDtypeStruct((8, BS), jnp.int32),
        compiler_params=params(4),
        name="over_caps",
    )(*pats)


def rows_kernel(row_ref, col_ref, rep_ref, *rest):
    pats, own, halves, (out_ref, held_ref) = rest[:SIDE], rest[SIDE], rest[SIDE + 1 : -2], rest[-2:]
    cut = halves[0].shape[0]
    for n, half in enumerate(halves):
        held_ref[n // 2, n % 2 * cut : (n % 2 + 1) * cut] = half[...]
    pieces = [own] + [held_ref.at[n] for n in range(SIDE - 1)]
    row, col, rep = row_ref[0], col_ref[0], rep_ref[0]
    units = out_ref.shape[0] // (SIDE * UNIT)
    parity = rep // UNITS
    starts = [((col ^ away) + SIDE - row * (SIDE // 2)) % SIDE * units for away in PLACES]

    def unit(j, free):
        free = list(free)
        for n, start in enumerate(starts):
            line = pl.ds(pl.multiple_of((start + j) * UNIT, UNIT), UNIT)
            values = []
            for a in range(out_ref.shape[1] // BS):
                slot, factor, free[n] = take_slot(pats[n][a, 2 * j + parity], free[n])
                values.append(pieces[n][slot] * factor)
            for a, value in enumerate(values):
                out_ref[line, pl.ds(a * BS, BS)] = value
        return tuple(free)

    lax.fori_loop(0, units, unit, (jnp.int32(0),) * SIDE)


def unpack_rows(where, pats, pieces, height, units):
    return pl.pallas_call(
        rows_kernel,
        in_specs=[SMEM_SPEC] * (3 + SIDE) + [VMEM_SPEC] * len(pieces),
        out_specs=VMEM_SPEC,
        out_shape=jax.ShapeDtypeStruct((SIDE * units * UNIT, height), jnp.bfloat16),
        scratch_shapes=[pltpu.VMEM((SIDE - 1, *pieces[0].shape), jnp.bfloat16)],
        compiler_params=params(8),
        name="unpack_rows",
    )(*where, *pats, *pieces)


def put_parts(rows, right, own_ref, other_ref, cols):
    half = own_ref.shape[0]
    acc = jnp.dot(rows, right, preferred_element_type=jnp.float32)
    own_ref[:, cols] = acc[:half]
    other_ref[:, cols] = acc[half:].astype(jnp.bfloat16)


def pairs_of(chunk, width):
    first, last = chunk * width // (2 * PAIR), -(-(chunk + 1) * width // (2 * PAIR))
    return first, last - first


def part_shapes(depth, pairs):
    shape = (depth // 2, pairs * PAIR)
    return [jax.ShapeDtypeStruct(shape, jnp.float32), jax.ShapeDtypeStruct(shape, jnp.bfloat16)]


def in_turn(pairs, prepare, buffers, rows_ref, own_ref, other_ref):
    prepare(0, buffers[0])
    for t in range(pairs):
        if t + 1 < pairs:
            prepare(t + 1, buffers[(t + 1) % 2])
        put_parts(rows_ref[...], buffers[t % 2][...], own_ref, other_ref, pl.ds(t * PAIR, PAIR))


def square_kernel(pat_ref, g_ref, h_ref, own_ref, other_ref, *buffers, first, pairs):
    def prepare(t, x_ref):
        for a in range(x_ref.shape[0] // BS):
            for b in range(PAIR // BS):
                col = (first + t) * (PAIR // BS) + b
                kept = pat_ref[a, col].astype(jnp.float32)
                factor = jnp.full((BS, BS), kept, jnp.float32).astype(jnp.bfloat16)
                rows = pl.ds(a * BS, BS)
                x_ref[rows, pl.ds(b * BS, BS)] = h_ref[rows, pl.ds(col * BS, BS)] * factor

    in_turn(pairs, prepare, buffers, g_ref, own_ref, other_ref)


def square_part(pattern, rows, tile, chunk):
    depth, height = rows.shape
    first, pairs = pairs_of(chunk, tile.shape[1])
    return pl.pallas_call(
        functools.partial(square_kernel, first=first, pairs=pairs),
        in_specs=[SMEM_SPEC, VMEM_SPEC, VMEM_SPEC],
        out_specs=[VMEM_SPEC, VMEM_SPEC],
        out_shape=part_shapes(depth, pairs),
        scratch_shapes=[pltpu.VMEM((height, PAIR), jnp.bfloat16)] * 2,
        compiler_params=params(16),
        cost_estimate=cost(2 * depth * height * PAIR * pairs, 2 * height * (PAIR * pairs + depth)),
        name="square_part",
    )(pattern, rows, tile)


def pack_kernel(rep_ref, pat_ref, own_ref, other_ref, *rest, chunk, offset, last):
    tile_ref, out_ref, held_ref = rest if last else (None, *rest)
    units, blocks = own_ref.shape[0] // UNIT, pat_ref.shape[1] // CHUNKS
    parity = rep_ref[0] // UNITS
    held_ref[...] = jnp.zeros_like(held_ref)
    count = jnp.int32(0)
    order = [(j, b) for b in range(blocks) for j in range(units)]
    for j, b in sorted(order) if last else order:
        kept = pat_ref[2 * j + parity, chunk * blocks + b]
        part, cols = pl.ds(j * UNIT, UNIT), pl.ds(offset + b * BS, BS)
        value = own_ref[part, cols] + other_ref[part, cols].astype(jnp.float32)
        if last:
            value = 1.5 * tile_ref[j, 0, :, pl.ds(b * BS, BS)].astype(jnp.float32) - 0.5 * value
        held_ref[count] = value.astype(jnp.bfloat16)
        count = count + kept
    out_ref[...] = held_ref[: out_ref.shape[0]]


def pack(rep, pattern, own, other, chunk, slots, width, tile=None):
    rows = own.shape[0]
    in_specs = [whole(own.shape), whole(other.shape)]
    operands = [own, other]
    span = width // CHUNKS
    if tile is not None:
        reps = tile.shape[0] // rows
        operands.append(tile.reshape(rows // UNIT, reps, UNIT, width))
        in_specs.append(
            pl.BlockSpec((rows // UNIT, 1, UNIT, span), lambda i, rep, pat: (0, rep[0], 0, chunk))
        )
    return pl.pallas_call(
        functools.partial(
            pack_kernel, chunk=chunk, offset=chunk * span % PAIR, last=tile is not None
        ),
        grid_spec=pltpu.PrefetchScalarGridSpec(
            num_scalar_prefetch=2,
            grid=(1,),
            in_specs=in_specs,
            out_specs=whole((slots, UNIT, BS)),
            scratch_shapes=[pltpu.VMEM((rows // UNIT * (span // BS) + 1, UNIT, BS), jnp.bfloat16)],
        ),
        out_shape=jax.ShapeDtypeStruct((slots, UNIT, BS), jnp.bfloat16),
        compiler_params=params(16),
        cost_estimate=cost(4 * rows * span, 8 * rows * span),
        name="pack",
    )(rep, pattern, *operands)


class Gathered:
    def __init__(self, rep, refs, chunk):
        self.refs, self.chunk = refs, chunk
        self.z, self.y = rep // SIDE, rep % SIDE

    def unit(self, q, p, slot):
        if q < SIDE - 1:
            return self.refs[q][p, slot]
        return self.refs[q + p // 2][p % 2, slot]

    def device(self, q, p):
        z, y = (p, q) if self.chunk == 0 else (q, p)
        return (self.z ^ PLACES[z]) * SIDE + (self.y ^ PLACES[y])

    def turned(self, q, p):
        return (p if self.chunk == 0 else q) // 2

    def parity(self, turned):
        return self.z // 2 ^ turned


def cube_kernel(rep_ref, pat_ref, g_ref, *rest, chunk, first, pairs):
    refs, (own_ref, other_ref, square_ref) = rest[:PIECES], rest[PIECES:]
    gathered = Gathered(rep_ref[0], refs, chunk)
    places = [(q, p) for q in range(SIDE) for p in range(SIDE)]
    lines = {place: gathered.device(*place) * UNIT for place in places}
    blocks = pat_ref.shape[1] // CHUNKS
    stride = UNIT * SIDE * SIDE

    def pair(t, free):
        free = list(free)
        for b in range(PAIR // BS):
            col = (first + t) * (PAIR // BS) + b
            inside = (col // blocks == chunk).astype(jnp.int32)
            for j in range(square_ref.shape[0] // stride):
                values = {}
                for turned in range(2):
                    kept = pat_ref[2 * j + gathered.parity(turned), col] * inside
                    slot, factor, free[turned] = take_slot(kept, free[turned])
                    for place in places:
                        if gathered.turned(*place) == turned:
                            values[place] = gathered.unit(*place, slot) * factor
                for place, value in values.items():
                    line = pl.ds(pl.multiple_of(j * stride + lines[place], UNIT), UNIT)
                    square_ref[line, pl.ds(b * BS, BS)] = value
        cols = pl.ds(pl.multiple_of(t * PAIR, PAIR), PAIR)
        put_parts(g_ref[...], square_ref[...], own_ref, other_ref, cols)
        return tuple(free)

    lax.fori_loop(0, pairs, pair, (jnp.int32(0), jnp.int32(0)))


def cube_part(rep, pattern, rows, pieces, chunk, width):
    depth, height = rows.shape
    first, pairs = pairs_of(chunk, width)
    return pl.pallas_call(
        functools.partial(cube_kernel, chunk=chunk, first=first, pairs=pairs),
        in_specs=[SMEM_SPEC, SMEM_SPEC, VMEM_SPEC] + [VMEM_SPEC] * PIECES,
        out_specs=[VMEM_SPEC, VMEM_SPEC],
        out_shape=part_shapes(depth, pairs),
        scratch_shapes=[pltpu.VMEM((height, PAIR), jnp.bfloat16)],
        compiler_params=params(8),
        cost_estimate=cost(2 * depth * height * PAIR * pairs, 2 * height * (PAIR * pairs + depth)),
        name="cube_part",
    )(rep, pattern, rows, *pieces)


def finish_kernel(rep_ref, pat_ref, *rest, chunk, far, count):
    refs, (out_ref, held_ref, sems) = rest[:count], rest[-3:]
    refs = [None] * (SIDE - 1) + list(refs) if far else refs
    gathered = Gathered(rep_ref[0], refs, chunk)
    seconds = [SIDE - 1] if far else range(SIDE - 1)
    units, blocks = held_ref.shape[1], held_ref.shape[3] // BS
    copies = []
    for turned in range(2):
        places = [(q, p) for q in seconds for p in range(SIDE) if gathered.turned(q, p) == turned]
        if not places:
            continue
        base = len(copies)

        def line(j, free, turned=turned, places=places, base=base):
            values = {}
            for b in range(blocks):
                kept = pat_ref[2 * j + gathered.parity(turned), chunk * blocks + b]
                slot, factor, free = take_slot(kept, free)
                for n, place in enumerate(places):
                    values[n, b] = gathered.unit(*place, slot) * factor
            for (n, b), value in values.items():
                held_ref[base + n, j, :, pl.ds(b * BS, BS)] = value
            return free

        lax.fori_loop(0, units, line, jnp.int32(0))
        cols = pl.ds(chunk * blocks * BS, blocks * BS)
        for n, place in enumerate(places):
            target = out_ref.at[:, gathered.device(*place), :, cols]
            copies.append(pltpu.make_async_copy(held_ref.at[base + n], target, sems.at[base + n]))
            copies[-1].start()
    for copy in copies:
        copy.wait()


def finish(rep, pattern, pieces, shape, chunk, far, so_far=None):
    units, reps, _, width = shape
    sources = (1 if far else SIDE - 1) * SIDE
    span = width // CHUNKS
    pieces = pieces[SIDE - 1 :] if far else pieces[: SIDE - 1]
    operands = [rep, pattern, *pieces] + ([] if so_far is None else [so_far])
    return pl.pallas_call(
        functools.partial(finish_kernel, chunk=chunk, far=far, count=len(pieces)),
        in_specs=[SMEM_SPEC, SMEM_SPEC]
        + [VMEM_SPEC] * len(pieces)
        + ([] if so_far is None else [ANY_SPEC]),
        out_specs=ANY_SPEC,
        out_shape=jax.ShapeDtypeStruct(shape, jnp.bfloat16),
        scratch_shapes=[
            pltpu.VMEM((sources, units, UNIT, span), jnp.bfloat16),
            pltpu.SemaphoreType.DMA((sources,)),
        ],
        input_output_aliases={} if so_far is None else {2 + len(pieces): 0},
        compiler_params=params(16),
        cost_estimate=cost(sources * units * UNIT * span, 4 * sources * units * UNIT * span),
        name="finish_far" if far else "finish_near",
    )(*operands)


def ring(piece, axis, pairs):
    one = lax.ppermute(piece, axis, pairs(1))
    three = lax.ppermute(piece, axis, pairs(3))
    cut = piece.shape[0] // 2
    top = lax.ppermute(three[:cut], axis, pairs(1))
    bottom = lax.ppermute(one[cut:], axis, pairs(3))
    return one, three, top, bottom


def col_ring(step):
    return [(i, i ^ step) for i in range(SIDE)]


def z_ring(step):
    return [(z * SIDE + y, (z ^ step) * SIDE + y) for z in range(SIDE) for y in range(SIDE)]


def y_ring(step):
    return [(z * SIDE + y, z * SIDE + (y ^ step)) for z in range(SIDE) for y in range(SIDE)]


def gather_col(packed):
    cut = packed.shape[0] // 2
    top, bottom = packed[:cut], packed[cut:]
    three_top = lax.ppermute(top, "col", col_ring(3))
    one_bottom = lax.ppermute(bottom, "col", col_ring(1))
    one = lax.ppermute(top, "col", col_ring(1)), one_bottom
    three = three_top, lax.ppermute(bottom, "col", col_ring(3))
    far = lax.ppermute(three_top, "col", col_ring(1)), lax.ppermute(one_bottom, "col", col_ring(3))
    return [packed, *one, *three, *far]


def gather_rep(packed, chunk):
    first, second = (z_ring, y_ring) if chunk == 0 else (y_ring, z_ring)
    one, three, top, bottom = ring(packed, "rep", first)
    payload = jnp.stack([packed, one, three, jnp.concatenate([top, bottom], axis=0)])
    return [payload, *ring(payload, "rep", second)]


def swap(part):
    return lax.ppermute(part, "row", [(0, 1), (1, 0)])


def after_kernel(value_ref, *rest):
    rest[-1][...] = value_ref[...]


def after(value, *others):
    return pl.pallas_call(
        after_kernel,
        in_specs=[VMEM_SPEC] + [ANY_SPEC] * len(others),
        out_specs=VMEM_SPEC,
        out_shape=jax.ShapeDtypeStruct(value.shape, value.dtype),
        compiler_params=params(4),
        name="after",
    )(value, *others)


def newton_step(hamiltonian, pattern, caps):
    height, width = hamiltonian.shape
    row_cap, chunk_cap = caps
    units = width // PAIR
    rep = lax.axis_index("rep").reshape(1)
    where = [lax.axis_index(axis).reshape(1) for axis in ("row", "col")] + [rep]

    picked = gather_col(pick(rep, pattern, hamiltonian, row_cap))
    sent = after(pattern, picked[1], picked[4])
    pats = [pattern] + [lax.ppermute(sent, "col", col_ring(a)) for a in PLACES[1:]]
    rows = unpack_rows(where, pats, picked, height, units)
    square, new = [], []
    for c in range(CHUNKS):
        own, other = square_part(pattern, rows, hamiltonian, c)
        square.append(gather_rep(pack(rep, pattern, own, swap(other), c, chunk_cap, width), c))
    for c in range(CHUNKS):
        own, other = cube_part(rep, pattern, rows, square[c], c, width)
        packed = pack(rep, pattern, own, swap(other), c, chunk_cap, width, hamiltonian)
        new.append(gather_rep(packed, c))
    return rep, pats, new


def shards(hamiltonian, pattern):
    shape = hamiltonian.shape
    row_full = shape[1] // PAIR * pattern.shape[0]
    chunk_full = pattern.shape[0] // 2 * (pattern.shape[1] // CHUNKS)

    units = shape[0] // (lax.axis_size("rep") * UNIT)
    split = (units, lax.axis_size("rep"), UNIT, shape[1])

    rep, pats, new = newton_step(hamiltonian, pattern, (ROW_CAP, CHUNK_CAP))
    excess = over_caps(pats)
    excess = jnp.maximum(excess, swap(excess))[0, 0]
    so_far = finish(rep, pattern, new[0], split, 0, False)
    so_far = finish(rep, pattern, new[1], split, 1, False, so_far)
    so_far = finish(rep, pattern, new[0], split, 0, True, so_far)

    def fits(hamiltonian, pattern, rep, pieces, so_far):
        return finish(rep, pattern, pieces, split, 1, True, so_far).reshape(shape)

    def any_pattern(hamiltonian, pattern, rep, pieces, so_far):
        rep, _, new = newton_step(hamiltonian, pattern, (row_full, chunk_full))
        out = None
        for c in range(CHUNKS):
            for far in (False, True):
                out = finish(rep, pattern, new[c], split, c, far, out)
        return out.reshape(shape)

    return lax.cond(excess > 0, any_pattern, fits, hamiltonian, pattern, rep, new[1], so_far)


def solution(mesh):
    in_specs = (P("row", "col"), P("row", "col"))
    out_specs = P("row", "col")
    return jax.shard_map(shards, mesh=mesh, in_specs=in_specs, out_specs=out_specs, check_vma=False)
```

```python
import functools

import jax
import jax.numpy as jnp
from jax import lax
from jax.experimental import pallas as pl
from jax.experimental.pallas import tpu as pltpu
from jax.sharding import PartitionSpec as P

BS = 128
UNIT = 16
UNITS = BS // UNIT
SIDE = 4
CHUNKS = 2
ROW_CAP = 120
CHUNK_CAP = 64
MIB = 1024 * 1024
SMEM_SPEC = pl.BlockSpec(memory_space=pltpu.SMEM)
ANY_SPEC = pl.BlockSpec(memory_space=pl.ANY)
VMEM_SPEC = pl.BlockSpec(memory_space=pltpu.VMEM)
PIECES = 5
PAIR = 2 * BS
PLACES = (0, 1, 3, 2)


def params(mib):
    return pltpu.CompilerParams(vmem_limit_bytes=mib * MIB)


def cost(flops, moved):
    return pl.CostEstimate(flops=flops, bytes_accessed=moved, transcendentals=0)


def whole(shape):
    return pl.BlockSpec(shape, lambda *_: (0,) * len(shape))


def take_slot(kept, free):
    factor = jnp.full((UNIT, BS), kept.astype(jnp.float32), jnp.float32).astype(jnp.bfloat16)
    return kept * free, factor, free + kept


def pick_kernel(rep_ref, pat_ref, h_ref, out_ref, held_ref, count_ref):
    step = pl.program_id(0)

    @pl.when(step == 0)
    def _():
        held_ref[...] = jnp.zeros_like(held_ref)
        count_ref[0] = 0

    first = (rep_ref[0] % UNITS) * UNIT
    u = lax.broadcasted_iota(jnp.int32, (UNIT, BS), 0)
    c = lax.broadcasted_iota(jnp.int32, (UNIT, BS), 1)
    chosen = jnp.where(c == u + first, 1.0, 0.0).astype(jnp.bfloat16)
    block_col = 2 * step + rep_ref[0] // UNITS
    turned = lax.dot_general(
        chosen, h_ref[...], (((1,), (1,)), ((), ())), preferred_element_type=jnp.float32
    ).astype(jnp.bfloat16)
    count = count_ref[0]
    for a in range(h_ref.shape[0] // BS):
        kept = pat_ref[a, block_col]
        held_ref[count] = turned[:, a * BS : (a + 1) * BS]
        count = count + kept
    count_ref[0] = count

    @pl.when(step == pl.num_programs(0) - 1)
    def _():
        out_ref[...] = held_ref[: out_ref.shape[0]]


def pick(rep, pattern, tile, slots):
    height, width = tile.shape
    full = width // PAIR * (height // BS)
    return pl.pallas_call(
        pick_kernel,
        grid_spec=pltpu.PrefetchScalarGridSpec(
            num_scalar_prefetch=2,
            grid=(width // (2 * BS),),
            in_specs=[pl.BlockSpec((height, BS), lambda j, rep, pat: (0, 2 * j + rep[0] // UNITS))],
            out_specs=whole((slots, UNIT, BS)),
            scratch_shapes=[
                pltpu.VMEM((full + 1, UNIT, BS), jnp.bfloat16),
                pltpu.SMEM((1,), jnp.int32),
            ],
        ),
        out_shape=jax.ShapeDtypeStruct((slots, UNIT, BS), jnp.bfloat16),
        compiler_params=params(16),
        cost_estimate=cost(2 * UNIT * height * width, height * width),
        name="pick",
    )(rep, pattern, tile)


def excess_kernel(*refs):
    pats, out_ref = refs[:-1], refs[-1]
    row = lax.broadcasted_iota(jnp.int32, pats[0].shape, 0)
    col = lax.broadcasted_iota(jnp.int32, pats[0].shape, 1)
    span = pats[0].shape[1] // CHUNKS
    most = jnp.int32(-(2**30))
    for pat in pats:
        flags = pat[...]
        for p in range(2):
            most = jnp.maximum(most, jnp.sum(jnp.where(col % 2 == p, flags, 0)) - ROW_CAP)
            for c in range(CHUNKS):
                chosen = (row % 2 == p) & (col // span == c)
                most = jnp.maximum(most, jnp.sum(jnp.where(chosen, flags, 0)) - CHUNK_CAP)
    out_ref[...] = jnp.full(out_ref.shape, most, jnp.int32)


def over_caps(pats):
    return pl.pallas_call(
        excess_kernel,
        in_specs=[pl.BlockSpec(memory_space=pltpu.VMEM)] * len(pats),
        out_specs=pl.BlockSpec(memory_space=pltpu.VMEM),
        out_shape=jax.ShapeDtypeStruct((8, BS), jnp.int32),
        compiler_params=params(4),
        name="over_caps",
    )(*pats)


def rows_kernel(row_ref, col_ref, rep_ref, *rest):
    pats, own, halves, (out_ref, held_ref) = rest[:SIDE], rest[SIDE], rest[SIDE + 1 : -2], rest[-2:]
    cut = halves[0].shape[0]
    for n, half in enumerate(halves):
        held_ref[n // 2, n % 2 * cut : (n % 2 + 1) * cut] = half[...]
    pieces = [own] + [held_ref.at[n] for n in range(SIDE - 1)]
    row, col, rep = row_ref[0], col_ref[0], rep_ref[0]
    units = out_ref.shape[0] // (SIDE * UNIT)
    parity = rep // UNITS
    starts = [((col ^ away) + SIDE - row * (SIDE // 2)) % SIDE * units for away in PLACES]

    def unit(j, free):
        free = list(free)
        for n, start in enumerate(starts):
            line = pl.ds(pl.multiple_of((start + j) * UNIT, UNIT), UNIT)
            values = []
            for a in range(out_ref.shape[1] // BS):
                slot, factor, free[n] = take_slot(pats[n][a, 2 * j + parity], free[n])
                values.append(pieces[n][slot] * factor)
            for a, value in enumerate(values):
                out_ref[line, pl.ds(a * BS, BS)] = value
        return tuple(free)

    lax.fori_loop(0, units, unit, (jnp.int32(0),) * SIDE)


def unpack_rows(where, pats, pieces, height, units):
    return pl.pallas_call(
        rows_kernel,
        in_specs=[SMEM_SPEC] * (3 + SIDE) + [VMEM_SPEC] * len(pieces),
        out_specs=VMEM_SPEC,
        out_shape=jax.ShapeDtypeStruct((SIDE * units * UNIT, height), jnp.bfloat16),
        scratch_shapes=[pltpu.VMEM((SIDE - 1, *pieces[0].shape), jnp.bfloat16)],
        compiler_params=params(8),
        name="unpack_rows",
    )(*where, *pats, *pieces)


def put_parts(rows, right, own_ref, other_ref, cols):
    half = own_ref.shape[0]
    acc = jnp.dot(rows, right, preferred_element_type=jnp.float32)
    own_ref[:, cols] = acc[:half]
    other_ref[:, cols] = acc[half:].astype(jnp.bfloat16)


def pairs_of(chunk, width):
    first, last = chunk * width // (2 * PAIR), -(-(chunk + 1) * width // (2 * PAIR))
    return first, last - first


def part_shapes(depth, pairs):
    shape = (depth // 2, pairs * PAIR)
    return [jax.ShapeDtypeStruct(shape, jnp.float32), jax.ShapeDtypeStruct(shape, jnp.bfloat16)]


def in_turn(pairs, prepare, buffers, rows_ref, own_ref, other_ref):
    prepare(0, buffers[0])
    for t in range(pairs):
        if t + 1 < pairs:
            prepare(t + 1, buffers[(t + 1) % 2])
        put_parts(rows_ref[...], buffers[t % 2][...], own_ref, other_ref, pl.ds(t * PAIR, PAIR))


def square_kernel(pat_ref, g_ref, h_ref, own_ref, other_ref, *buffers, first, pairs):
    def prepare(t, x_ref):
        for a in range(x_ref.shape[0] // BS):
            for b in range(PAIR // BS):
                col = (first + t) * (PAIR // BS) + b
                kept = pat_ref[a, col].astype(jnp.float32)
                factor = jnp.full((BS, BS), kept, jnp.float32).astype(jnp.bfloat16)
                rows = pl.ds(a * BS, BS)
                x_ref[rows, pl.ds(b * BS, BS)] = h_ref[rows, pl.ds(col * BS, BS)] * factor

    in_turn(pairs, prepare, buffers, g_ref, own_ref, other_ref)


def square_part(pattern, rows, tile, chunk):
    depth, height = rows.shape
    first, pairs = pairs_of(chunk, tile.shape[1])
    return pl.pallas_call(
        functools.partial(square_kernel, first=first, pairs=pairs),
        in_specs=[SMEM_SPEC, VMEM_SPEC, VMEM_SPEC],
        out_specs=[VMEM_SPEC, VMEM_SPEC],
        out_shape=part_shapes(depth, pairs),
        scratch_shapes=[pltpu.VMEM((height, PAIR), jnp.bfloat16)] * 2,
        compiler_params=params(16),
        cost_estimate=cost(2 * depth * height * PAIR * pairs, 2 * height * (PAIR * pairs + depth)),
        name="square_part",
    )(pattern, rows, tile)


def pack_kernel(rep_ref, pat_ref, own_ref, other_ref, *rest, chunk, offset, last):
    tile_ref, out_ref, held_ref = rest if last else (None, *rest)
    units, blocks = own_ref.shape[0] // UNIT, pat_ref.shape[1] // CHUNKS
    parity = rep_ref[0] // UNITS
    held_ref[...] = jnp.zeros_like(held_ref)
    count = jnp.int32(0)
    order = [(j, b) for b in range(blocks) for j in range(units)]
    for j, b in sorted(order) if last else order:
        kept = pat_ref[2 * j + parity, chunk * blocks + b]
        part, cols = pl.ds(j * UNIT, UNIT), pl.ds(offset + b * BS, BS)
        value = own_ref[part, cols] + other_ref[part, cols].astype(jnp.float32)
        if last:
            value = 1.5 * tile_ref[j, 0, :, pl.ds(b * BS, BS)].astype(jnp.float32) - 0.5 * value
        held_ref[count] = value.astype(jnp.bfloat16)
        count = count + kept
    out_ref[...] = held_ref[: out_ref.shape[0]]


def pack(rep, pattern, own, other, chunk, slots, width, tile=None):
    rows = own.shape[0]
    in_specs = [whole(own.shape), whole(other.shape)]
    operands = [own, other]
    span = width // CHUNKS
    if tile is not None:
        reps = tile.shape[0] // rows
        operands.append(tile.reshape(rows // UNIT, reps, UNIT, width))
        in_specs.append(
            pl.BlockSpec((rows // UNIT, 1, UNIT, span), lambda i, rep, pat: (0, rep[0], 0, chunk))
        )
    return pl.pallas_call(
        functools.partial(
            pack_kernel, chunk=chunk, offset=chunk * span % PAIR, last=tile is not None
        ),
        grid_spec=pltpu.PrefetchScalarGridSpec(
            num_scalar_prefetch=2,
            grid=(1,),
            in_specs=in_specs,
            out_specs=whole((slots, UNIT, BS)),
            scratch_shapes=[pltpu.VMEM((rows // UNIT * (span // BS) + 1, UNIT, BS), jnp.bfloat16)],
        ),
        out_shape=jax.ShapeDtypeStruct((slots, UNIT, BS), jnp.bfloat16),
        compiler_params=params(16),
        cost_estimate=cost(4 * rows * span, 8 * rows * span),
        name="pack",
    )(rep, pattern, *operands)


class Gathered:
    def __init__(self, rep, refs, chunk):
        self.refs, self.chunk = refs, chunk
        self.z, self.y = rep // SIDE, rep % SIDE

    def unit(self, q, p, slot):
        if q < SIDE - 1:
            return self.refs[q][p, slot]
        return self.refs[q + p // 2][p % 2, slot]

    def device(self, q, p):
        z, y = (p, q) if self.chunk == 0 else (q, p)
        return (self.z ^ PLACES[z]) * SIDE + (self.y ^ PLACES[y])

    def turned(self, q, p):
        return (p if self.chunk == 0 else q) // 2

    def parity(self, turned):
        return self.z // 2 ^ turned


def cube_kernel(rep_ref, pat_ref, g_ref, *rest, chunk, first, pairs):
    refs, (own_ref, other_ref, square_ref) = rest[:PIECES], rest[PIECES:]
    gathered = Gathered(rep_ref[0], refs, chunk)
    places = [(q, p) for q in range(SIDE) for p in range(SIDE)]
    lines = {place: gathered.device(*place) * UNIT for place in places}
    blocks = pat_ref.shape[1] // CHUNKS
    stride = UNIT * SIDE * SIDE

    def pair(t, free):
        free = list(free)
        for b in range(PAIR // BS):
            col = (first + t) * (PAIR // BS) + b
            inside = (col // blocks == chunk).astype(jnp.int32)
            for j in range(square_ref.shape[0] // stride):
                values = {}
                for turned in range(2):
                    kept = pat_ref[2 * j + gathered.parity(turned), col] * inside
                    slot, factor, free[turned] = take_slot(kept, free[turned])
                    for place in places:
                        if gathered.turned(*place) == turned:
                            values[place] = gathered.unit(*place, slot) * factor
                for place, value in values.items():
                    line = pl.ds(pl.multiple_of(j * stride + lines[place], UNIT), UNIT)
                    square_ref[line, pl.ds(b * BS, BS)] = value
        cols = pl.ds(pl.multiple_of(t * PAIR, PAIR), PAIR)
        put_parts(g_ref[...], square_ref[...], own_ref, other_ref, cols)
        return tuple(free)

    lax.fori_loop(0, pairs, pair, (jnp.int32(0), jnp.int32(0)))


def cube_part(rep, pattern, rows, pieces, chunk, width):
    depth, height = rows.shape
    first, pairs = pairs_of(chunk, width)
    return pl.pallas_call(
        functools.partial(cube_kernel, chunk=chunk, first=first, pairs=pairs),
        in_specs=[SMEM_SPEC, SMEM_SPEC, VMEM_SPEC] + [VMEM_SPEC] * PIECES,
        out_specs=[VMEM_SPEC, VMEM_SPEC],
        out_shape=part_shapes(depth, pairs),
        scratch_shapes=[pltpu.VMEM((height, PAIR), jnp.bfloat16)],
        compiler_params=params(8),
        cost_estimate=cost(2 * depth * height * PAIR * pairs, 2 * height * (PAIR * pairs + depth)),
        name="cube_part",
    )(rep, pattern, rows, *pieces)


def finish_kernel(rep_ref, pat_ref, *rest, chunk, far, count):
    refs, (out_ref, held_ref, sems) = rest[:count], rest[-3:]
    refs = [None] * (SIDE - 1) + list(refs) if far else refs
    gathered = Gathered(rep_ref[0], refs, chunk)
    seconds = [SIDE - 1] if far else range(SIDE - 1)
    units, blocks = held_ref.shape[1], held_ref.shape[3] // BS
    copies = []
    for turned in range(2):
        places = [(q, p) for q in seconds for p in range(SIDE) if gathered.turned(q, p) == turned]
        if not places:
            continue
        base = len(copies)

        def line(j, free, turned=turned, places=places, base=base):
            values = {}
            for b in range(blocks):
                kept = pat_ref[2 * j + gathered.parity(turned), chunk * blocks + b]
                slot, factor, free = take_slot(kept, free)
                for n, place in enumerate(places):
                    values[n, b] = gathered.unit(*place, slot) * factor
            for (n, b), value in values.items():
                held_ref[base + n, j, :, pl.ds(b * BS, BS)] = value
            return free

        lax.fori_loop(0, units, line, jnp.int32(0))
        cols = pl.ds(chunk * blocks * BS, blocks * BS)
        for n, place in enumerate(places):
            target = out_ref.at[:, gathered.device(*place), :, cols]
            copies.append(pltpu.make_async_copy(held_ref.at[base + n], target, sems.at[base + n]))
            copies[-1].start()
    for copy in copies:
        copy.wait()


def finish(rep, pattern, pieces, shape, chunk, far, so_far=None):
    units, reps, _, width = shape
    sources = (1 if far else SIDE - 1) * SIDE
    span = width // CHUNKS
    pieces = pieces[SIDE - 1 :] if far else pieces[: SIDE - 1]
    operands = [rep, pattern, *pieces] + ([] if so_far is None else [so_far])
    return pl.pallas_call(
        functools.partial(finish_kernel, chunk=chunk, far=far, count=len(pieces)),
        in_specs=[SMEM_SPEC, SMEM_SPEC]
        + [VMEM_SPEC] * len(pieces)
        + ([] if so_far is None else [ANY_SPEC]),
        out_specs=ANY_SPEC,
        out_shape=jax.ShapeDtypeStruct(shape, jnp.bfloat16),
        scratch_shapes=[
            pltpu.VMEM((sources, units, UNIT, span), jnp.bfloat16),
            pltpu.SemaphoreType.DMA((sources,)),
        ],
        input_output_aliases={} if so_far is None else {2 + len(pieces): 0},
        compiler_params=params(16),
        cost_estimate=cost(sources * units * UNIT * span, 4 * sources * units * UNIT * span),
        name="finish_far" if far else "finish_near",
    )(*operands)


def ring(piece, axis, pairs):
    one = lax.ppermute(piece, axis, pairs(1))
    three = lax.ppermute(piece, axis, pairs(3))
    cut = piece.shape[0] // 2
    top = lax.ppermute(three[:cut], axis, pairs(1))
    bottom = lax.ppermute(one[cut:], axis, pairs(3))
    return one, three, top, bottom


def col_ring(step):
    return [(i, i ^ step) for i in range(SIDE)]


def z_ring(step):
    return [(z * SIDE + y, (z ^ step) * SIDE + y) for z in range(SIDE) for y in range(SIDE)]


def y_ring(step):
    return [(z * SIDE + y, z * SIDE + (y ^ step)) for z in range(SIDE) for y in range(SIDE)]


def gather_col(packed, beside):
    cut = packed.shape[0] // 2
    top, bottom = packed[:cut], packed[cut:]
    three_top = lax.ppermute(top, "col", col_ring(3))
    one_bottom = lax.ppermute(bottom, "col", col_ring(1))
    one = lax.ppermute(top, "col", col_ring(1)), one_bottom
    three = three_top, lax.ppermute(bottom, "col", col_ring(3))
    top, bottom, beside = lax.optimization_barrier((three_top, one_bottom, beside))
    far = lax.ppermute(top, "col", col_ring(1)), lax.ppermute(bottom, "col", col_ring(3))
    return [packed, *one, *three, *far], beside


def gather_rep(packed, chunk):
    first, second = (z_ring, y_ring) if chunk == 0 else (y_ring, z_ring)
    one, three, top, bottom = ring(packed, "rep", first)
    payload = jnp.stack([packed, one, three, jnp.concatenate([top, bottom], axis=0)])
    return [payload, *ring(payload, "rep", second)]


def swap(part):
    return lax.ppermute(part, "row", [(0, 1), (1, 0)])


def after_kernel(value_ref, *rest):
    rest[-1][...] = value_ref[...]


def after(value, *others):
    return pl.pallas_call(
        after_kernel,
        in_specs=[VMEM_SPEC] + [ANY_SPEC] * len(others),
        out_specs=VMEM_SPEC,
        out_shape=jax.ShapeDtypeStruct(value.shape, value.dtype),
        compiler_params=params(4),
        name="after",
    )(value, *others)


def hold_kernel(tile_ref, other_ref, out_ref, sem):
    copy = pltpu.make_async_copy(tile_ref, out_ref, sem)
    copy.start()
    copy.wait()


def hold(tile, other):
    return pl.pallas_call(
        hold_kernel,
        in_specs=[ANY_SPEC, ANY_SPEC],
        out_specs=VMEM_SPEC,
        out_shape=jax.ShapeDtypeStruct(tile.shape, tile.dtype),
        scratch_shapes=[pltpu.SemaphoreType.DMA(())],
        compiler_params=params(16),
        cost_estimate=cost(0, 2 * tile.size * 2),
        name="hold",
    )(tile, other)


def newton_step(hamiltonian, pattern, caps):
    height, width = hamiltonian.shape
    row_cap, chunk_cap = caps
    units = width // PAIR
    rep = lax.axis_index("rep").reshape(1)
    where = [lax.axis_index(axis).reshape(1) for axis in ("row", "col")] + [rep]

    packed = pick(rep, pattern, hamiltonian, row_cap)
    picked, held = gather_col(packed, hold(hamiltonian, packed))
    sent = after(pattern, picked[1], picked[4])
    pats = [pattern] + [lax.ppermute(sent, "col", col_ring(a)) for a in PLACES[1:]]
    rows = unpack_rows(where, pats, picked, height, units)
    square, new = [], []
    for c in range(CHUNKS):
        own, other = square_part(pattern, rows, held, c)
        square.append(gather_rep(pack(rep, pattern, own, swap(other), c, chunk_cap, width), c))
    for c in range(CHUNKS):
        own, other = cube_part(rep, pattern, rows, square[c], c, width)
        packed = pack(rep, pattern, own, swap(other), c, chunk_cap, width, hamiltonian)
        new.append(gather_rep(packed, c))
    return rep, pats, new


def shards(hamiltonian, pattern):
    shape = hamiltonian.shape
    row_full = shape[1] // PAIR * pattern.shape[0]
    chunk_full = pattern.shape[0] // 2 * (pattern.shape[1] // CHUNKS)

    units = shape[0] // (lax.axis_size("rep") * UNIT)
    split = (units, lax.axis_size("rep"), UNIT, shape[1])

    rep, pats, new = newton_step(hamiltonian, pattern, (ROW_CAP, CHUNK_CAP))
    excess = over_caps(pats)
    excess = jnp.maximum(excess, swap(excess))[0, 0]
    so_far = finish(rep, pattern, new[0], split, 0, False)
    so_far = finish(rep, pattern, new[1], split, 1, False, so_far)
    so_far = finish(rep, pattern, new[0], split, 0, True, so_far)

    def fits(hamiltonian, pattern, rep, pieces, so_far):
        return finish(rep, pattern, pieces, split, 1, True, so_far).reshape(shape)

    def any_pattern(hamiltonian, pattern, rep, pieces, so_far):
        rep, _, new = newton_step(hamiltonian, pattern, (row_full, chunk_full))
        out = None
        for c in range(CHUNKS):
            for far in (False, True):
                out = finish(rep, pattern, new[c], split, c, far, out)
        return out.reshape(shape)

    return lax.cond(excess > 0, any_pattern, fits, hamiltonian, pattern, rep, new[1], so_far)


def solution(mesh):
    in_specs = (P("row", "col"), P("row", "col"))
    out_specs = P("row", "col")
    return jax.shard_map(shards, mesh=mesh, in_specs=in_specs, out_specs=out_specs, check_vma=False)
```
